32 devices in a mesh: dp: 8 (over y, x, core), mp: 4 (over z).
Axes of the slice: x: 2, y: 2, z: 4, core: 2. Of those that a mesh axis runs over, the one named last changes fastest.
Arguments:
- tokens: bfloat16 [4096, 1536], P('dp'), may hold values from -40 to 40
- context: bfloat16 [512, 768], P('dp'), may hold values from -6 to 6
- frame_counts: int32 [4], replicated, may hold values from 512 to 1023, as said below
- text_counts: int32 [4], replicated, may hold values from 65 to 128, as said below
- w_qkv: bfloat16 [1536, 3, 1536], P('dp', None, 'mp'), may hold values from -0.15625 to 0.15625
- w_attn_out: bfloat16 [1536, 1536], P('mp', 'dp'), may hold values from -3 to 3
- w_cross_q: bfloat16 [1536, 1536], P('dp', 'mp'), may hold values from -0.15625 to 0.15625
- w_cross_kv: bfloat16 [768, 2, 1536], P('dp', None, 'mp'), may hold values from -0.21875 to 0.21875
- w_cross_out: bfloat16 [1536, 1536], P('mp', 'dp'), may hold values from -1 to 1
- w_in: bfloat16 [1536, 2, 6144], P('dp', None, 'mp'), may hold values from -0.15625 to 0.15625
- w_out: bfloat16 [6144, 1536], P('mp', 'dp'), may hold values from -0.078125 to 0.078125
- norm_gains: bfloat16 [3, 1536], P(None, 'dp'), may hold values from 0.5 to 1.5
- b_in: bfloat16 [2, 6144], P(None, ('mp', 'dp')), may hold values from -1.5 to 1.5
- b_out: bfloat16 [1536], P('dp'), may hold values from -1.5 to 1.5
- cotangent: bfloat16 [4096, 1536], P('dp'), may hold values from -6 to 6
Outputs:
- mixed: bfloat16 [4096, 1536], P('dp')
- grad_tokens: float32 [4096, 1536], P('dp')
- grad_qkv: float32 [1536, 3, 1536], P('dp', None, 'mp')
- grad_attn_out: float32 [1536, 1536], P('mp', 'dp')
- grad_cross_q: float32 [1536, 1536], P('dp', 'mp')
- grad_cross_kv: float32 [768, 2, 1536], P('dp', None, 'mp')
- grad_cross_out: float32 [1536, 1536], P('mp', 'dp')
- grad_in: float32 [1536, 2, 6144], P('dp', None, 'mp')
- grad_out: float32 [6144, 1536], P('mp', 'dp')
- grad_gains: float32 [3, 1536], P(None, 'dp')
- grad_b_in: float32 [2, 6144], P(None, ('mp', 'dp'))
- grad_b_out: float32 [1536], P('dp')
The draws below stay inside these ranges and needn't reach their ends.
Inputs may be any that keep to these rules, and one draw needn't show every extreme that they name: Rows 1 to frame_counts[c] of clip c carry audio; one clip of every draw has 1023. `text_counts`: one clip of every draw has all 128 text tokens live.
All inputs are finite; a program needn't handle non-finite values.
Results may differ from the reference program's by a relative error of at most 0.018.
Values may be sent and summed in bfloat16 or wider, within the bound.
A program may use at most 192 MiB of HBM per device.

```python
import jax
import jax.numpy as jnp
from jax import lax

D = 1536
H = 24
HD = 64
FF = 6144
CTX_DIM = 768
CTX = 128
FRAMES = 1024
CLIPS = 4
TOKENS = 4096


def draw_tokens(key, part):
    key = jax.random.fold_in(key, 11)
    base_key, column_key, row_key = jax.random.split(key, 3)
    columns = 10.0 ** jax.random.uniform(column_key, (1, D), jnp.float32, -0.5, 0.5)
    row_scale = 10.0 ** jax.random.uniform(row_key, (TOKENS, 1), jnp.float32, -0.5, 0.5)
    base_draw = jnp.clip(jax.random.normal(base_key, (TOKENS, D), jnp.float32), -4.0, 4.0)
    return (base_draw * columns * row_scale).astype(jnp.bfloat16)


def draw_frame_counts(key, part):
    key = jax.random.fold_in(key, 23)
    count_key, pick_key = jax.random.split(key)
    counts = jax.random.randint(count_key, (CLIPS,), FRAMES // 2, FRAMES, jnp.int32)
    chosen = jax.random.randint(pick_key, (), 0, CLIPS, jnp.int32)
    return counts.at[chosen].set(FRAMES - 1)


def draw_text_counts(key, part):
    key = jax.random.fold_in(key, 37)
    count_key, pick_key = jax.random.split(key)
    counts = jax.random.randint(count_key, (CLIPS,), CTX // 2 + 1, CTX + 1, jnp.int32)
    chosen = jax.random.randint(pick_key, (), 0, CLIPS, jnp.int32)
    return counts.at[chosen].set(CTX)


def with_spikes(entries, key, source, target, parts, factor):
    def block_of(axis_at):
        return (jnp.arange(entries.shape[axis_at]) // (entries.shape[axis_at] // parts)).reshape((-1,) + (1,) * (entries.ndim - 1 - axis_at))

    one_side = jax.random.permutation(key, parts)[block_of(target)]
    far = (block_of(target) + parts // 2) % parts
    return jnp.where((block_of(source) == one_side) | (block_of(source) == far), factor * entries, entries)


def block_levels(stream_key, shape, cuts, smallest, high):
    gain = 1.0
    for dim, shards_of in cuts:
        steps = jax.random.uniform(jax.random.fold_in(jax.random.fold_in(stream_key, 6), dim), (shards_of,), jnp.float32, smallest / len(cuts), high / len(cuts))
        gain = gain * jnp.repeat(jnp.exp(steps), shape[dim] // shards_of).reshape((-1,) + (1,) * (len(shape) - 1 - dim))
    return gain


def noise(stream_key, dims, deviation, most, cuts=(), kind=jnp.bfloat16):
    gain = block_levels(stream_key, dims, cuts, -0.22, 0.18) if cuts else 1.0
    drawn = jax.random.normal(stream_key, dims, jnp.float32) * deviation * gain
    return jnp.minimum(jnp.maximum(drawn, -most), most).astype(kind)


def heavy_noise(key, extent, scale, bound, pieces, heavy, held_as=jnp.bfloat16):
    values = scale * jax.random.normal(key, extent, jnp.float32)
    if pieces:
        values = values * block_levels(key, extent, pieces, -0.22, 0.18)
    return jnp.clip(with_spikes(values, jax.random.fold_in(key, 3), *heavy), -bound, bound).astype(held_as)


def setup_inputs(seed: int = 0) -> dict:
    key_of = jax.random.split(jax.random.key(seed), 16)
    return {
        "tokens": draw_tokens(jax.random.fold_in(key_of[15], 71), 0),
        "context": noise(key_of[1], (CLIPS * CTX, CTX_DIM), 1.0, 6.0, ((0, 8),)),
        "frame_counts": draw_frame_counts(jax.random.fold_in(key_of[15], 71), 0),
        "text_counts": draw_text_counts(jax.random.fold_in(key_of[15], 71), 0),
        "w_qkv": noise(key_of[4], (D, 3, D), D ** -0.5, 0.15625, ((0, 8), (2, 4))),
        "w_attn_out": noise(key_of[5], (D, D), (max(1, 3 * D // FRAMES)) ** -0.5, 3.0, ((0, 4), (1, 8))),
        "w_cross_q": noise(key_of[6], (D, D), D ** -0.5, 0.15625, ((0, 8), (1, 4))),
        "w_cross_kv": noise(key_of[7], (CTX_DIM, 2, D), CTX_DIM ** -0.5, 0.21875, ((0, 8), (2, 4))),
        "w_cross_out": noise(key_of[8], (D, D), (max(1, 3 * D // CTX)) ** -0.5, 1.0, ((0, 4), (1, 8))),
        "w_in": noise(key_of[9], (D, 2, FF), D ** -0.5, 0.15625, ((0, 8), (2, 4))),
        "w_out": noise(key_of[10], (FF, D), FF ** -0.5, 0.078125, ((0, 4), (1, 8))),
        "norm_gains": jnp.clip(1.0 + 0.1 * jax.random.normal(key_of[11], (3, D), jnp.float32), 0.5, 1.5).astype(jnp.bfloat16),
        "b_in": noise(key_of[12], (2, FF), 0.3, 1.5, ((1, 32),)),
        "b_out": noise(key_of[13], (D,), 0.3, 1.5, ((0, 8),)),
        "cotangent": heavy_noise(key_of[14], (TOKENS, D), 1.0, 6.0, ((0, 8),), (0, 1, 8, 2.0)),
    }


@jax.custom_vjp
def low(v):
    return lax.optimization_barrier(v.astype(jnp.bfloat16)).astype(jnp.float32)

@jax.custom_vjp
def low_back(v):
    return v

def low_keep(v):
    return (low(v), None)

def low_pass(kept, grad):
    return (grad,)

def back_keep(v):
    return (v, None)

def back_low(kept, grad):
    return (low(grad),)
low.defvjp(low_keep, low_pass)
low_back.defvjp(back_keep, back_low)
epsilon = 1e-05

def product(left_side, right_side):
    return jnp.dot(left_side, right_side, precision=lax.Precision.HIGHEST, preferred_element_type=jnp.float32)

def layer_norm(values, gain_row):
    centered = values - lax.optimization_barrier(jnp.mean(values, axis=-1, keepdims=True))
    spread = lax.optimization_barrier(jnp.mean(centered * centered, axis=-1, keepdims=True))
    return centered * lax.rsqrt(spread + epsilon) * gain_row

def rotate(tensor, positions):
    quarter = tensor.shape[-1] // 4
    frequency = 10000.0 ** (-jnp.arange(quarter, dtype=jnp.float32) / quarter)
    angles = positions[:, None] * frequency[None, :]
    cosine = jnp.cos(angles)[:, None, :]
    sine_part = jnp.sin(angles)[:, None, :]
    first_part = tensor[..., :quarter]
    second = tensor[..., quarter:2 * quarter]
    return jnp.concatenate([first_part * cosine - second * sine_part, second * cosine + first_part * sine_part, tensor[..., 2 * quarter:]], axis=-1)

def attend(queries, key_all, value_all, key_live):
    scores = low_back(jnp.einsum('qhd,khd->hqk', queries, key_all, precision=lax.Precision.HIGHEST) * HD ** (-0.5))
    scores = jnp.where(key_live[None, None, :], scores, -1e+30)
    row_max = lax.optimization_barrier(jnp.max(scores, axis=-1, keepdims=True))
    weights = jnp.exp(scores - row_max)
    attn_probs = weights / lax.optimization_barrier(jnp.sum(weights, axis=-1, keepdims=True))
    return jnp.einsum('hqk,khd->qhd', low(attn_probs), value_all, precision=lax.Precision.HIGHEST)

def clip_forward(tokens_in, context_in, frame_live, text_live, params):
    w_qkv, w_attn_out, w_cross_q, w_cross_kv, w_cross_out, w_in, w_out, norm_gains, b_in, b_out = params
    positions = jnp.arange(FRAMES, dtype=jnp.float32)
    key_live = jnp.arange(FRAMES) <= frame_live
    token_live = jnp.arange(CTX) < text_live
    h_one = low(layer_norm(tokens_in, norm_gains[0]))
    qkv = product(h_one, w_qkv.reshape(D, 3 * D)).reshape(FRAMES, 3, H, HD)
    queries = low(rotate(low_back(qkv[:, 0]), positions))
    key_all = low(rotate(low_back(qkv[:, 1]), positions))
    value_all = low(low_back(qkv[:, 2]))
    self_out = low(low_back(attend(queries, key_all, value_all, key_live))).reshape(FRAMES, D)
    x_one = tokens_in + low_back(product(self_out, w_attn_out))
    h_two = low(layer_norm(x_one, norm_gains[1]))
    cross_queries = low(low_back(product(h_two, w_cross_q))).reshape(FRAMES, H, HD)
    text_kv = product(context_in, w_cross_kv.reshape(CTX_DIM, 2 * D)).reshape(CTX, 2, H, HD)
    text_keys = low(low_back(text_kv[:, 0]))
    text_values = low(low_back(text_kv[:, 1]))
    cross_out = low(low_back(attend(cross_queries, text_keys, text_values, token_live))).reshape(FRAMES, D)
    x_two = x_one + low_back(product(cross_out, w_cross_out))
    h_three = low(layer_norm(x_two, norm_gains[2]))
    both = product(h_three, w_in.reshape(D, 2 * FF)).reshape(FRAMES, 2, FF) + b_in
    gate = low_back(both[:, 0])
    upward = low_back(both[:, 1])
    hidden = low(gate * jax.nn.sigmoid(gate) * upward)
    return x_two + product(hidden, w_out) + b_out

def reference(tokens, context, frame_counts, text_counts, w_qkv, w_attn_out, w_cross_q, w_cross_kv, w_cross_out, w_in, w_out, norm_gains, b_in, b_out, cotangent):
    params = tuple((weight.astype(jnp.float32) for weight in (w_qkv, w_attn_out, w_cross_q, w_cross_kv, w_cross_out, w_in, w_out, norm_gains, b_in, b_out)))
    clip_tokens = tokens.astype(jnp.float32).reshape(CLIPS, FRAMES, D)
    clip_context = context.astype(jnp.float32).reshape(CLIPS, CTX, CTX_DIM)
    clip_grads = cotangent.astype(jnp.float32).reshape(CLIPS, FRAMES, D)

    def scan_step(totals, clip_item):
        tokens_clip, context_clip, grad_clip, frame_live, text_live = clip_item

        def forward(tokens_in, *weights):
            return clip_forward(tokens_in, context_clip, frame_live, text_live, weights)
        result, pull = jax.vjp(forward, tokens_clip, *params)
        gradients = pull(grad_clip)
        summed = tuple((total + piece for total, piece in zip(totals, gradients[1:])))
        return (summed, (result.astype(jnp.bfloat16), gradients[0]))
    start = tuple((jnp.zeros(weight.shape, jnp.float32) for weight in params))
    totals, (mixed, grad_tokens) = lax.scan(scan_step, start, (clip_tokens, clip_context, clip_grads, frame_counts, text_counts))
    return (mixed.reshape(TOKENS, D), grad_tokens.reshape(TOKENS, D), totals[0], totals[1], totals[2], totals[3], totals[4], totals[5], totals[6], totals[7], totals[8], totals[9])
```

```python
import functools

import jax
import jax.numpy as jnp
from jax import lax
from jax.experimental import pallas as pl
from jax.experimental.pallas import tpu as pltpu
from jax.sharding import PartitionSpec as P

HD = 64
MESH = pl.DeviceIdType.MESH
HBM = pl.BlockSpec(memory_space=pl.ANY)


def greet(peers):
    barrier = pltpu.get_barrier_semaphore()
    for peer in peers:
        pl.semaphore_signal(barrier, inc=1, device_id=peer, device_id_type=MESH)
    pl.semaphore_wait(barrier, len(peers))


def send(src, dst, send_sem, recv_sem, peer):
    return pltpu.make_async_remote_copy(
        src_ref=src,
        dst_ref=dst,
        send_sem=send_sem,
        recv_sem=recv_sem,
        device_id=peer,
        device_id_type=MESH,
    )


def dp_peers():
    d = lax.axis_index("dp")
    m = lax.axis_index("mp")
    return d, [(jnp.bitwise_xor(d, 1), m), (jnp.bitwise_xor(d, 2), m), (jnp.bitwise_xor(d, 4), m)]


def gather_kernel(count, *refs):
    ins, outs = refs[:count], refs[count : 2 * count]
    send_sems, recv_sems, local_sems = refs[2 * count :]
    d, (core, xn, yn) = dp_peers()
    greet((core, xn, yn))
    started = []
    local = []

    def go(a, k, block, rows, peer):
        lo, size = rows
        part = outs[a].at[block, pl.ds(lo, size)] if size else outs[a].at[block]
        cp = send(part, part, send_sems.at[a, k], recv_sems.at[a, k], peer)
        cp.start()
        started.append(cp)

    def own(a, k, peer):
        cp = send(ins[a], outs[a].at[d], send_sems.at[a, k], recv_sems.at[a, k], peer)
        cp.start()
        started.append(cp)

    def got(a, k, block, rows, peer):
        lo, size = rows
        part = outs[a].at[block, pl.ds(lo, size)] if size else outs[a].at[block]
        send(part, part, send_sems.at[a, k], recv_sems.at[a, k], peer).wait_recv()

    bx, by, bd = jnp.bitwise_xor(d, 2), jnp.bitwise_xor(d, 4), jnp.bitwise_xor(d, 6)
    b1 = jnp.bitwise_xor(d, 1)
    whole = (0, 0)
    for a in range(count):
        own(a, 0, xn)
        own(a, 1, yn)
        own(a, 2, core)
        cp = pltpu.make_async_copy(ins[a], outs[a].at[d], local_sems.at[a])
        cp.start()
        local.append(cp)
    for a in range(count):
        half = ins[a].shape[0] // 2
        top, bottom = (0, half), (half, half)
        got(a, 0, bx, whole, xn)
        go(a, 3, bx, top, yn)
        go(a, 5, bx, whole, core)
        got(a, 1, by, whole, yn)
        go(a, 4, by, bottom, xn)
        go(a, 6, by, whole, core)
        got(a, 3, bd, top, yn)
        go(a, 7, bd, top, core)
        got(a, 4, bd, bottom, xn)
        go(a, 8, bd, bottom, core)
    for a in range(count):
        half = ins[a].shape[0] // 2
        top, bottom = (0, half), (half, half)
        got(a, 2, b1, whole, core)
        got(a, 5, jnp.bitwise_xor(bx, 1), whole, core)
        got(a, 6, jnp.bitwise_xor(by, 1), whole, core)
        got(a, 7, jnp.bitwise_xor(bd, 1), top, core)
        got(a, 8, jnp.bitwise_xor(bd, 1), bottom, core)
    for cp in started:
        cp.wait_send()
    for cp in local:
        cp.wait()


def gather_all(arrays, collective_id):
    count = len(arrays)
    outs = pl.pallas_call(
        functools.partial(gather_kernel, count),
        out_shape=[jax.ShapeDtypeStruct((8,) + a.shape, a.dtype) for a in arrays],
        in_specs=[HBM] * count,
        out_specs=[HBM] * count,
        scratch_shapes=[
            pltpu.SemaphoreType.DMA((count, 9)),
            pltpu.SemaphoreType.DMA((count, 9)),
            pltpu.SemaphoreType.DMA((count,)),
        ],
        compiler_params=pltpu.CompilerParams(collective_id=collective_id, has_side_effects=True),
        name="gather_all",
    )(*arrays)
    return [o.reshape((-1,) + o.shape[2:]) for o in outs]


CH = 32


def line_kernel(n, x_ref, o_ref, own, got, res, load_sem, send_sems, recv_sems, back_send, back_recv):
    d = lax.axis_index("dp")
    z = lax.axis_index("mp")
    rows = x_ref.shape[0]
    half = rows // 2
    chunks = half // CH
    load = pltpu.make_async_copy(x_ref, own, load_sem)
    load.start()
    barrier = pltpu.get_barrier_semaphore()

    @pl.when(z > 0)
    def _():
        pl.semaphore_signal(barrier, inc=1, device_id=(d, z - 1), device_id_type=MESH)

    @pl.when(z < n - 1)
    def _():
        pl.semaphore_signal(barrier, inc=1, device_id=(d, z + 1), device_id_type=MESH)

    @pl.when((z > 0) & (z < n - 1))
    def _():
        pl.semaphore_wait(barrier, 2)

    @pl.when((z == 0) | (z == n - 1))
    def _():
        pl.semaphore_wait(barrier, 1)

    load.wait()

    def out_copy(f, c, nxt):
        at = pl.ds(pl.multiple_of(f * half + c * CH, CH), CH)
        return send(own.at[at], got.at[at], send_sems.at[f, c], recv_sems.at[f, c], (d, nxt))

    def back_copy(f, c, prv):
        at = pl.ds(pl.multiple_of(f * half + c * CH, CH), CH)
        return send(res.at[at], res.at[at], back_send.at[f, c], back_recv.at[f, c], (d, prv))

    def slot(s, carry):
        for f in range(2):
            p = z if f else n - 1 - z
            nxt = z + 1 if f else z - 1
            prv = z - 1 if f else z + 1
            c = s - p

            @pl.when((c >= 0) & (c < chunks))
            def _():
                at = pl.ds(pl.multiple_of(f * half + c * CH, CH), CH)

                @pl.when(p > 0)
                def _():
                    out_copy(f, c, nxt).wait_recv()
                    own[at] = (own[at].astype(jnp.float32) + got[at].astype(jnp.float32)).astype(
                        jnp.bfloat16
                    )

                @pl.when(p < n - 1)
                def _():
                    out_copy(f, c, nxt).start()

                @pl.when(p == n - 1)
                def _():
                    res[at] = own[at]
                    back_copy(f, c, prv).start()

            b = s - 2 * (n - 1) + p

            @pl.when((b >= 0) & (b < chunks) & (p < n - 1))
            def _():
                back_copy(f, b, prv).wait_recv()

                @pl.when(p > 0)
                def _():
                    back_copy(f, b, prv).start()

        return carry

    lax.fori_loop(0, chunks + 2 * (n - 1), slot, 0)

    def drain(c, carry):
        for f in range(2):
            p = z if f else n - 1 - z
            nxt = z + 1 if f else z - 1
            prv = z - 1 if f else z + 1

            @pl.when(p < n - 1)
            def _():
                out_copy(f, c, nxt).wait_send()

            @pl.when(p > 0)
            def _():
                back_copy(f, c, prv).wait_send()

        return carry

    lax.fori_loop(0, chunks, drain, 0)
    store = pltpu.make_async_copy(res, o_ref, load_sem)
    store.start()
    store.wait()


def line_sum(x, n, collective_id):
    shape = x.shape
    chunks = shape[0] // 2 // CH
    return pl.pallas_call(
        functools.partial(line_kernel, n),
        out_shape=jax.ShapeDtypeStruct(shape, x.dtype),
        in_specs=[HBM],
        out_specs=HBM,
        scratch_shapes=[pltpu.VMEM(shape, x.dtype)] * 3
        + [pltpu.SemaphoreType.DMA]
        + [pltpu.SemaphoreType.DMA((2, chunks))] * 4,
        compiler_params=pltpu.CompilerParams(
            collective_id=collective_id, has_side_effects=True, vmem_limit_bytes=32 * 2**20
        ),
        name="line_sum",
    )(x)


def scatter_kernel(count, *refs):
    ins, outs = refs[:count], refs[count : 2 * count]
    rest = refs[2 * count :]
    own, got, one, two, out_v = [rest[i * count : (i + 1) * count] for i in range(5)]
    send_sems, recv_sems, local_sems = rest[5 * count :]
    d, (core, xn, yn) = dp_peers()
    c = lax.rem(d, 2)
    x = lax.rem(d // 2, 2)
    y = d // 4
    greet((core, xn, yn))
    copies = [{} for _ in range(count)]
    loads, stores = [], []

    def go(a, k, src, dst, peer):
        cp = send(src, dst, send_sems.at[a, k], recv_sems.at[a, k], peer)
        cp.start()
        copies[a][k] = cp

    for a in range(count):
        go(a, 0, ins[a].at[:, 1 - c], got[a], core)
        cp = pltpu.make_async_copy(ins[a].at[:, c], own[a], local_sems.at[a])
        cp.start()
        loads.append(cp)

    def add_core(a):
        loads[a].wait()
        copies[a][0].wait_recv()
        rows = own[a].shape[1]

        def tile(i, carry):
            j, t = i // (rows // 16), lax.rem(i, rows // 16)
            at = pl.ds(pl.multiple_of(t * 16, 16), 16)
            own[a][j, at] = (own[a][j, at].astype(jnp.float32) + got[a][j, at].astype(jnp.float32)).astype(
                jnp.bfloat16
            )
            return carry

        lax.fori_loop(0, 4 * (rows // 16), tile, 0)
        half = rows // 2
        top, bottom = pl.ds(0, half), pl.ds(half, half)
        for b in range(2):
            go(a, 1 + b, own[a].at[2 * b + 1 - x, top], one[a].at[0, b], xn)
            go(a, 3 + b, own[a].at[2 * (1 - y) + b, bottom], one[a].at[1, b], yn)

    def plus(a, at_block, lo, part):
        half = own[a].shape[1] // 2

        def tile(t, carry):
            at = pl.ds(pl.multiple_of(lo + t * 16, 16), 16)
            frm = pl.ds(pl.multiple_of(t * 16, 16), 16)
            own[a][at_block, at] = (
                own[a][at_block, at].astype(jnp.float32) + part[frm].astype(jnp.float32)
            ).astype(jnp.bfloat16)
            return carry

        lax.fori_loop(0, half // 16, tile, 0)

    def add_one(a):
        half = own[a].shape[1] // 2
        top, bottom = pl.ds(0, half), pl.ds(half, half)
        for b in range(2):
            copies[a][1 + b].wait_recv()
            plus(a, 2 * b + x, 0, one[a].at[0, b])
            copies[a][3 + b].wait_recv()
            plus(a, 2 * y + b, half, one[a].at[1, b])
        go(a, 5, own[a].at[2 * (1 - y) + x, top], two[a].at[0], yn)
        go(a, 6, own[a].at[2 * y + 1 - x, bottom], two[a].at[1], xn)

    def add_two(a):
        half = own[a].shape[1] // 2
        for part in range(2):
            copies[a][5 + part].wait_recv()

            def tile(t, carry, part=part):
                at = pl.ds(pl.multiple_of(part * half + t * 16, 16), 16)
                frm = pl.ds(pl.multiple_of(t * 16, 16), 16)
                out_v[a][at] = own[a][2 * y + x, at].astype(jnp.float32) + two[a][part, frm].astype(jnp.float32)
                return carry

            lax.fori_loop(0, half // 16, tile, 0)
        cp = pltpu.make_async_copy(out_v[a], outs[a], local_sems.at[a])
        cp.start()
        stores.append(cp)

    for s in range(count + 2):
        if s < count:
            add_core(s)
        if 0 <= s - 1 < count:
            add_one(s - 1)
        if 0 <= s - 2 < count:
            add_two(s - 2)
    for a in range(count):
        for cp in copies[a].values():
            cp.wait_send()
    for cp in stores:
        cp.wait()


def scatter_all(arrays, collective_id):
    count = len(arrays)
    views = [a.reshape(4, 2, a.shape[0] // 8, a.shape[1]) for a in arrays]
    sizes = [v.shape[2:] for v in views]
    bf = jnp.bfloat16
    return pl.pallas_call(
        functools.partial(scatter_kernel, count),
        out_shape=[jax.ShapeDtypeStruct(s, jnp.float32) for s in sizes],
        in_specs=[HBM] * count,
        out_specs=[HBM] * count,
        scratch_shapes=[pltpu.VMEM((4,) + s, bf) for s in sizes]
        + [pltpu.VMEM((4,) + s, bf) for s in sizes]
        + [pltpu.VMEM((2, 2, s[0] // 2, s[1]), bf) for s in sizes]
        + [pltpu.VMEM((2, s[0] // 2, s[1]), bf) for s in sizes]
        + [pltpu.VMEM(s, jnp.float32) for s in sizes]
        + [
            pltpu.SemaphoreType.DMA((count, 7)),
            pltpu.SemaphoreType.DMA((count, 7)),
            pltpu.SemaphoreType.DMA((count,)),
        ],
        compiler_params=pltpu.CompilerParams(
            collective_id=collective_id, has_side_effects=True, vmem_limit_bytes=60 * 2**20
        ),
        name="scatter_all",
    )(*views)


epsilon = 1e-05


def from_partner(block, axis, stride):
    count = lax.axis_size(axis)
    route = []
    for low in range(count):
        high = low | 1 << stride
        if high != low and high < count:
            route += [(low, high), (high, low)]
    return lax.ppermute(block, axis, route)


def layer_norm(values, gain_row):
    centered = values - jnp.mean(values, axis=-1, keepdims=True)
    spread = jnp.mean(centered * centered, axis=-1, keepdims=True)
    return centered * lax.rsqrt(spread + epsilon) * gain_row


def rotate(tensor, positions):
    quarter = tensor.shape[-1] // 4
    frequency = 10000.0 ** (-jnp.arange(quarter, dtype=jnp.float32) / quarter)
    angles = positions[:, None] * frequency[None, :]
    cosine = jnp.cos(angles)[:, None, :]
    sine_part = jnp.sin(angles)[:, None, :]
    first_part = tensor[..., :quarter]
    second = tensor[..., quarter : 2 * quarter]
    return jnp.concatenate(
        [
            first_part * cosine - second * sine_part,
            second * cosine + first_part * sine_part,
            tensor[..., 2 * quarter :],
        ],
        axis=-1,
    )


def gated_unit(both):
    gate = both[:, 0]
    return gate * jax.nn.sigmoid(gate) * both[:, 1]


def in_order(own_part, other_part, which_half):
    lower_first = jnp.concatenate([own_part, other_part], axis=0)
    upper_first = jnp.concatenate([other_part, own_part], axis=0)
    return jnp.where(which_half == 0, lower_first, upper_first)


def own_rows(whole, which_half, row_count):
    return lax.dynamic_slice_in_dim(whole, which_half * row_count, row_count, 0)


def partner_rows(whole, which_half, row_count):
    return lax.dynamic_slice_in_dim(whole, (1 - which_half) * row_count, row_count, 0)


def masked_scores(query_block, key_all, key_live):
    scale = query_block.shape[-1] ** (-0.5)
    raw_scores = (
        jnp.einsum("qhd,khd->hqk", query_block, key_all, preferred_element_type=jnp.float32) * scale
    )
    return jnp.where(key_live[None, None, :], raw_scores, -1e30)


def attend_forward(queries, key_all, value_all, key_live):
    row_count, head_count, head_size = queries.shape
    block_rows = min(512, row_count)
    blocks = queries.reshape(row_count // block_rows, block_rows, head_count, head_size)

    def per_block(query_block):
        scores = masked_scores(query_block, key_all, key_live)
        row_max = jnp.max(scores, axis=-1, keepdims=True)
        weights = jnp.exp(scores - row_max)
        row_total = jnp.sum(weights, axis=-1, keepdims=True)
        attn_probs = weights / row_total
        block_out = jnp.einsum(
            "hqk,khd->qhd",
            attn_probs.astype(jnp.bfloat16),
            value_all,
            preferred_element_type=jnp.float32,
        )
        return (block_out, row_max + jnp.log(row_total))

    outputs, log_sums = lax.map(per_block, blocks)
    return (outputs.reshape(row_count, head_count, head_size), log_sums)


def attend_backward(queries, key_all, value_all, key_live, log_sums, grad_out):
    row_count, head_count, head_size = queries.shape
    block_rows = min(512, row_count)
    block_shape = (row_count // block_rows, block_rows, head_count, head_size)
    scale = head_size ** (-0.5)

    def per_block(running, block_item):
        query_block, grad_block, lse_block = block_item
        attn_probs = jnp.exp(masked_scores(query_block, key_all, key_live) - lse_block)
        grad_probs = jnp.einsum(
            "qhd,khd->hqk", grad_block, value_all, preferred_element_type=jnp.float32
        )
        row_inner = jnp.sum(attn_probs * grad_probs, axis=-1, keepdims=True)
        grad_scores = (attn_probs * (grad_probs - row_inner)).astype(jnp.bfloat16)
        grad_query = (
            jnp.einsum("hqk,khd->qhd", grad_scores, key_all, preferred_element_type=jnp.float32)
            * scale
        )
        grad_key = (
            running[0]
            + jnp.einsum(
                "hqk,qhd->khd", grad_scores, query_block, preferred_element_type=jnp.float32
            )
            * scale
        )
        grad_value = running[1] + jnp.einsum(
            "hqk,qhd->khd",
            attn_probs.astype(jnp.bfloat16),
            grad_block,
            preferred_element_type=jnp.float32,
        )
        return ((grad_key, grad_value), grad_query)

    zero_keys = jnp.zeros(key_all.shape, jnp.float32)
    (grad_key, grad_value), grad_query = lax.scan(
        per_block,
        (zero_keys, zero_keys),
        (queries.reshape(block_shape), grad_out.reshape(block_shape), log_sums),
    )
    return (grad_query.reshape(row_count, head_count, head_size), grad_key, grad_value)


def branch_total(partial_sum):
    return lax.psum(partial_sum, "mp")


def grad_total(partial_sum):
    return lax.psum(partial_sum, "mp")


def near_body(
    tokens,
    context,
    frame_counts,
    text_counts,
    w_qkv,
    w_attn_out,
    w_cross_q,
    w_cross_kv,
    w_cross_out,
    w_in,
    w_out,
    norm_gains,
    b_in,
    b_out,
    cotangent,
):
    n = lax.axis_size("mp")
    shard, _, head_cols = w_qkv.shape
    unit_cols = w_in.shape[2]
    bf = jnp.bfloat16
    vec = jnp.concatenate([norm_gains, b_in, b_out[None]], axis=0)
    vec = jnp.pad(vec, ((0, 32 - vec.shape[0]), (0, 256 - shard)))
    vec_full, qkv_full, small_full, ckv_full, out_t, in_full = gather_all(
        [
            vec,
            w_qkv.reshape(shard, 3 * head_cols),
            jnp.concatenate([w_attn_out.T, w_cross_q, w_cross_out.T], axis=1),
            w_cross_kv.reshape(w_cross_kv.shape[0], 2 * head_cols),
            w_out.T,
            w_in.reshape(shard, 2 * unit_cols),
        ],
        0,
    )
    row_count, model_width = tokens.shape
    text_rows, text_width = context.shape
    vec_rows = vec_full.reshape(8, 32, 256)[:, :6, :shard].transpose(1, 0, 2).reshape(6, model_width)
    gain_rows = vec_rows[:3].astype(jnp.float32)
    b_in_full = vec_rows[3:5].astype(jnp.float32)
    b_out_full = vec_rows[5].astype(jnp.float32)
    ao_t = small_full[:, :head_cols]
    cross_q_full = small_full[:, head_cols : 2 * head_cols]
    co_t = small_full[:, 2 * head_cols :]
    ids = iter(range(2, 12))

    def total(partial_sum):
        return line_sum(partial_sum.astype(bf), n, next(ids)).astype(jnp.float32)

    def nt(a, b):
        return lax.dot_general(a, b, (((1,), (1,)), ((), ())), preferred_element_type=jnp.float32)

    def tn(a, b):
        return lax.dot_general(a, b, (((0,), (0,)), ((), ())), preferred_element_type=jnp.float32)

    head_count = head_cols // HD
    device_row = lax.axis_index("dp")
    which_half = device_row % 2
    clip_index = device_row // 2
    frame_live = lax.dynamic_index_in_dim(frame_counts, clip_index, 0, keepdims=False)
    text_live = lax.dynamic_index_in_dim(text_counts, clip_index, 0, keepdims=False)
    positions = (which_half * row_count + jnp.arange(row_count)).astype(jnp.float32)
    key_live = jnp.arange(2 * row_count) <= frame_live
    token_live = jnp.arange(2 * text_rows) < text_live
    tokens_f = tokens.astype(jnp.float32)
    grad_y = cotangent.astype(jnp.float32)
    norm_one, pull_one = jax.vjp(layer_norm, tokens_f, gain_rows[0])
    h_one = norm_one.astype(bf)
    qkv = jnp.dot(h_one, qkv_full, preferred_element_type=jnp.float32).reshape(
        row_count, 3, head_count, HD
    )
    queries = rotate(qkv[:, 0], positions).astype(bf)
    own_keys = rotate(qkv[:, 1], positions).astype(bf).reshape(row_count, head_cols)
    own_values = qkv[:, 2].astype(bf).reshape(row_count, head_cols)
    own_text = jnp.dot(context, ckv_full, preferred_element_type=jnp.float32).astype(bf)
    other = from_partner((own_keys, own_values, own_text), "dp", 0)
    key_all = in_order(own_keys, other[0], which_half).reshape(2 * row_count, head_count, HD)
    value_all = in_order(own_values, other[1], which_half).reshape(2 * row_count, head_count, HD)
    text_all = in_order(own_text, other[2], which_half).reshape(2 * text_rows, 2, head_count, HD)
    text_keys = text_all[:, 0]
    text_values = text_all[:, 1]
    self_attn, self_lse = attend_forward(queries, key_all, value_all, key_live)
    self_out = self_attn.reshape(row_count, head_cols).astype(bf)
    x_one = tokens_f + total(nt(self_out, ao_t))
    norm_two, pull_two = jax.vjp(layer_norm, x_one, gain_rows[1])
    h_two = norm_two.astype(bf)
    cross_queries = (
        jnp.dot(h_two, cross_q_full, preferred_element_type=jnp.float32)
        .astype(bf)
        .reshape(row_count, head_count, HD)
    )
    cross_attn, cross_lse = attend_forward(cross_queries, text_keys, text_values, token_live)
    cross_out = cross_attn.reshape(row_count, head_cols).astype(bf)
    x_two = x_one + total(nt(cross_out, co_t))
    norm_three, pull_three = jax.vjp(layer_norm, x_two, gain_rows[2])
    h_three = norm_three.astype(bf)
    both = (
        jnp.dot(h_three, in_full, preferred_element_type=jnp.float32).reshape(
            row_count, 2, unit_cols
        )
        + b_in_full
    )
    hidden_f, pull_unit = jax.vjp(gated_unit, both)
    hidden = hidden_f.astype(bf)
    mixed = (x_two + total(nt(hidden, out_t)) + b_out_full).astype(bf)
    grad_out_w = tn(cotangent, hidden)
    grad_b_out = jnp.sum(grad_y, axis=0)
    grad_hidden = jnp.dot(cotangent, out_t, preferred_element_type=jnp.float32)
    grad_both = pull_unit(grad_hidden)[0].astype(bf).reshape(row_count, 2 * unit_cols)
    grad_b_in = jnp.sum(grad_both, axis=0, dtype=jnp.float32).reshape(2, unit_cols)
    grad_in_w = tn(h_three, grad_both)
    grad_x_norm, grad_gain_three = pull_three(total(nt(grad_both, in_full)))
    grad_x_two = grad_y + grad_x_norm
    grad_two_b = grad_x_two.astype(bf)
    grad_cross_out_w = tn(grad_two_b, cross_out)
    grad_cross = (
        jnp.dot(grad_two_b, co_t, preferred_element_type=jnp.float32)
        .astype(bf)
        .reshape(row_count, head_count, HD)
    )
    grad_cq, grad_text_key, grad_text_value = attend_backward(
        cross_queries, text_keys, text_values, token_live, cross_lse, grad_cross
    )
    grad_cq_b = grad_cq.reshape(row_count, head_cols).astype(bf)
    grad_cross_q_w = tn(h_two, grad_cq_b)
    grad_text = jnp.stack([grad_text_key, grad_text_value], axis=1).reshape(
        2 * text_rows, 2 * head_cols
    )
    grad_x_norm, grad_gain_two = pull_two(total(nt(grad_cq_b, cross_q_full)))
    grad_x_one = grad_x_two + grad_x_norm
    grad_one_b = grad_x_one.astype(bf)
    grad_attn_out_w = tn(grad_one_b, self_out)
    grad_self = (
        jnp.dot(grad_one_b, ao_t, preferred_element_type=jnp.float32)
        .astype(bf)
        .reshape(row_count, head_count, HD)
    )
    grad_query, grad_key_all, grad_value_all = attend_backward(
        queries, key_all, value_all, key_live, self_lse, grad_self
    )
    grad_key_flat = grad_key_all.reshape(2 * row_count, head_cols)
    grad_value_flat = grad_value_all.reshape(2 * row_count, head_cols)
    back = from_partner(
        (
            partner_rows(grad_key_flat, which_half, row_count),
            partner_rows(grad_value_flat, which_half, row_count),
            partner_rows(grad_text, which_half, text_rows),
        ),
        "dp",
        0,
    )
    grad_key_own = (own_rows(grad_key_flat, which_half, row_count) + back[0]).reshape(
        row_count, head_count, HD
    )
    grad_value_own = own_rows(grad_value_flat, which_half, row_count) + back[1]
    grad_text_own = (own_rows(grad_text, which_half, text_rows) + back[2]).astype(bf)
    grad_query_raw = rotate(grad_query, -positions).reshape(row_count, head_cols)
    grad_key_raw = rotate(grad_key_own, -positions).reshape(row_count, head_cols)
    grad_qkv_b = (
        jnp.stack([grad_query_raw, grad_key_raw, grad_value_own], axis=1)
        .astype(bf)
        .reshape(row_count, 3 * head_cols)
    )
    grad_qkv_w = tn(h_one, grad_qkv_b)
    grad_cross_kv_w = tn(context, grad_text_own)
    grad_x_norm, grad_gain_one = pull_one(total(nt(grad_qkv_b, qkv_full)))
    grad_tokens = grad_x_one + grad_x_norm
    grad_small_w = jnp.concatenate([grad_attn_out_w, grad_cross_q_w, grad_cross_out_w], axis=1)
    g_out, g_in, g_small, g_ckv, g_qkv = scatter_all(
        [
            grad_out_w.astype(bf),
            grad_in_w.astype(bf),
            grad_small_w.astype(bf),
            grad_cross_kv_w.astype(bf),
            grad_qkv_w.astype(bf),
        ],
        1,
    )
    rows = jnp.concatenate(
        [grad_gain_one[None], grad_gain_two[None], grad_gain_three[None], grad_b_in, grad_b_out[None]]
    )
    vec_sum = lax.psum_scatter(rows, "dp", scatter_dimension=1, tiled=True)
    return (
        mixed,
        grad_tokens,
        g_qkv.reshape(shard, 3, head_cols),
        g_small[:, :head_cols].T,
        g_small[:, head_cols : 2 * head_cols],
        g_ckv.reshape(-1, 2, head_cols),
        g_small[:, 2 * head_cols :].T,
        g_in.reshape(shard, 2, unit_cols),
        g_out.T,
        vec_sum[:3],
        vec_sum[3:5],
        vec_sum[5],
    )


def body(
    tokens,
    context,
    frame_counts,
    text_counts,
    w_qkv,
    w_attn_out,
    w_cross_q,
    w_cross_kv,
    w_cross_out,
    w_in,
    w_out,
    norm_gains,
    b_in,
    b_out,
    cotangent,
):
    gathered = (
        lax.all_gather(w_qkv, "dp", axis=0, tiled=True),
        lax.all_gather(w_attn_out, "dp", axis=1, tiled=True),
        lax.all_gather(w_cross_q, "dp", axis=0, tiled=True),
        lax.all_gather(w_cross_kv, "dp", axis=0, tiled=True),
        lax.all_gather(w_cross_out, "dp", axis=1, tiled=True),
        lax.all_gather(w_in, "dp", axis=0, tiled=True),
        lax.all_gather(w_out, "dp", axis=1, tiled=True),
        lax.all_gather(norm_gains, "dp", axis=1, tiled=True),
        lax.all_gather(b_in, "dp", axis=1, tiled=True),
        lax.all_gather(b_out, "dp", axis=0, tiled=True),
    )
    (
        qkv_full,
        attn_out_full,
        cross_q_full,
        cross_kv_full,
        cross_out_full,
        in_full,
        out_full,
        gains_full,
        b_in_full,
        b_out_full,
    ) = gathered
    row_count, model_width = tokens.shape
    text_rows, text_width = context.shape
    head_cols = qkv_full.shape[2]
    unit_cols = in_full.shape[2]
    head_count = head_cols // HD
    device_row = lax.axis_index("dp")
    which_half = device_row % 2
    clip_index = device_row // 2
    frame_live = lax.dynamic_index_in_dim(frame_counts, clip_index, 0, keepdims=False)
    text_live = lax.dynamic_index_in_dim(text_counts, clip_index, 0, keepdims=False)
    positions = (which_half * row_count + jnp.arange(row_count)).astype(jnp.float32)
    key_live = jnp.arange(2 * row_count) <= frame_live
    token_live = jnp.arange(2 * text_rows) < text_live
    gain_rows = gains_full.astype(jnp.float32)
    tokens_f = tokens.astype(jnp.float32)
    grad_y_mine = cotangent.astype(jnp.float32)
    norm_one, pull_one = jax.vjp(layer_norm, tokens_f, gain_rows[0])
    h_one = norm_one.astype(jnp.bfloat16)
    qkv = jnp.dot(
        h_one, qkv_full.reshape(model_width, 3 * head_cols), preferred_element_type=jnp.float32
    ).reshape(row_count, 3, head_count, HD)
    queries = rotate(qkv[:, 0], positions).astype(jnp.bfloat16)
    own_keys = rotate(qkv[:, 1], positions).astype(jnp.bfloat16).reshape(row_count, head_cols)
    own_values = qkv[:, 2].astype(jnp.bfloat16).reshape(row_count, head_cols)
    own_text = jnp.dot(
        context,
        cross_kv_full.reshape(text_width, 2 * head_cols),
        preferred_element_type=jnp.float32,
    ).astype(jnp.bfloat16)
    other = from_partner((own_keys, own_values, own_text), "dp", 0)
    key_all = in_order(own_keys, other[0], which_half).reshape(2 * row_count, head_count, HD)
    value_all = in_order(own_values, other[1], which_half).reshape(2 * row_count, head_count, HD)
    text_all = in_order(own_text, other[2], which_half).reshape(2 * text_rows, 2, head_count, HD)
    text_keys = text_all[:, 0]
    text_values = text_all[:, 1]
    self_attn, self_lse = attend_forward(queries, key_all, value_all, key_live)
    self_out = self_attn.reshape(row_count, head_cols).astype(jnp.bfloat16)
    self_part = jnp.dot(self_out, attn_out_full, preferred_element_type=jnp.float32)
    x_one = tokens_f + branch_total(self_part)
    norm_two, pull_two = jax.vjp(layer_norm, x_one, gain_rows[1])
    h_two = norm_two.astype(jnp.bfloat16)
    cross_queries = (
        jnp.dot(h_two, cross_q_full, preferred_element_type=jnp.float32)
        .astype(jnp.bfloat16)
        .reshape(row_count, head_count, HD)
    )
    cross_attn, cross_lse = attend_forward(cross_queries, text_keys, text_values, token_live)
    cross_out = cross_attn.reshape(row_count, head_cols).astype(jnp.bfloat16)
    cross_part = jnp.dot(cross_out, cross_out_full, preferred_element_type=jnp.float32)
    x_two = x_one + branch_total(cross_part)
    norm_three, pull_three = jax.vjp(layer_norm, x_two, gain_rows[2])
    h_three = norm_three.astype(jnp.bfloat16)
    both = jnp.dot(
        h_three, in_full.reshape(model_width, 2 * unit_cols), preferred_element_type=jnp.float32
    ).reshape(row_count, 2, unit_cols) + b_in_full.astype(jnp.float32)
    hidden_f, pull_unit = jax.vjp(gated_unit, both)
    hidden = hidden_f.astype(jnp.bfloat16)
    down_part = jnp.dot(hidden, out_full, preferred_element_type=jnp.float32)
    mixed = (x_two + branch_total(down_part) + b_out_full.astype(jnp.float32)).astype(jnp.bfloat16)
    again = (
        lax.all_gather(w_qkv, "dp", axis=0, tiled=True),
        lax.all_gather(w_attn_out, "dp", axis=1, tiled=True),
        lax.all_gather(w_cross_q, "dp", axis=0, tiled=True),
        lax.all_gather(w_cross_out, "dp", axis=1, tiled=True),
        lax.all_gather(w_in, "dp", axis=0, tiled=True),
        lax.all_gather(w_out, "dp", axis=1, tiled=True),
    )
    qkv_back = again[0]
    attn_out_back = again[1]
    cross_q_back = again[2]
    cross_out_back = again[3]
    in_back = again[4]
    out_back = again[5]
    grad_y = cotangent.astype(jnp.float32)
    grad_out_w = jnp.dot(hidden.T, cotangent, preferred_element_type=jnp.float32)
    grad_b_out = jnp.sum(grad_y, axis=0)
    grad_hidden = jnp.dot(cotangent, out_back.T, preferred_element_type=jnp.float32)
    grad_both = pull_unit(grad_hidden)[0].astype(jnp.bfloat16).reshape(row_count, 2 * unit_cols)
    grad_b_in = jnp.sum(grad_both, axis=0, dtype=jnp.float32).reshape(2, unit_cols)
    grad_in_w = jnp.dot(h_three.T, grad_both, preferred_element_type=jnp.float32).reshape(
        model_width, 2, unit_cols
    )
    three_part = jnp.dot(
        grad_both, in_back.reshape(model_width, 2 * unit_cols).T, preferred_element_type=jnp.float32
    )
    grad_x_norm, grad_gain_three = pull_three(grad_total(three_part))
    grad_x_two = grad_y_mine + grad_x_norm
    grad_two_b = grad_x_two.astype(jnp.bfloat16)
    grad_cross_out_w = jnp.dot(cross_out.T, grad_two_b, preferred_element_type=jnp.float32)
    grad_cross = (
        jnp.dot(grad_two_b, cross_out_back.T, preferred_element_type=jnp.float32)
        .astype(jnp.bfloat16)
        .reshape(row_count, head_count, HD)
    )
    grad_cq, grad_text_key, grad_text_value = attend_backward(
        cross_queries, text_keys, text_values, token_live, cross_lse, grad_cross
    )
    grad_cq_b = grad_cq.reshape(row_count, head_cols).astype(jnp.bfloat16)
    grad_cross_q_w = jnp.dot(h_two.T, grad_cq_b, preferred_element_type=jnp.float32)
    grad_text = jnp.stack([grad_text_key, grad_text_value], axis=1).reshape(
        2 * text_rows, 2 * head_cols
    )
    two_part = jnp.dot(grad_cq_b, cross_q_back.T, preferred_element_type=jnp.float32)
    grad_x_norm, grad_gain_two = pull_two(grad_total(two_part))
    grad_x_one = grad_x_two + grad_x_norm
    grad_one_b = grad_x_one.astype(jnp.bfloat16)
    grad_attn_out_w = jnp.dot(self_out.T, grad_one_b, preferred_element_type=jnp.float32)
    grad_self = (
        jnp.dot(grad_one_b, attn_out_back.T, preferred_element_type=jnp.float32)
        .astype(jnp.bfloat16)
        .reshape(row_count, head_count, HD)
    )
    grad_query, grad_key_all, grad_value_all = attend_backward(
        queries, key_all, value_all, key_live, self_lse, grad_self
    )
    grad_key_flat = grad_key_all.reshape(2 * row_count, head_cols)
    grad_value_flat = grad_value_all.reshape(2 * row_count, head_cols)
    back = from_partner(
        (
            partner_rows(grad_key_flat, which_half, row_count),
            partner_rows(grad_value_flat, which_half, row_count),
            partner_rows(grad_text, which_half, text_rows),
        ),
        "dp",
        0,
    )
    grad_key_own = (own_rows(grad_key_flat, which_half, row_count) + back[0]).reshape(
        row_count, head_count, HD
    )
    grad_value_own = own_rows(grad_value_flat, which_half, row_count) + back[1]
    grad_text_own = (own_rows(grad_text, which_half, text_rows) + back[2]).astype(jnp.bfloat16)
    grad_query_raw = rotate(grad_query, -positions).reshape(row_count, head_cols)
    grad_key_raw = rotate(grad_key_own, -positions).reshape(row_count, head_cols)
    grad_qkv_b = (
        jnp.stack([grad_query_raw, grad_key_raw, grad_value_own], axis=1)
        .astype(jnp.bfloat16)
        .reshape(row_count, 3 * head_cols)
    )
    grad_qkv_w = jnp.dot(h_one.T, grad_qkv_b, preferred_element_type=jnp.float32).reshape(
        model_width, 3, head_cols
    )
    grad_cross_kv_w = jnp.dot(context.T, grad_text_own, preferred_element_type=jnp.float32).reshape(
        text_width, 2, head_cols
    )
    one_part = jnp.dot(
        grad_qkv_b,
        qkv_back.reshape(model_width, 3 * head_cols).T,
        preferred_element_type=jnp.float32,
    )
    grad_x_norm, grad_gain_one = pull_one(grad_total(one_part))
    grad_tokens = grad_x_one + grad_x_norm
    grad_gains = jnp.stack([grad_gain_one, grad_gain_two, grad_gain_three], axis=0)
    summed = (
        lax.psum_scatter(grad_qkv_w, "dp", scatter_dimension=0, tiled=True),
        lax.psum_scatter(grad_attn_out_w, "dp", scatter_dimension=1, tiled=True),
        lax.psum_scatter(grad_cross_q_w, "dp", scatter_dimension=0, tiled=True),
        lax.psum_scatter(grad_cross_kv_w, "dp", scatter_dimension=0, tiled=True),
        lax.psum_scatter(grad_cross_out_w, "dp", scatter_dimension=1, tiled=True),
        lax.psum_scatter(grad_in_w, "dp", scatter_dimension=0, tiled=True),
        lax.psum_scatter(grad_out_w, "dp", scatter_dimension=1, tiled=True),
        lax.psum_scatter(grad_gains, "dp", scatter_dimension=1, tiled=True),
        lax.psum_scatter(grad_b_in, "dp", scatter_dimension=1, tiled=True),
        lax.psum_scatter(grad_b_out, "dp", scatter_dimension=0, tiled=True),
    )
    return (
        mixed,
        grad_tokens,
        summed[0],
        summed[1],
        summed[2],
        summed[3],
        summed[4],
        summed[5],
        summed[6],
        summed[7],
        summed[8],
        summed[9],
    )


def solution(mesh):
    in_specs = (
        P("dp", None),
        P("dp", None),
        P(),
        P(),
        P("dp", None, "mp"),
        P("mp", "dp"),
        P("dp", "mp"),
        P("dp", None, "mp"),
        P("mp", "dp"),
        P("dp", None, "mp"),
        P("mp", "dp"),
        P(None, "dp"),
        P(None, ("mp", "dp")),
        P("dp"),
        P("dp", None),
    )
    out_specs = (
        P("dp", None),
        P("dp", None),
        P("dp", None, "mp"),
        P("mp", "dp"),
        P("dp", "mp"),
        P("dp", None, "mp"),
        P("mp", "dp"),
        P("dp", None, "mp"),
        P("mp", "dp"),
        P(None, "dp"),
        P(None, ("mp", "dp")),
        P("dp"),
    )
    near = mesh.shape["dp"] == 8
    return jax.shard_map(
        near_body if near else body,
        mesh=mesh,
        in_specs=in_specs,
        out_specs=out_specs,
        check_vma=False,
    )
```

```python
import functools

import jax
import jax.numpy as jnp
from jax import lax
from jax.experimental import pallas as pl
from jax.experimental.pallas import tpu as pltpu
from jax.sharding import PartitionSpec as P

HD = 64
MESH = pl.DeviceIdType.MESH
HBM = pl.BlockSpec(memory_space=pl.ANY)
BF = jnp.bfloat16
F32 = jnp.float32
epsilon = 1e-05
CH = 32
LAG = 2
DMA = pltpu.SemaphoreType.DMA
WHOLE = (0, 0)


def dot_nn(a, b):
    return lax.dot_general(a, b, (((1,), (0,)), ((), ())), preferred_element_type=F32)


def dot_nt(a, b):
    return lax.dot_general(a, b, (((1,), (1,)), ((), ())), preferred_element_type=F32)


def dot_tn(a, b):
    return lax.dot_general(a, b, (((0,), (0,)), ((), ())), preferred_element_type=F32)


def send(src, dst, send_sem, recv_sem, peer):
    return pltpu.make_async_remote_copy(
        src_ref=src,
        dst_ref=dst,
        send_sem=send_sem,
        recv_sem=recv_sem,
        device_id=peer,
        device_id_type=MESH,
    )


def rows_at(start, size):
    return pl.ds(pl.multiple_of(start, 16), size)


def greet_all(d, z, n, dp):
    barrier = pltpu.get_barrier_semaphore()
    for k in range(1, dp):
        pl.semaphore_signal(barrier, inc=1, device_id=(jnp.bitwise_xor(d, k), z), device_id_type=MESH)

    @pl.when(z > 0)
    def _():
        pl.semaphore_signal(barrier, inc=1, device_id=(d, z - 1), device_id_type=MESH)

    @pl.when(z < n - 1)
    def _():
        pl.semaphore_signal(barrier, inc=1, device_id=(d, z + 1), device_id_type=MESH)

    @pl.when((z > 0) & (z < n - 1))
    def _():
        pl.semaphore_wait(barrier, dp + 1)

    @pl.when((z == 0) | (z == n - 1))
    def _():
        pl.semaphore_wait(barrier, dp)


def normal(x):
    centered = x - jnp.mean(x, axis=-1, keepdims=True)
    r = lax.rsqrt(jnp.mean(centered * centered, axis=-1, keepdims=True) + epsilon)
    return centered * r, r


class Line:
    def __init__(self, d, z, n, own, got, dst, base, sems, k, fin):
        self.d, self.z, self.n = d, z, n
        self.own, self.got, self.dst, self.base = own, got, dst, base
        self.sems, self.k, self.fin = sems, k, fin
        self.half = own.shape[0] // 2
        self.chunks = self.half // CH
        self.slots = self.chunks + 2 * LAG * (n - 1)
        self.next = 0

    def place(self, f):
        z, n = self.z, self.n
        return (z, z + 1, z - 1) if f else (n - 1 - z, z - 1, z + 1)

    def fore(self, f, c, nxt):
        at = rows_at(f * self.half + c * CH, CH)
        s, r = self.sems[0], self.sems[1]
        return send(
            self.own.at[at], self.got.at[at], s.at[self.k, f, c], r.at[self.k, f, c], (self.d, nxt)
        )

    def back(self, f, c, prv):
        at = rows_at(self.base + f * self.half + c * CH, CH)
        s, r = self.sems[2], self.sems[3]
        return send(
            self.dst.at[at], self.dst.at[at], s.at[self.k, f, c], r.at[self.k, f, c], (self.d, prv)
        )

    def slot(self, s):
        n = self.n
        for f in range(2):
            p, nxt, prv = self.place(f)
            c = s - LAG * p
            valid = (c >= 0) & (c < self.chunks)

            @pl.when(valid & (p == 0))
            def _():
                self.fore(f, c, nxt).start()

            @pl.when(valid & (p > 0))
            def _():
                at = rows_at(f * self.half + c * CH, CH)
                self.fore(f, c, nxt).wait_recv()
                total = self.own[at].astype(F32) + self.got[at].astype(F32)

                @pl.when(p < n - 1)
                def _():
                    self.own[at] = total.astype(BF)
                    self.fore(f, c, nxt).start()

                @pl.when(p == n - 1)
                def _():
                    self.fin(f * self.half + c * CH, total)
                    self.back(f, c, prv).start()

            b = s - LAG * (2 * (n - 1) - p)

            @pl.when((b >= 0) & (b < self.chunks) & (p < n - 1))
            def _():
                self.back(f, b, prv).wait_recv()

                @pl.when(p > 0)
                def _():
                    self.back(f, b, prv).start()

    def step(self):
        self.slot(self.next)
        self.next += 1

    def left(self):
        return self.slots - self.next

    def drain(self):
        def body(c, carry):
            for f in range(2):
                p, nxt, prv = self.place(f)

                @pl.when(p < self.n - 1)
                def _():
                    self.fore(f, c, nxt).wait_send()

                @pl.when(p > 0)
                def _():
                    self.back(f, c, prv).wait_send()

            return carry

        lax.fori_loop(0, self.chunks, body, 0)


def run(count, *lines):
    lines = [line for line in lines if line.next < line.slots]
    first = [line.next for line in lines]

    def body(s, carry):
        for line, at in zip(lines, first):
            line.slot(at + s)
        return carry

    lax.fori_loop(0, count, body, 0)
    for line in lines:
        line.next += count


class Gather:
    def __init__(self, d, z, shard, full, send_sems, recv_sems, local_sems, a):
        self.d, self.z, self.shard, self.full, self.a = d, z, shard, full, a
        self.send_sems, self.recv_sems, self.local = send_sems, recv_sems, local_sems
        self.size = shard.shape[0]
        self.core, self.xn, self.yn = [(jnp.bitwise_xor(d, k), z) for k in (1, 2, 4)]
        self.bx, self.by, self.bd = [jnp.bitwise_xor(d, k) for k in (2, 4, 6)]
        half = self.size // 2
        self.top, self.bottom = (0, half), (half, half)
        self.started = []

    def part(self, block, rows):
        lo, size = rows
        return self.full.at[rows_at(block * self.size + lo, size or self.size)]

    def copy(self, k, block, rows, peer):
        part = self.part(block, rows)
        return send(part, part, self.send_sems.at[self.a, k], self.recv_sems.at[self.a, k], peer)

    def go(self, k, block, rows, peer):
        cp = self.copy(k, block, rows, peer)
        cp.start()
        self.started.append(cp)

    def got(self, k, block, rows, peer):
        self.copy(k, block, rows, peer).wait_recv()

    def begin(self):
        for k, peer in ((0, self.xn), (1, self.yn), (2, self.core)):
            cp = send(
                self.shard,
                self.part(self.d, WHOLE),
                self.send_sems.at[self.a, k],
                self.recv_sems.at[self.a, k],
                peer,
            )
            cp.start()
            self.started.append(cp)
        self.mine = pltpu.make_async_copy(self.shard, self.part(self.d, WHOLE), self.local.at[self.a])
        self.mine.start()

    def near(self):
        self.got(0, self.bx, WHOLE, self.xn)
        self.go(3, self.bx, self.top, self.yn)
        self.go(5, self.bx, WHOLE, self.core)
        self.got(1, self.by, WHOLE, self.yn)
        self.go(4, self.by, self.bottom, self.xn)
        self.go(6, self.by, WHOLE, self.core)

    def far(self):
        self.got(3, self.bd, self.top, self.yn)
        self.go(7, self.bd, self.top, self.core)
        self.got(4, self.bd, self.bottom, self.xn)
        self.go(8, self.bd, self.bottom, self.core)

    def last(self):
        o = [jnp.bitwise_xor(b, 1) for b in (self.d, self.bx, self.by, self.bd)]
        self.got(2, o[0], WHOLE, self.core)
        self.got(5, o[1], WHOLE, self.core)
        self.got(6, o[2], WHOLE, self.core)
        self.got(7, o[3], self.top, self.core)
        self.got(8, o[3], self.bottom, self.core)
        self.mine.wait()

    def drain(self):
        for cp in self.started:
            cp.wait_send()


class Moves:
    def __init__(self, sems):
        self.sems, self.used = sems, 0

    def start(self, src, dst):
        cp = pltpu.make_async_copy(src, dst, self.sems.at[self.used])
        self.used += 1
        cp.start()
        return cp


def turn(u, cosine, low, high):
    return u * cosine + pltpu.roll(u, 112, 1) * low + pltpu.roll(u, 16, 1) * high


def half_mask(rows, e):
    lane = lax.broadcasted_iota(jnp.int32, (rows, 128), 1)
    return (lane >= 64) == (e == 1)


def softmax(s):
    w = jnp.exp(s - jnp.max(s, axis=-1, keepdims=True))
    return w * (1.0 / jnp.sum(w, axis=-1, keepdims=True))


FWD_LINES = 4


def forward_kernel(
    n,
    dp,
    tokens,
    context,
    tables,
    key_bias,
    text_bias,
    vec,
    s_qkv,
    s_small,
    s_ckv,
    s_out,
    s_in,
    w_qkv,
    w_small,
    w_out,
    w_in,
    o_gv,
    o_h1,
    o_q,
    o_k,
    o_v,
    o_p,
    o_so,
    o_x1,
    o_h2,
    o_cq,
    o_tkv,
    o_pc,
    o_co,
    o_x2,
    o_h3,
    v_vec,
    gv,
    v_qkv,
    v_small,
    v_ckv,
    tok,
    ctx,
    tab,
    kb,
    tb,
    h1,
    q,
    k,
    v,
    probs,
    so,
    x1,
    h2,
    cq,
    tkv,
    pc,
    co,
    x2,
    h3,
    own,
    got,
    g_send,
    g_recv,
    g_local,
    v_send,
    v_recv,
    k_send,
    k_recv,
    fs,
    fr,
    bs,
    br,
    moves,
):
    d = lax.axis_index("dp")
    z = lax.axis_index("mp")
    rows = tokens.shape[0]
    group = rows // 2
    cols = so.shape[1]
    pairs = cols // 128
    half = lax.rem(d, 2)
    mv = Moves(moves)
    ld_tok = mv.start(tokens, tok)
    ld_small = [
        mv.start(a, b) for a, b in ((context, ctx), (tables, tab), (key_bias, kb), (text_bias, tb))
    ]
    ld_vec = mv.start(vec, v_vec.at[d])
    greet_all(d, z, n, dp)
    vec_copies = []
    for j in range(1, dp):
        peer = (jnp.bitwise_xor(d, j), z)
        cp = send(vec, v_vec.at[d], v_send.at[j], v_recv.at[j], peer)
        cp.start()
        vec_copies.append(cp)
    gathers = [
        Gather(d, z, shard, full, g_send, g_recv, g_local, a)
        for a, (shard, full) in enumerate(
            ((s_qkv, v_qkv), (s_ckv, v_ckv), (s_small, v_small), (s_out, w_out), (s_in, w_in))
        )
    ]
    g_qkv, g_ckv, g_small, g_out, g_in = gathers
    g_qkv.begin()
    ld_tok.wait()
    ld_vec.wait()
    for j in range(1, dp):
        b = jnp.bitwise_xor(d, j)
        send(v_vec.at[b], v_vec.at[b], v_send.at[j], v_recv.at[j], (b, z)).wait_recv()
    width = s_qkv.shape[0]
    for b in range(dp):
        gv[:, b * width : (b + 1) * width] = v_vec[b][:8, :width].astype(F32)

    def norm_rows(i, carry):
        at = rows_at(i * CH, CH)
        nrm, _ = normal(tok[at].astype(F32))
        h1[at] = (nrm * gv[0:1]).astype(BF)
        return carry

    lax.fori_loop(0, rows // CH // 2, norm_rows, 0)
    g_qkv.near()
    g_ckv.begin()
    g_small.begin()
    lax.fori_loop(rows // CH // 2, rows // CH, norm_rows, 0)
    st = [mv.start(h1, o_h1)]
    g_qkv.far()
    g_qkv.last()
    for ld in ld_small:
        ld.wait()
    my_rows = half * rows

    def project(g, carry):
        at = rows_at(g * group, group)
        mine = rows_at(my_rows + g * group, group)
        x = h1[at]
        for part in (1, 2, 0):
            u = dot_nn(x, v_qkv[:, part * cols : (part + 1) * cols])
            if part == 2:
                v[mine] = u.astype(BF)
                continue
            for j in range(pairs):
                r = turn(u[:, j * 128 : (j + 1) * 128], tab[0, at], tab[1, at], tab[2, at])
                if part:
                    k[mine, j * 128 : (j + 1) * 128] = r.astype(BF)
                else:
                    q[at, j * 128 : (j + 1) * 128] = (r * HD ** (-0.5)).astype(BF)
        return carry

    lax.fori_loop(0, 2, project, 0)
    core = (jnp.bitwise_xor(d, 1), z)
    mine, theirs = rows_at(my_rows, rows), rows_at((1 - half) * rows, rows)
    kv = [send(r.at[mine], r.at[mine], k_send.at[i], k_recv.at[i], core) for i, r in enumerate((k, v))]
    for cp in kv:
        cp.start()
    g_ckv.near()
    g_small.near()
    g_out.begin()
    g_ckv.far()
    g_ckv.last()
    g_small.far()
    g_in.begin()
    text = ctx.shape[0]
    t_mine, t_theirs = rows_at(half * text, text), rows_at((1 - half) * text, text)
    tkv[t_mine] = dot_nn(ctx[...], v_ckv[...]).astype(BF)
    kv.append(send(tkv.at[t_mine], tkv.at[t_mine], k_send.at[2], k_recv.at[2], core))
    kv[2].start()
    for i, (r, at) in enumerate(((k, theirs), (v, theirs))):
        send(r.at[at], r.at[at], k_send.at[i], k_recv.at[i], core).wait_recv()
    st += [mv.start(v_qkv, w_qkv), mv.start(q, o_q), mv.start(k, o_k), mv.start(v, o_v)]

    def attend(g, queries, keys, key_lo, values, value_lo, bias, save, out, between):
        at = rows_at(g * group, group)

        def head(h, carry):
            j, e = h // 2, lax.rem(h, 2)
            lo = pl.multiple_of(j * 128, 128)
            mask = half_mask(group, e)
            qb = jnp.where(mask, queries[at, pl.ds(lo, 128)], jnp.zeros((), BF))
            s = dot_nt(qb, keys[:, pl.ds(pl.multiple_of(key_lo + lo, 128), 128)]) + bias[0:1]
            p = softmax(s).astype(BF)
            save[h, at] = p
            o = dot_nn(p, values[:, pl.ds(pl.multiple_of(value_lo + lo, 128), 128)])
            out[at, pl.ds(lo, 128)] = jnp.where(mask, o.astype(BF), out[at, pl.ds(lo, 128)])
            between(h)
            return carry

        lax.fori_loop(0, 2 * pairs, head, 0)

    def quiet(h):
        pass

    def with_line(line, every):
        first = line.next

        def between(h):
            if every == 1:
                line.slot(first + h)
            else:

                @pl.when(lax.rem(h, every) == 0)
                def _():
                    line.slot(first + h // every)

        line.next += -(-2 * pairs // every)
        return between

    sems = (fs, fr, bs, br)

    def finish_one(g):
        def fin(lo, total):
            at = rows_at(g * group + lo, CH)
            mine = rows_at(g * group // 2 + lax.rem(lo, group // 2), CH)
            x = tok[at].astype(F32) + total
            x1[mine] = x
            h2[at] = (normal(x)[0] * gv[1:2]).astype(BF)

        return fin

    def finish_two(g):
        def fin(lo, total):
            at = rows_at(g * group + lo, CH)
            mine = rows_at(g * group // 2 + lax.rem(lo, group // 2), CH)
            x = x1[mine] + total
            x2[mine] = x
            h3[at] = (normal(x)[0] * gv[2:3]).astype(BF)

        return fin

    one = [
        Line(d, z, n, own.at[g], got.at[g], h2, g * group, sems, g, finish_one(g)) for g in range(2)
    ]
    two = [
        Line(d, z, n, own.at[2 + g], got.at[2 + g], h3, g * group, sems, 2 + g, finish_two(g))
        for g in range(2)
    ]

    def self_part(g):
        at = rows_at(g * group, group)
        own[g] = dot_nt(so[at], v_small[:, 0:cols]).astype(BF)

    def cross_project(g):
        at = rows_at(g * group, group)
        cq[at] = (dot_nn(h2[at], v_small[:, cols : 2 * cols]) ).astype(BF) * jnp.asarray(HD ** (-0.5), BF)

    def cross_part(g):
        at = rows_at(g * group, group)
        own[2 + g] = dot_nt(co[at], v_small[:, 2 * cols :]).astype(BF)

    attend(0, q, k, 0, v, 0, kb, probs, so, quiet)
    g_small.last()
    st.append(mv.start(v_small, w_small))
    self_part(0)
    st.append(mv.start(probs.at[:, rows_at(0, group)], o_p.at[:, rows_at(0, group)]))
    attend(1, q, k, 0, v, 0, kb, probs, so, with_line(one[0], 2))
    self_part(1)
    st.append(mv.start(probs.at[:, rows_at(group, group)], o_p.at[:, rows_at(group, group)]))
    st.append(mv.start(so, o_so))
    run(one[0].left(), one[0], one[1])
    send(tkv.at[t_theirs], tkv.at[t_theirs], k_send.at[2], k_recv.at[2], core).wait_recv()
    st.append(mv.start(tkv, o_tkv))
    cross_project(0)
    attend(0, cq, tkv, 0, tkv, cols, tb, pc, co, with_line(one[1], 6))
    cross_part(0)
    g_out.near()
    g_in.near()
    run(one[1].left(), one[1], two[0])
    cross_project(1)
    attend(1, cq, tkv, 0, tkv, cols, tb, pc, co, with_line(two[0], 3))
    cross_part(1)
    st += [mv.start(h2, o_h2), mv.start(x1, o_x1), mv.start(cq, o_cq), mv.start(pc, o_pc), mv.start(co, o_co)]
    run(4, two[0], two[1])
    g_out.far()
    g_in.far()
    run(two[0].left(), two[0], two[1])
    run(two[1].left(), two[1])
    st += [mv.start(h3, o_h3), mv.start(x2, o_x2), mv.start(gv, o_gv)]
    g_out.last()
    g_in.last()
    for g in gathers:
        g.drain()
    for cp in vec_copies + kv:
        cp.wait_send()
    for line in one + two:
        line.drain()
    for cp in st:
        cp.wait()


def run_forward(n, dp, tokens, context, tables, key_bias, text_bias, vec, s_qkv, s_small, s_ckv, s_out, s_in):
    rows, width = tokens.shape
    cols3 = s_qkv.shape[1]
    cols = cols3 // 3
    heads = cols // HD
    text = context.shape[0]
    half_rows = rows // 2
    sds = jax.ShapeDtypeStruct
    outs = [
        sds((width, cols3), BF),
        sds((width, cols3), BF),
        sds((width, s_out.shape[1]), BF),
        sds((width, s_in.shape[1]), BF),
        sds((8, width), F32),
        sds((rows, width), BF),
        sds((rows, cols), BF),
        sds((2 * rows, cols), BF),
        sds((2 * rows, cols), BF),
        sds((heads, rows, 2 * rows), BF),
        sds((rows, cols), BF),
        sds((half_rows, width), F32),
        sds((rows, width), BF),
        sds((rows, cols), BF),
        sds((2 * text, 2 * cols), BF),
        sds((heads, rows, 2 * text), BF),
        sds((rows, cols), BF),
        sds((half_rows, width), F32),
        sds((rows, width), BF),
    ]
    vm = pltpu.VMEM
    chunks = rows // 4 // CH
    saved = [vm(o.shape, o.dtype) for o in outs[5:]]
    scratch = [
        vm((dp,) + vec.shape, BF),
        vm((8, width), F32),
        vm((width, cols3), BF),
        vm((width, cols3), BF),
        vm((s_ckv.shape[0] * dp, s_ckv.shape[1]), BF),
        vm(tokens.shape, BF),
        vm(context.shape, BF),
        vm(tables.shape, F32),
        vm(key_bias.shape, F32),
        vm(text_bias.shape, F32),
        *saved,
        vm((4, half_rows, width), BF),
        vm((4, half_rows, width), BF),
        DMA((5, 9)),
        DMA((5, 9)),
        DMA((5,)),
        DMA((dp,)),
        DMA((dp,)),
        DMA((3,)),
        DMA((3,)),
        *[DMA((FWD_LINES, 2, chunks))] * 4,
        DMA((32,)),
    ]
    return pl.pallas_call(
        functools.partial(forward_kernel, n, dp),
        out_shape=outs,
        in_specs=[HBM] * 11,
        out_specs=[HBM] * len(outs),
        scratch_shapes=scratch,
        compiler_params=pltpu.CompilerParams(
            collective_id=0, has_side_effects=True, vmem_limit_bytes=58 * 2**20
        ),
        name="forward",
    )(tokens, context, tables, key_bias, text_bias, vec, s_qkv, s_small, s_ckv, s_out, s_in)


def backward_kernel(
    n,
    dp,
    tokens,
    context,
    cotangent,
    tables,
    w_qkv,
    w_small,
    w_out,
    w_in,
    i_gv,
    i_h1,
    i_q,
    i_k,
    i_v,
    i_p,
    i_so,
    i_x1,
    i_h2,
    i_cq,
    i_tkv,
    i_pc,
    i_co,
    i_x2,
    i_h3,
    o_mixed,
    o_gt,
    o_gg,
    o_out,
    o_in,
    o_small,
    o_ckv,
    o_qkv,
    gv,
    win,
    wout,
    wsmall,
    h2,
    h3,
    dy,
    hid,
    dgu,
    dx2r,
    dx1r,
    mixed,
    gt,
    x1,
    x2,
    dx,
    q,
    k,
    v,
    so,
    co,
    cq,
    dco,
    dcq,
    dso,
    dqkv,
    tkv,
    dtkv,
    pc,
    pst,
    dk,
    dv,
    ctx,
    tab,
    gg,
    own,
    got,
    kst,
    krv,
    tst,
    trv,
    gst,
    k_send,
    k_recv,
    fs,
    fr,
    bs,
    br,
    p_sem,
    g_sem,
    moves,
):
    d = lax.axis_index("dp")
    z = lax.axis_index("mp")
    rows, width = tokens.shape
    group = rows // 2
    cols = so.shape[1]
    units = hid.shape[1]
    pairs = cols // 128
    half = lax.rem(d, 2)
    core = (jnp.bitwise_xor(d, 1), z)
    mv = Moves(moves)
    first = [mv.start(a, b) for a, b in ((cotangent, dy), (i_gv, gv), (i_h3, h3))]
    pieces = 2
    piece = units // pieces
    w_loads = []
    for i in range(pieces):
        at = slice(i * piece, (i + 1) * piece)
        up = slice(units + i * piece, units + (i + 1) * piece)
        w_loads.append(
            [
                mv.start(w_in.at[:, at], win.at[:, at]),
                mv.start(w_in.at[:, up], win.at[:, up]),
                mv.start(w_out.at[:, at], wout.at[:, at]),
            ]
        )
    later = [
        mv.start(a, b)
        for a, b in (
            (i_x2, x2),
            (w_small, wsmall),
            (i_x1, x1),
            (i_h2, h2),
            (i_co, co),
            (i_cq, cq),
            (i_tkv, tkv),
            (i_pc, pc),
            (i_q, q),
            (i_k, k),
            (i_v, v),
            (i_so, so),
            (context, ctx),
            (tables, tab),
        )
    ]
    greet_all(d, z, n, dp)
    gg[...] = jnp.zeros_like(gg)
    dtkv[...] = jnp.zeros_like(dtkv)

    def clear(i, carry):
        at = rows_at(i * CH, CH)
        dk[at] = jnp.zeros((CH, cols), F32)
        dv[at] = jnp.zeros((CH, cols), F32)
        return carry

    lax.fori_loop(0, 2 * rows // CH, clear, 0)
    for cp in first:
        cp.wait()

    def bias_sum(i, carry):
        gg[5:6] += jnp.sum(dy[rows_at(i * CH, CH)].astype(F32), axis=0, keepdims=True)
        return carry

    lax.fori_loop(0, rows // CH, bias_sum, 0)
    tile = 256

    def feed(g, lo, count, between):
        at = rows_at(g * group, group)

        def step(i, carry):
            u = pl.multiple_of(i * tile, tile)
            us, ups = pl.ds(u, tile), pl.ds(pl.multiple_of(units + u, tile), tile)
            x = h3[at]
            gate = dot_nn(x, win[:, us]) + gv[3:4, us]
            up = dot_nn(x, win[:, ups]) + gv[4:5, us]
            dh = dot_nn(dy[at], wout[:, us])
            sig = jax.nn.sigmoid(gate)
            act = gate * sig
            hid[at, us] = (act * up).astype(BF)
            d_gate = (dh * up * (sig * (1.0 + gate * (1.0 - sig)))).astype(BF)
            d_up = (dh * act).astype(BF)
            dgu[at, us] = d_gate
            dgu[at, ups] = d_up
            gg[3:4, us] += jnp.sum(d_gate.astype(F32), axis=0, keepdims=True)
            gg[4:5, us] += jnp.sum(d_up.astype(F32), axis=0, keepdims=True)
            between(i)
            return carry

        lax.fori_loop(lo, lo + count, step, 0)

    def norm_back(x, dn, gain, row):
        nrm, r = normal(x)
        gg[row : row + 1] += jnp.sum(dn * nrm, axis=0, keepdims=True)
        e = dn * gain
        return r * (
            e
            - jnp.mean(e, axis=-1, keepdims=True)
            - nrm * jnp.mean(e * nrm, axis=-1, keepdims=True)
        )

    def places(g, lo):
        return rows_at(g * group + lo, CH), rows_at(
            g * group // 2 + lax.rem(lo, group // 2), CH
        )

    def finish_mixed(g):
        def fin(lo, total):
            at, mine = places(g, lo)
            mixed[at] = (x2[mine] + total + gv[5:6]).astype(BF)

        return fin

    def finish_three(g):
        def fin(lo, total):
            at, mine = places(g, lo)
            x = dy[at].astype(F32) + norm_back(x2[mine], total, gv[2:3], 2)
            dx[mine] = x
            dx2r[at] = x.astype(BF)

        return fin

    def finish_two(g):
        def fin(lo, total):
            at, mine = places(g, lo)
            x = dx[mine] + norm_back(x1[mine], total, gv[1:2], 1)
            dx[mine] = x
            dx1r[at] = x.astype(BF)

        return fin

    def finish_one(g):
        def fin(lo, total):
            at, mine = places(g, lo)
            x = dx[mine] + norm_back(h3[at].astype(F32), total, gv[0:1], 0)
            gt[at] = x.astype(BF)

        return fin

    sems = (fs, fr, bs, br)

    def lines(dst, slot, index, fin):
        return [
            Line(
                d, z, n, own.at[slot + g], got.at[slot + g], dst, g * group, sems, index + g, fin(g)
            )
            for g in range(2)
        ]

    mix = lines(mixed, 2, 0, finish_mixed)
    three = lines(dx2r, 0, 2, finish_three)
    two = lines(dx1r, 0, 4, finish_two)
    one = lines(gt, 0, 6, finish_one)

    def quiet(i):
        pass

    def with_lines(total, every, *ls):
        ls = [line for line in ls if line.next < line.slots]
        starts = [line.next for line in ls]

        def between(i):
            def go():
                for line, s in zip(ls, starts):
                    line.slot(s + i // every)

            if every == 1:
                go()
            else:
                pl.when(lax.rem(i, every) == 0)(go)

        for line in ls:
            line.next += -(-total // every)
        return between

    tiles = units // tile
    per = tiles // pieces

    def grads(left, right, lo, size, out, out_lo, between):
        step_rows = 384
        steps = left.shape[1] // step_rows

        def out_copy(t, slot):
            return pltpu.make_async_copy(
                gst.at[slot, :, pl.ds(0, size)],
                out.at[pl.ds(pl.multiple_of(t * step_rows, 16), step_rows), pl.ds(out_lo, size)],
                g_sem.at[slot],
            )

        def step(t, carry):
            slot = lax.rem(t, 2)

            @pl.when(t >= 2)
            def _():
                out_copy(t - 2, slot).wait()

            part = dot_tn(
                left[:, pl.ds(pl.multiple_of(t * step_rows, 128), step_rows)],
                right[:, lo : lo + size],
            )
            gst[slot, :, 0:size] = part.astype(BF)
            out_copy(t, slot).start()
            between(t)
            return carry

        lax.fori_loop(0, steps, step, 0)
        for t in range(max(0, steps - 2), steps):
            out_copy(t, t % 2).wait()

    def attend_back(g, d_out, queries, keys, key_lo, values, value_lo, probs, dkr, dk_lo, dvr, dv_lo, dq, between):
        at = rows_at(g * group, group)

        def head(h, carry):
            j, e = h // 2, lax.rem(h, 2)
            lo = pl.multiple_of(j * 128, 128)
            here = pl.ds(lo, 128)
            mask = half_mask(group, e)
            zero = jnp.zeros((), BF)
            do = jnp.where(mask, d_out[at, here], zero)
            qb = jnp.where(mask, queries[at, here], zero)
            p = probs(h)
            pf = p.astype(F32)
            dp_ = dot_nt(do, values[:, pl.ds(pl.multiple_of(value_lo + lo, 128), 128)])
            ds = (pf * (dp_ - jnp.sum(pf * dp_, axis=-1, keepdims=True))).astype(BF)
            g_q = dot_nn(ds, keys[:, pl.ds(pl.multiple_of(key_lo + lo, 128), 128)]) * HD ** (-0.5)
            dkr[:, pl.ds(pl.multiple_of(dk_lo + lo, 128), 128)] += dot_tn(ds, qb)
            dvr[:, pl.ds(pl.multiple_of(dv_lo + lo, 128), 128)] += dot_tn(p, do)
            dq(h, at, here, mask, g_q)
            between(h)
            return carry

        lax.fori_loop(0, 2 * pairs, head, 0)

    def cross_back(g, between):
        at = rows_at(g * group, group)
        dco[at] = dot_nn(dx2r[at], wsmall[:, 2 * cols :]).astype(BF)

        def dq(h, at, here, mask, g_q):
            dcq[at, here] = jnp.where(mask, g_q.astype(BF), dcq[at, here])

        attend_back(
            g, dco, cq, tkv, 0, tkv, cols, lambda h: pc[h, at], dtkv, 0, dtkv, cols, dq, between
        )

    def self_back(g, between):
        at = rows_at(g * group, group)

        def load(h):
            slot = lax.rem(h, 2)
            return pltpu.make_async_copy(i_p.at[h, at], pst.at[slot], p_sem.at[slot])

        load(0).start()
        dso[at] = dot_nn(dx1r[at], wsmall[:, 0:cols]).astype(BF)

        def probs(h):
            @pl.when(h + 1 < 2 * pairs)
            def _():
                load(h + 1).start()

            load(h).wait()
            return pst[lax.rem(h, 2)]

        def dq(h, at, here, mask, g_q):
            r = turn(g_q, tab[0, at], -tab[1, at], -tab[2, at]).astype(BF)
            dqkv[at, here] = jnp.where(mask, r, dqkv[at, here])

        attend_back(g, dso, q, k, 0, v, 0, probs, dk, 0, dv, 0, dq, between)

    def three_part(g):
        at = rows_at(g * group, group)
        own[g] = dot_nt(dgu[at], win[...]).astype(BF)

    def down_part(g):
        at = rows_at(g * group, group)
        own[2 + g] = dot_nt(hid[at], wout[...]).astype(BF)

    def two_part(g):
        at = rows_at(g * group, group)
        own[g] = dot_nt(dcq[at], wsmall[:, cols : 2 * cols]).astype(BF)

    def one_part(g):
        at = rows_at(g * group, group)
        own[g] = dot_nt(dqkv[at], win[:, 0 : 3 * cols]).astype(BF)

    for i in range(pieces):
        for cp in w_loads[i]:
            cp.wait()
        feed(0, i * per, per, quiet)
    three_part(0)
    for cp in later:
        cp.wait()
    feed(1, 0, tiles, with_lines(tiles, 1, three[0]))
    three_part(1)
    down_part(0)
    run(1, three[0], three[1])
    down_part(1)
    ld_qkv = mv.start(w_qkv, win.at[:, pl.ds(0, 3 * cols)])
    run(1, three[0], three[1])
    grads(dy, hid, 0, units, o_out, 0, with_lines(4, 1, three[0], three[1]))
    grads(h3, dgu, 0, units, o_in, 0, with_lines(4, 1, three[0], three[1]))
    run(three[0].left(), three[0], three[1])
    ld_h1 = mv.start(i_h1, hid)
    cross_back(0, with_lines(6, 3, three[1]))
    three[0].drain()
    two_part(0)
    run(three[1].left(), three[1], two[0])
    cross_back(1, with_lines(6, 3, two[0]))
    three[1].drain()
    two_part(1)
    text = ctx.shape[0]
    t_mine, t_theirs = rows_at(half * text, text), rows_at((1 - half) * text, text)
    tst[...] = dtkv[t_theirs].astype(BF)
    t_copy = send(tst, trv, k_send.at[2], k_recv.at[2], core)
    t_copy.start()
    grads(h3, dgu, units, units, o_in, units, with_lines(4, 1, two[0], two[1]))
    ld_tok = mv.start(tokens, h3)
    grads(dx2r, co, 0, cols, o_small, 2 * cols, with_lines(4, 2, two[0], two[1]))
    grads(h2, dcq, 0, cols, o_small, cols, with_lines(4, 2, two[0], two[1]))
    run(two[0].left(), two[0], two[1])
    self_back(0, with_lines(6, 1, two[1]))
    two[0].drain()
    run(two[1].left(), two[1])
    self_back(1, with_lines(6, 1, mix[0], mix[1]))
    two[1].drain()
    mine, theirs = rows_at(half * rows, rows), rows_at((1 - half) * rows, rows)
    kst[0] = dk[theirs].astype(BF)
    k_copy = send(kst.at[0], krv.at[0], k_send.at[0], k_recv.at[0], core)
    k_copy.start()
    kst[1] = dv[theirs].astype(BF)
    v_copy = send(kst.at[1], krv.at[1], k_send.at[1], k_recv.at[1], core)
    v_copy.start()
    ld_h1.wait()
    ld_qkv.wait()
    ld_tok.wait()
    k_copy.wait_recv()
    for g in range(2):
        at = slice(g * group, (g + 1) * group)
        own_at = rows_at(half * rows + g * group, group)
        for j in range(pairs):
            here = slice(j * 128, (j + 1) * 128)
            u = dk[own_at, here] + krv[0, at, here].astype(F32)
            dqkv[at, cols + j * 128 : cols + (j + 1) * 128] = turn(
                u, tab[0, at], -tab[1, at], -tab[2, at]
            ).astype(BF)
        if g == 0:
            v_copy.wait_recv()
        dqkv[at, 2 * cols :] = (dv[own_at] + krv[1, at].astype(F32)).astype(BF)
        one_part(g)
        if g == 0:
            run(2, one[0], mix[0], mix[1])
    grads(dx1r, so, 0, cols, o_small, 0, with_lines(4, 1, one[0], one[1], mix[0], mix[1]))
    grads(hid, dqkv, 0, 3 * cols, o_qkv, 0, with_lines(4, 1, one[0], one[1], mix[0], mix[1]))
    t_copy.wait()
    tst[...] = (dtkv[t_mine] + trv[...].astype(F32)).astype(BF)
    grads(ctx, tst, 0, 2 * cols, o_ckv, 0, with_lines(2, 1, one[0], one[1], mix[0], mix[1]))
    run(one[1].left() - 2, one[0], one[1], mix[0], mix[1])
    st = [mv.start(gg, o_gg), mv.start(mixed, o_mixed)]
    run(one[1].left(), one[1])
    st.append(mv.start(gt, o_gt))
    k_copy.wait_send()
    v_copy.wait_send()
    for line in mix + one:
        line.drain()
    for cp in st:
        cp.wait()


def run_backward(n, dp, tokens, context, cotangent, tables, saved):
    rows, width = tokens.shape
    w_qkv, w_in = saved[0], saved[3]
    cols = w_qkv.shape[1] // 3
    units = w_in.shape[1] // 2
    heads = cols // HD
    text, text_width = context.shape
    half_rows = rows // 2
    sds = jax.ShapeDtypeStruct
    outs = [
        sds((rows, width), BF),
        sds((rows, width), BF),
        sds((8, width), F32),
        sds((width, units), BF),
        sds((width, 2 * units), BF),
        sds((width, 3 * cols), BF),
        sds((text_width, 2 * cols), BF),
        sds((width, 3 * cols), BF),
    ]
    vm = pltpu.VMEM
    chunks = rows // 4 // CH
    full, head, own_x = vm((rows, width), BF), vm((rows, cols), BF), vm((half_rows, width), F32)
    keys = vm((2 * rows, cols), BF)
    scratch = [
        vm((8, width), F32),
        vm((width, 2 * units), BF),
        vm((width, units), BF),
        vm((width, 3 * cols), BF),
        full,
        full,
        full,
        vm((rows, units), BF),
        vm((rows, 2 * units), BF),
        full,
        full,
        full,
        full,
        own_x,
        own_x,
        own_x,
        head,
        keys,
        keys,
        head,
        head,
        head,
        head,
        head,
        head,
        vm((rows, 3 * cols), BF),
        vm((2 * text, 2 * cols), BF),
        vm((2 * text, 2 * cols), F32),
        vm((heads, rows, 2 * text), BF),
        vm((2, half_rows, 2 * rows), BF),
        vm((2 * rows, cols), F32),
        vm((2 * rows, cols), F32),
        vm(context.shape, BF),
        vm(tables.shape, F32),
        vm((8, width), F32),
        vm((4, half_rows, width), BF),
        vm((4, half_rows, width), BF),
        vm((2, rows, cols), BF),
        vm((2, rows, cols), BF),
        vm((text, 2 * cols), BF),
        vm((text, 2 * cols), BF),
        vm((2, 384, units), BF),
        DMA((3,)),
        DMA((3,)),
        *[DMA((8, 2, chunks))] * 4,
        DMA((2,)),
        DMA((2,)),
        DMA((40,)),
    ]
    ins = (tokens, context, cotangent, tables, *saved)
    return pl.pallas_call(
        functools.partial(backward_kernel, n, dp),
        out_shape=outs,
        in_specs=[HBM] * len(ins),
        out_specs=[HBM] * len(outs),
        scratch_shapes=scratch,
        compiler_params=pltpu.CompilerParams(
            collective_id=1, has_side_effects=True, vmem_limit_bytes=63 * 2**20
        ),
        name="backward",
    )(*ins)


def scatter_kernel(count, *refs):
    ins, outs = refs[:count], refs[count : 2 * count]
    rest = refs[2 * count :]
    own, got, one, two, out_v = [rest[i * count : (i + 1) * count] for i in range(5)]
    send_sems, recv_sems, local_sems = rest[5 * count :]
    d = lax.axis_index("dp")
    m = lax.axis_index("mp")
    core, xn, yn = [(jnp.bitwise_xor(d, k), m) for k in (1, 2, 4)]
    c = lax.rem(d, 2)
    x = lax.rem(d // 2, 2)
    y = d // 4
    barrier = pltpu.get_barrier_semaphore()
    for peer in (core, xn, yn):
        pl.semaphore_signal(barrier, inc=1, device_id=peer, device_id_type=MESH)
    pl.semaphore_wait(barrier, 3)
    copies = [{} for _ in range(count)]
    loads, stores = [], []

    def go(a, k, src, dst, peer):
        cp = send(src, dst, send_sems.at[a, k], recv_sems.at[a, k], peer)
        cp.start()
        copies[a][k] = cp

    for a in range(count):
        go(a, 0, ins[a].at[:, 1 - c], got[a], core)
        cp = pltpu.make_async_copy(ins[a].at[:, c], own[a], local_sems.at[a])
        cp.start()
        loads.append(cp)

    def add_core(a):
        loads[a].wait()
        copies[a][0].wait_recv()
        rows = own[a].shape[1]

        def tile(i, carry):
            j, t = i // (rows // 16), lax.rem(i, rows // 16)
            at = pl.ds(pl.multiple_of(t * 16, 16), 16)
            own[a][j, at] = (own[a][j, at].astype(jnp.float32) + got[a][j, at].astype(jnp.float32)).astype(
                jnp.bfloat16
            )
            return carry

        lax.fori_loop(0, 4 * (rows // 16), tile, 0)
        half = rows // 2
        top, bottom = pl.ds(0, half), pl.ds(half, half)
        for b in range(2):
            go(a, 1 + b, own[a].at[2 * b + 1 - x, top], one[a].at[0, b], xn)
            go(a, 3 + b, own[a].at[2 * (1 - y) + b, bottom], one[a].at[1, b], yn)

    def plus(a, at_block, lo, part):
        half = own[a].shape[1] // 2

        def tile(t, carry):
            at = pl.ds(pl.multiple_of(lo + t * 16, 16), 16)
            frm = pl.ds(pl.multiple_of(t * 16, 16), 16)
            own[a][at_block, at] = (
                own[a][at_block, at].astype(jnp.float32) + part[frm].astype(jnp.float32)
            ).astype(jnp.bfloat16)
            return carry

        lax.fori_loop(0, half // 16, tile, 0)

    def add_one(a):
        half = own[a].shape[1] // 2
        top, bottom = pl.ds(0, half), pl.ds(half, half)
        for b in range(2):
            copies[a][1 + b].wait_recv()
            plus(a, 2 * b + x, 0, one[a].at[0, b])
            copies[a][3 + b].wait_recv()
            plus(a, 2 * y + b, half, one[a].at[1, b])
        go(a, 5, own[a].at[2 * (1 - y) + x, top], two[a].at[0], yn)
        go(a, 6, own[a].at[2 * y + 1 - x, bottom], two[a].at[1], xn)

    def add_two(a):
        half = own[a].shape[1] // 2
        for part in range(2):
            copies[a][5 + part].wait_recv()

            def tile(t, carry, part=part):
                at = pl.ds(pl.multiple_of(part * half + t * 16, 16), 16)
                frm = pl.ds(pl.multiple_of(t * 16, 16), 16)
                out_v[a][at] = own[a][2 * y + x, at].astype(jnp.float32) + two[a][part, frm].astype(jnp.float32)
                return carry

            lax.fori_loop(0, half // 16, tile, 0)
        cp = pltpu.make_async_copy(out_v[a], outs[a], local_sems.at[a])
        cp.start()
        stores.append(cp)

    for s in range(count + 2):
        if s < count:
            add_core(s)
        if 0 <= s - 1 < count:
            add_one(s - 1)
        if 0 <= s - 2 < count:
            add_two(s - 2)
    for a in range(count):
        for cp in copies[a].values():
            cp.wait_send()
    for cp in stores:
        cp.wait()


def scatter_all(arrays, collective_id):
    count = len(arrays)
    views = [a.reshape(4, 2, a.shape[0] // 8, a.shape[1]) for a in arrays]
    sizes = [v.shape[2:] for v in views]
    bf = jnp.bfloat16
    return pl.pallas_call(
        functools.partial(scatter_kernel, count),
        out_shape=[jax.ShapeDtypeStruct(s, jnp.float32) for s in sizes],
        in_specs=[HBM] * count,
        out_specs=[HBM] * count,
        scratch_shapes=[pltpu.VMEM((4,) + s, bf) for s in sizes]
        + [pltpu.VMEM((4,) + s, bf) for s in sizes]
        + [pltpu.VMEM((2, 2, s[0] // 2, s[1]), bf) for s in sizes]
        + [pltpu.VMEM((2, s[0] // 2, s[1]), bf) for s in sizes]
        + [pltpu.VMEM(s, jnp.float32) for s in sizes]
        + [
            pltpu.SemaphoreType.DMA((count, 7)),
            pltpu.SemaphoreType.DMA((count, 7)),
            pltpu.SemaphoreType.DMA((count,)),
        ],
        compiler_params=pltpu.CompilerParams(
            collective_id=collective_id, has_side_effects=True, vmem_limit_bytes=60 * 2**20
        ),
        name="scatter_all",
    )(*views)


def prepare(tokens, context, frame_counts, text_counts, w_qkv, w_attn_out, w_cross_q, w_cross_kv, w_cross_out, w_in, w_out, norm_gains, b_in, b_out):
    shard, _, cols = w_qkv.shape
    rows = tokens.shape[0]
    text = context.shape[0]
    vec = jnp.concatenate([norm_gains, b_in, b_out[None]], axis=0)
    vec = jnp.pad(vec, ((0, 16 - vec.shape[0]), (0, 256 - shard)))
    d = lax.axis_index("dp")
    clip, half = d // 2, d % 2
    frames = lax.dynamic_index_in_dim(frame_counts, clip, 0, keepdims=False)
    texts = lax.dynamic_index_in_dim(text_counts, clip, 0, keepdims=False)
    key_bias = jnp.where(jnp.arange(2 * rows) <= frames, 0.0, -1e30).astype(F32)[None]
    text_bias = jnp.where(jnp.arange(2 * text) < texts, 0.0, -1e30).astype(F32)[None]
    m = HD // 4
    lane = jnp.arange(128) % HD
    frequency = 10000.0 ** (-(lane % m).astype(F32) / m)
    angle = (half * rows + jnp.arange(rows)).astype(F32)[:, None] * frequency[None]
    sine = jnp.sin(angle)
    tables = jnp.stack(
        [
            jnp.where(lane < 2 * m, jnp.cos(angle), 1.0),
            jnp.where(lane < m, -sine, 0.0),
            jnp.where((lane >= m) & (lane < 2 * m), sine, 0.0),
        ]
    )
    return (
        tables,
        jnp.broadcast_to(key_bias, (8, 2 * rows)),
        jnp.broadcast_to(text_bias, (8, 2 * text)),
        vec,
        w_qkv.reshape(shard, 3 * cols),
        jnp.concatenate([w_attn_out.T, w_cross_q, w_cross_out.T], axis=1),
        w_cross_kv.reshape(w_cross_kv.shape[0], 2 * cols),
        w_out.T,
        w_in.reshape(shard, -1),
    )


def from_partner(block, axis, stride):
    count = lax.axis_size(axis)
    route = []
    for low in range(count):
        high = low | 1 << stride
        if high != low and high < count:
            route += [(low, high), (high, low)]
    return lax.ppermute(block, axis, route)


def layer_norm(values, gain_row):
    centered = values - jnp.mean(values, axis=-1, keepdims=True)
    spread = jnp.mean(centered * centered, axis=-1, keepdims=True)
    return centered * lax.rsqrt(spread + epsilon) * gain_row


def rotate(tensor, positions):
    quarter = tensor.shape[-1] // 4
    frequency = 10000.0 ** (-jnp.arange(quarter, dtype=jnp.float32) / quarter)
    angles = positions[:, None] * frequency[None, :]
    cosine = jnp.cos(angles)[:, None, :]
    sine_part = jnp.sin(angles)[:, None, :]
    first_part = tensor[..., :quarter]
    second = tensor[..., quarter : 2 * quarter]
    return jnp.concatenate(
        [
            first_part * cosine - second * sine_part,
            second * cosine + first_part * sine_part,
            tensor[..., 2 * quarter :],
        ],
        axis=-1,
    )


def gated_unit(both):
    gate = both[:, 0]
    return gate * jax.nn.sigmoid(gate) * both[:, 1]


def in_order(own_part, other_part, which_half):
    lower_first = jnp.concatenate([own_part, other_part], axis=0)
    upper_first = jnp.concatenate([other_part, own_part], axis=0)
    return jnp.where(which_half == 0, lower_first, upper_first)


def own_rows(whole, which_half, row_count):
    return lax.dynamic_slice_in_dim(whole, which_half * row_count, row_count, 0)


def partner_rows(whole, which_half, row_count):
    return lax.dynamic_slice_in_dim(whole, (1 - which_half) * row_count, row_count, 0)


def masked_scores(query_block, key_all, key_live):
    scale = query_block.shape[-1] ** (-0.5)
    raw_scores = (
        jnp.einsum("qhd,khd->hqk", query_block, key_all, preferred_element_type=jnp.float32) * scale
    )
    return jnp.where(key_live[None, None, :], raw_scores, -1e30)


def attend_forward(queries, key_all, value_all, key_live):
    row_count, head_count, head_size = queries.shape
    block_rows = min(512, row_count)
    blocks = queries.reshape(row_count // block_rows, block_rows, head_count, head_size)

    def per_block(query_block):
        scores = masked_scores(query_block, key_all, key_live)
        row_max = jnp.max(scores, axis=-1, keepdims=True)
        weights = jnp.exp(scores - row_max)
        row_total = jnp.sum(weights, axis=-1, keepdims=True)
        attn_probs = weights / row_total
        block_out = jnp.einsum(
            "hqk,khd->qhd",
            attn_probs.astype(jnp.bfloat16),
            value_all,
            preferred_element_type=jnp.float32,
        )
        return (block_out, row_max + jnp.log(row_total))

    outputs, log_sums = lax.map(per_block, blocks)
    return (outputs.reshape(row_count, head_count, head_size), log_sums)


def attend_backward(queries, key_all, value_all, key_live, log_sums, grad_out):
    row_count, head_count, head_size = queries.shape
    block_rows = min(512, row_count)
    block_shape = (row_count // block_rows, block_rows, head_count, head_size)
    scale = head_size ** (-0.5)

    def per_block(running, block_item):
        query_block, grad_block, lse_block = block_item
        attn_probs = jnp.exp(masked_scores(query_block, key_all, key_live) - lse_block)
        grad_probs = jnp.einsum(
            "qhd,khd->hqk", grad_block, value_all, preferred_element_type=jnp.float32
        )
        row_inner = jnp.sum(attn_probs * grad_probs, axis=-1, keepdims=True)
        grad_scores = (attn_probs * (grad_probs - row_inner)).astype(jnp.bfloat16)
        grad_query = (
            jnp.einsum("hqk,khd->qhd", grad_scores, key_all, preferred_element_type=jnp.float32)
            * scale
        )
        grad_key = (
            running[0]
            + jnp.einsum(
                "hqk,qhd->khd", grad_scores, query_block, preferred_element_type=jnp.float32
            )
            * scale
        )
        grad_value = running[1] + jnp.einsum(
            "hqk,qhd->khd",
            attn_probs.astype(jnp.bfloat16),
            grad_block,
            preferred_element_type=jnp.float32,
        )
        return ((grad_key, grad_value), grad_query)

    zero_keys = jnp.zeros(key_all.shape, jnp.float32)
    (grad_key, grad_value), grad_query = lax.scan(
        per_block,
        (zero_keys, zero_keys),
        (queries.reshape(block_shape), grad_out.reshape(block_shape), log_sums),
    )
    return (grad_query.reshape(row_count, head_count, head_size), grad_key, grad_value)


def branch_total(partial_sum):
    return lax.psum(partial_sum, "mp")


def grad_total(partial_sum):
    return lax.psum(partial_sum, "mp")


def body(
    tokens,
    context,
    frame_counts,
    text_counts,
    w_qkv,
    w_attn_out,
    w_cross_q,
    w_cross_kv,
    w_cross_out,
    w_in,
    w_out,
    norm_gains,
    b_in,
    b_out,
    cotangent,
):
    gathered = (
        lax.all_gather(w_qkv, "dp", axis=0, tiled=True),
        lax.all_gather(w_attn_out, "dp", axis=1, tiled=True),
        lax.all_gather(w_cross_q, "dp", axis=0, tiled=True),
        lax.all_gather(w_cross_kv, "dp", axis=0, tiled=True),
        lax.all_gather(w_cross_out, "dp", axis=1, tiled=True),
        lax.all_gather(w_in, "dp", axis=0, tiled=True),
        lax.all_gather(w_out, "dp", axis=1, tiled=True),
        lax.all_gather(norm_gains, "dp", axis=1, tiled=True),
        lax.all_gather(b_in, "dp", axis=1, tiled=True),
        lax.all_gather(b_out, "dp", axis=0, tiled=True),
    )
    (
        qkv_full,
        attn_out_full,
        cross_q_full,
        cross_kv_full,
        cross_out_full,
        in_full,
        out_full,
        gains_full,
        b_in_full,
        b_out_full,
    ) = gathered
    row_count, model_width = tokens.shape
    text_rows, text_width = context.shape
    head_cols = qkv_full.shape[2]
    unit_cols = in_full.shape[2]
    head_count = head_cols // HD
    device_row = lax.axis_index("dp")
    which_half = device_row % 2
    clip_index = device_row // 2
    frame_live = lax.dynamic_index_in_dim(frame_counts, clip_index, 0, keepdims=False)
    text_live = lax.dynamic_index_in_dim(text_counts, clip_index, 0, keepdims=False)
    positions = (which_half * row_count + jnp.arange(row_count)).astype(jnp.float32)
    key_live = jnp.arange(2 * row_count) <= frame_live
    token_live = jnp.arange(2 * text_rows) < text_live
    gain_rows = gains_full.astype(jnp.float32)
    tokens_f = tokens.astype(jnp.float32)
    grad_y_mine = cotangent.astype(jnp.float32)
    norm_one, pull_one = jax.vjp(layer_norm, tokens_f, gain_rows[0])
    h_one = norm_one.astype(jnp.bfloat16)
    qkv = jnp.dot(
        h_one, qkv_full.reshape(model_width, 3 * head_cols), preferred_element_type=jnp.float32
    ).reshape(row_count, 3, head_count, HD)
    queries = rotate(qkv[:, 0], positions).astype(jnp.bfloat16)
    own_keys = rotate(qkv[:, 1], positions).astype(jnp.bfloat16).reshape(row_count, head_cols)
    own_values = qkv[:, 2].astype(jnp.bfloat16).reshape(row_count, head_cols)
    own_text = jnp.dot(
        context,
        cross_kv_full.reshape(text_width, 2 * head_cols),
        preferred_element_type=jnp.float32,
    ).astype(jnp.bfloat16)
    other = from_partner((own_keys, own_values, own_text), "dp", 0)
    key_all = in_order(own_keys, other[0], which_half).reshape(2 * row_count, head_count, HD)
    value_all = in_order(own_values, other[1], which_half).reshape(2 * row_count, head_count, HD)
    text_all = in_order(own_text, other[2], which_half).reshape(2 * text_rows, 2, head_count, HD)
    text_keys = text_all[:, 0]
    text_values = text_all[:, 1]
    self_attn, self_lse = attend_forward(queries, key_all, value_all, key_live)
    self_out = self_attn.reshape(row_count, head_cols).astype(jnp.bfloat16)
    self_part = jnp.dot(self_out, attn_out_full, preferred_element_type=jnp.float32)
    x_one = tokens_f + branch_total(self_part)
    norm_two, pull_two = jax.vjp(layer_norm, x_one, gain_rows[1])
    h_two = norm_two.astype(jnp.bfloat16)
    cross_queries = (
        jnp.dot(h_two, cross_q_full, preferred_element_type=jnp.float32)
        .astype(jnp.bfloat16)
        .reshape(row_count, head_count, HD)
    )
    cross_attn, cross_lse = attend_forward(cross_queries, text_keys, text_values, token_live)
    cross_out = cross_attn.reshape(row_count, head_cols).astype(jnp.bfloat16)
    cross_part = jnp.dot(cross_out, cross_out_full, preferred_element_type=jnp.float32)
    x_two = x_one + branch_total(cross_part)
    norm_three, pull_three = jax.vjp(layer_norm, x_two, gain_rows[2])
    h_three = norm_three.astype(jnp.bfloat16)
    both = jnp.dot(
        h_three, in_full.reshape(model_width, 2 * unit_cols), preferred_element_type=jnp.float32
    ).reshape(row_count, 2, unit_cols) + b_in_full.astype(jnp.float32)
    hidden_f, pull_unit = jax.vjp(gated_unit, both)
    hidden = hidden_f.astype(jnp.bfloat16)
    down_part = jnp.dot(hidden, out_full, preferred_element_type=jnp.float32)
    mixed = (x_two + branch_total(down_part) + b_out_full.astype(jnp.float32)).astype(jnp.bfloat16)
    again = (
        lax.all_gather(w_qkv, "dp", axis=0, tiled=True),
        lax.all_gather(w_attn_out, "dp", axis=1, tiled=True),
        lax.all_gather(w_cross_q, "dp", axis=0, tiled=True),
        lax.all_gather(w_cross_out, "dp", axis=1, tiled=True),
        lax.all_gather(w_in, "dp", axis=0, tiled=True),
        lax.all_gather(w_out, "dp", axis=1, tiled=True),
    )
    qkv_back = again[0]
    attn_out_back = again[1]
    cross_q_back = again[2]
    cross_out_back = again[3]
    in_back = again[4]
    out_back = again[5]
    grad_y = cotangent.astype(jnp.float32)
    grad_out_w = jnp.dot(hidden.T, cotangent, preferred_element_type=jnp.float32)
    grad_b_out = jnp.sum(grad_y, axis=0)
    grad_hidden = jnp.dot(cotangent, out_back.T, preferred_element_type=jnp.float32)
    grad_both = pull_unit(grad_hidden)[0].astype(jnp.bfloat16).reshape(row_count, 2 * unit_cols)
    grad_b_in = jnp.sum(grad_both, axis=0, dtype=jnp.float32).reshape(2, unit_cols)
    grad_in_w = jnp.dot(h_three.T, grad_both, preferred_element_type=jnp.float32).reshape(
        model_width, 2, unit_cols
    )
    three_part = jnp.dot(
        grad_both, in_back.reshape(model_width, 2 * unit_cols).T, preferred_element_type=jnp.float32
    )
    grad_x_norm, grad_gain_three = pull_three(grad_total(three_part))
    grad_x_two = grad_y_mine + grad_x_norm
    grad_two_b = grad_x_two.astype(jnp.bfloat16)
    grad_cross_out_w = jnp.dot(cross_out.T, grad_two_b, preferred_element_type=jnp.float32)
    grad_cross = (
        jnp.dot(grad_two_b, cross_out_back.T, preferred_element_type=jnp.float32)
        .astype(jnp.bfloat16)
        .reshape(row_count, head_count, HD)
    )
    grad_cq, grad_text_key, grad_text_value = attend_backward(
        cross_queries, text_keys, text_values, token_live, cross_lse, grad_cross
    )
    grad_cq_b = grad_cq.reshape(row_count, head_cols).astype(jnp.bfloat16)
    grad_cross_q_w = jnp.dot(h_two.T, grad_cq_b, preferred_element_type=jnp.float32)
    grad_text = jnp.stack([grad_text_key, grad_text_value], axis=1).reshape(
        2 * text_rows, 2 * head_cols
    )
    two_part = jnp.dot(grad_cq_b, cross_q_back.T, preferred_element_type=jnp.float32)
    grad_x_norm, grad_gain_two = pull_two(grad_total(two_part))
    grad_x_one = grad_x_two + grad_x_norm
    grad_one_b = grad_x_one.astype(jnp.bfloat16)
    grad_attn_out_w = jnp.dot(self_out.T, grad_one_b, preferred_element_type=jnp.float32)
    grad_self = (
        jnp.dot(grad_one_b, attn_out_back.T, preferred_element_type=jnp.float32)
        .astype(jnp.bfloat16)
        .reshape(row_count, head_count, HD)
    )
    grad_query, grad_key_all, grad_value_all = attend_backward(
        queries, key_all, value_all, key_live, self_lse, grad_self
    )
    grad_key_flat = grad_key_all.reshape(2 * row_count, head_cols)
    grad_value_flat = grad_value_all.reshape(2 * row_count, head_cols)
    back = from_partner(
        (
            partner_rows(grad_key_flat, which_half, row_count),
            partner_rows(grad_value_flat, which_half, row_count),
            partner_rows(grad_text, which_half, text_rows),
        ),
        "dp",
        0,
    )
    grad_key_own = (own_rows(grad_key_flat, which_half, row_count) + back[0]).reshape(
        row_count, head_count, HD
    )
    grad_value_own = own_rows(grad_value_flat, which_half, row_count) + back[1]
    grad_text_own = (own_rows(grad_text, which_half, text_rows) + back[2]).astype(jnp.bfloat16)
    grad_query_raw = rotate(grad_query, -positions).reshape(row_count, head_cols)
    grad_key_raw = rotate(grad_key_own, -positions).reshape(row_count, head_cols)
    grad_qkv_b = (
        jnp.stack([grad_query_raw, grad_key_raw, grad_value_own], axis=1)
        .astype(jnp.bfloat16)
        .reshape(row_count, 3 * head_cols)
    )
    grad_qkv_w = jnp.dot(h_one.T, grad_qkv_b, preferred_element_type=jnp.float32).reshape(
        model_width, 3, head_cols
    )
    grad_cross_kv_w = jnp.dot(context.T, grad_text_own, preferred_element_type=jnp.float32).reshape(
        text_width, 2, head_cols
    )
    one_part = jnp.dot(
        grad_qkv_b,
        qkv_back.reshape(model_width, 3 * head_cols).T,
        preferred_element_type=jnp.float32,
    )
    grad_x_norm, grad_gain_one = pull_one(grad_total(one_part))
    grad_tokens = grad_x_one + grad_x_norm
    grad_gains = jnp.stack([grad_gain_one, grad_gain_two, grad_gain_three], axis=0)
    summed = (
        lax.psum_scatter(grad_qkv_w, "dp", scatter_dimension=0, tiled=True),
        lax.psum_scatter(grad_attn_out_w, "dp", scatter_dimension=1, tiled=True),
        lax.psum_scatter(grad_cross_q_w, "dp", scatter_dimension=0, tiled=True),
        lax.psum_scatter(grad_cross_kv_w, "dp", scatter_dimension=0, tiled=True),
        lax.psum_scatter(grad_cross_out_w, "dp", scatter_dimension=1, tiled=True),
        lax.psum_scatter(grad_in_w, "dp", scatter_dimension=0, tiled=True),
        lax.psum_scatter(grad_out_w, "dp", scatter_dimension=1, tiled=True),
        lax.psum_scatter(grad_gains, "dp", scatter_dimension=1, tiled=True),
        lax.psum_scatter(grad_b_in, "dp", scatter_dimension=1, tiled=True),
        lax.psum_scatter(grad_b_out, "dp", scatter_dimension=0, tiled=True),
    )
    return (
        mixed,
        grad_tokens,
        summed[0],
        summed[1],
        summed[2],
        summed[3],
        summed[4],
        summed[5],
        summed[6],
        summed[7],
        summed[8],
        summed[9],
    )


def near_body(
    tokens,
    context,
    frame_counts,
    text_counts,
    w_qkv,
    w_attn_out,
    w_cross_q,
    w_cross_kv,
    w_cross_out,
    w_in,
    w_out,
    norm_gains,
    b_in,
    b_out,
    cotangent,
):
    n, dp = lax.axis_size("mp"), lax.axis_size("dp")
    shard, _, cols = w_qkv.shape
    tables, key_bias, text_bias, vec, *shards = prepare(
        tokens,
        context,
        frame_counts,
        text_counts,
        w_qkv,
        w_attn_out,
        w_cross_q,
        w_cross_kv,
        w_cross_out,
        w_in,
        w_out,
        norm_gains,
        b_in,
        b_out,
    )
    saved = run_forward(n, dp, tokens, context, tables, key_bias, text_bias, vec, *shards)
    mixed, gt, gg, *parts = run_backward(n, dp, tokens, context, cotangent, tables, saved)
    g_out, g_in, g_small, g_ckv, g_qkv = scatter_all(parts, 2)
    vec_sum = lax.psum_scatter(gg, "dp", scatter_dimension=1, tiled=True)
    return (
        mixed,
        gt.astype(F32),
        g_qkv.reshape(shard, 3, cols),
        g_small[:, :cols].T,
        g_small[:, cols : 2 * cols],
        g_ckv.reshape(-1, 2, cols),
        g_small[:, 2 * cols :].T,
        g_in.reshape(shard, 2, -1),
        g_out.T,
        lax.psum(vec_sum[:3], "mp"),
        vec_sum[3:5],
        vec_sum[5],
    )


def solution(mesh):
    in_specs = (
        P("dp", None),
        P("dp", None),
        P(),
        P(),
        P("dp", None, "mp"),
        P("mp", "dp"),
        P("dp", "mp"),
        P("dp", None, "mp"),
        P("mp", "dp"),
        P("dp", None, "mp"),
        P("mp", "dp"),
        P(None, "dp"),
        P(None, ("mp", "dp")),
        P("dp"),
        P("dp", None),
    )
    out_specs = (
        P("dp", None),
        P("dp", None),
        P("dp", None, "mp"),
        P("mp", "dp"),
        P("dp", "mp"),
        P("dp", None, "mp"),
        P("mp", "dp"),
        P("dp", None, "mp"),
        P("mp", "dp"),
        P(None, "dp"),
        P(None, ("mp", "dp")),
        P("dp"),
    )
    near = mesh.shape["dp"] == 8
    return jax.shard_map(
        near_body if near else body,
        mesh=mesh,
        in_specs=in_specs,
        out_specs=out_specs,
        check_vma=False,
    )
```

```python
import functools

import jax
import jax.numpy as jnp
from jax import lax
from jax.experimental import pallas as pl
from jax.experimental.pallas import tpu as pltpu
from jax.sharding import PartitionSpec as P

HD = 64
MESH = pl.DeviceIdType.MESH
HBM = pl.BlockSpec(memory_space=pl.ANY)
BF = jnp.bfloat16
F32 = jnp.float32
epsilon = 1e-05
CH = 32
LAG = 2
DMA = pltpu.SemaphoreType.DMA
WHOLE = (0, 0)


def dot_nn(a, b):
    return lax.dot_general(a, b, (((1,), (0,)), ((), ())), preferred_element_type=F32)


def dot_nt(a, b):
    return lax.dot_general(a, b, (((1,), (1,)), ((), ())), preferred_element_type=F32)


def dot_tn(a, b):
    return lax.dot_general(a, b, (((0,), (0,)), ((), ())), preferred_element_type=F32)


def send(src, dst, send_sem, recv_sem, peer):
    return pltpu.make_async_remote_copy(
        src_ref=src,
        dst_ref=dst,
        send_sem=send_sem,
        recv_sem=recv_sem,
        device_id=peer,
        device_id_type=MESH,
    )


def rows_at(start, size):
    return pl.ds(pl.multiple_of(start, 16), size)


def greet_all(d, z, n, dp):
    barrier = pltpu.get_barrier_semaphore()
    for k in range(1, dp):
        pl.semaphore_signal(barrier, inc=1, device_id=(jnp.bitwise_xor(d, k), z), device_id_type=MESH)
    for k in range(1, n):
        pl.semaphore_signal(barrier, inc=1, device_id=(d, lax.rem(z + k, n)), device_id_type=MESH)
    pl.semaphore_wait(barrier, dp + n - 2)


def normal(x):
    centered = x - jnp.mean(x, axis=-1, keepdims=True)
    r = lax.rsqrt(jnp.mean(centered * centered, axis=-1, keepdims=True) + epsilon)
    return centered * r, r


class Line:
    def __init__(self, d, z, n, own, got, dst, base, sems, k, fin):
        self.d, self.z, self.n = d, z, n
        self.own, self.got, self.dst, self.base = own, got, dst, base
        self.sems, self.k, self.fin = sems, k, fin
        self.half = own.shape[0] // 2
        self.chunks = self.half // CH
        self.slots = self.chunks + 2 * LAG * (n - 1)
        self.next = 0

    def place(self, f):
        z, n = self.z, self.n
        return (z, z + 1, z - 1) if f else (n - 1 - z, z - 1, z + 1)

    def fore(self, f, c, nxt):
        at = rows_at(f * self.half + c * CH, CH)
        s, r = self.sems[0], self.sems[1]
        return send(
            self.own.at[at], self.got.at[at], s.at[self.k, f, c], r.at[self.k, f, c], (self.d, nxt)
        )

    def back(self, f, c, prv):
        at = rows_at(self.base + f * self.half + c * CH, CH)
        s, r = self.sems[2], self.sems[3]
        return send(
            self.dst.at[at], self.dst.at[at], s.at[self.k, f, c], r.at[self.k, f, c], (self.d, prv)
        )

    def slot(self, s):
        n = self.n
        for f in range(2):
            p, nxt, prv = self.place(f)
            c = s - LAG * p
            valid = (c >= 0) & (c < self.chunks)

            @pl.when(valid & (p == 0))
            def _():
                self.fore(f, c, nxt).start()

            @pl.when(valid & (p > 0))
            def _():
                at = rows_at(f * self.half + c * CH, CH)
                self.fore(f, c, nxt).wait_recv()
                total = self.own[at].astype(F32) + self.got[at].astype(F32)

                @pl.when(p < n - 1)
                def _():
                    self.own[at] = total.astype(BF)
                    self.fore(f, c, nxt).start()

                @pl.when(p == n - 1)
                def _():
                    self.fin(f * self.half + c * CH, total)
                    self.back(f, c, prv).start()

            b = s - LAG * (2 * (n - 1) - p)

            @pl.when((b >= 0) & (b < self.chunks) & (p < n - 1))
            def _():
                self.back(f, b, prv).wait_recv()

                @pl.when(p > 0)
                def _():
                    self.back(f, b, prv).start()

    def step(self):
        self.slot(self.next)
        self.next += 1

    def left(self):
        return self.slots - self.next

    def drain(self):
        def body(c, carry):
            for f in range(2):
                p, nxt, prv = self.place(f)

                @pl.when(p < self.n - 1)
                def _():
                    self.fore(f, c, nxt).wait_send()

                @pl.when(p > 0)
                def _():
                    self.back(f, c, prv).wait_send()

            return carry

        lax.fori_loop(0, self.chunks, body, 0)


def run(count, *lines):
    lines = [line for line in lines if line.next < line.slots]
    first = [line.next for line in lines]

    def body(s, carry):
        for line, at in zip(lines, first):
            line.slot(at + s)
        return carry

    lax.fori_loop(0, count, body, 0)
    for line in lines:
        line.next += count


class Gather:
    def __init__(self, d, z, shard, full, send_sems, recv_sems, local_sems, a):
        self.d, self.z, self.shard, self.full, self.a = d, z, shard, full, a
        self.send_sems, self.recv_sems, self.local = send_sems, recv_sems, local_sems
        self.size = shard.shape[0]
        self.core, self.xn, self.yn = [(jnp.bitwise_xor(d, k), z) for k in (1, 2, 4)]
        self.bx, self.by, self.bd = [jnp.bitwise_xor(d, k) for k in (2, 4, 6)]
        half = self.size // 2
        self.top, self.bottom = (0, half), (half, half)
        self.started = []

    def part(self, block, rows):
        lo, size = rows
        return self.full.at[rows_at(block * self.size + lo, size or self.size)]

    def copy(self, k, block, rows, peer):
        part = self.part(block, rows)
        return send(part, part, self.send_sems.at[self.a, k], self.recv_sems.at[self.a, k], peer)

    def go(self, k, block, rows, peer):
        cp = self.copy(k, block, rows, peer)
        cp.start()
        self.started.append(cp)

    def got(self, k, block, rows, peer):
        self.copy(k, block, rows, peer).wait_recv()

    def begin(self):
        for k, peer in ((0, self.xn), (1, self.yn), (2, self.core)):
            cp = send(
                self.shard,
                self.part(self.d, WHOLE),
                self.send_sems.at[self.a, k],
                self.recv_sems.at[self.a, k],
                peer,
            )
            cp.start()
            self.started.append(cp)
        self.mine = pltpu.make_async_copy(self.shard, self.part(self.d, WHOLE), self.local.at[self.a])
        self.mine.start()

    def near(self):
        self.got(0, self.bx, WHOLE, self.xn)
        self.go(3, self.bx, self.top, self.yn)
        self.go(5, self.bx, WHOLE, self.core)
        self.got(1, self.by, WHOLE, self.yn)
        self.go(4, self.by, self.bottom, self.xn)
        self.go(6, self.by, WHOLE, self.core)

    def far(self):
        self.got(3, self.bd, self.top, self.yn)
        self.go(7, self.bd, self.top, self.core)
        self.got(4, self.bd, self.bottom, self.xn)
        self.go(8, self.bd, self.bottom, self.core)

    def last(self):
        o = [jnp.bitwise_xor(b, 1) for b in (self.d, self.bx, self.by, self.bd)]
        self.got(2, o[0], WHOLE, self.core)
        self.got(5, o[1], WHOLE, self.core)
        self.got(6, o[2], WHOLE, self.core)
        self.got(7, o[3], self.top, self.core)
        self.got(8, o[3], self.bottom, self.core)
        self.mine.wait()

    def drain(self):
        for cp in self.started:
            cp.wait_send()


class Moves:
    def __init__(self, sems):
        self.sems, self.used = sems, 0

    def start(self, src, dst):
        cp = pltpu.make_async_copy(src, dst, self.sems.at[self.used])
        self.used += 1
        cp.start()
        return cp


def turn(u, cosine, low, high):
    return u * cosine + pltpu.roll(u, 112, 1) * low + pltpu.roll(u, 16, 1) * high


def half_mask(rows, e):
    lane = lax.broadcasted_iota(jnp.int32, (rows, 128), 1)
    return (lane >= 64) == (e == 1)


def softmax(s):
    w = jnp.exp(s - jnp.max(s, axis=-1, keepdims=True))
    return w * (1.0 / jnp.sum(w, axis=-1, keepdims=True))


class Scatter:
    def __init__(self, d, z, got, one, two, out, sems, out_sem):
        self.d, self.z = d, z
        self.got, self.one, self.two, self.out = got, one, two, out
        self.sems, self.out_sem = sems, out_sem
        self.c, self.x, self.y = lax.rem(d, 2), lax.rem(d // 2, 2), d // 4
        self.core, self.xn, self.yn = [(jnp.bitwise_xor(d, k), z) for k in (1, 2, 4)]
        self.arrays, self.copies, self.now = [], [], 0

    def add(self, size, buf, place, compute, dst):
        self.arrays.append((size, buf, place, compute, dst))
        self.copies.append({})

    def block(self, a, j, c, lo=0, size=None):
        shard, buf, place, _, _ = self.arrays[a]
        row, lane = place(j)
        width = self.got.shape[-1]
        return buf.at[rows_at(row + c * shard + lo, size or shard), pl.ds(pl.multiple_of(lane, 128), width)]

    def go(self, a, stage, k, src, dst, peer):
        sd, rv = self.sems[stage]
        cp = send(src, dst, sd.at[a % 2, k], rv.at[a % 2, k], peer)
        cp.start()
        self.copies[a][stage, k] = cp

    def core_copy(self, a, t):
        sd, rv = self.sems[0]
        shard = self.arrays[a][0]
        return send(
            self.block(a, t, 1 - self.c),
            self.got.at[a % 2, t, pl.ds(0, shard)],
            sd.at[a % 2, t],
            rv.at[a % 2, t],
            self.core,
        )

    def compute(self, a, between):
        _, buf, place, tile, _ = self.arrays[a]

        def step(t, carry):
            tile(t)
            self.core_copy(a, t).start()
            between(t)
            return carry

        lax.fori_loop(0, 4, step, 0)

    def plus(self, ref, part):
        piece = 48

        def body(i, carry):
            at = rows_at(i * piece, piece)
            ref[at] = ref[at] + part[at]
            return carry

        lax.fori_loop(0, ref.shape[0] // piece, body, 0)

    def add_core(self, a):
        shard = self.arrays[a][0]
        half = shard // 2

        def body(j, carry):
            self.core_copy(a, j).wait_recv()
            self.plus(self.block(a, j, self.c), self.got.at[a % 2, j])
            return carry

        lax.fori_loop(0, 4, body, 0)
        for b in range(2):
            for side, j, lo, peer in (
                (0, 2 * b + 1 - self.x, 0, self.xn),
                (1, 2 * (1 - self.y) + b, half, self.yn),
            ):
                self.go(
                    a,
                    1,
                    2 * side + b,
                    self.block(a, j, self.c, lo, half),
                    self.one.at[a % 2, side, b, pl.ds(0, half)],
                    peer,
                )

    def add_one(self, a):
        half = self.arrays[a][0] // 2
        for b in range(2):
            for side, j, lo in ((0, 2 * b + self.x, 0), (1, 2 * self.y + b, half)):
                self.copies[a][1, 2 * side + b].wait_recv()
                self.plus(self.block(a, j, self.c, lo, half), self.one.at[a % 2, side, b])
        for side, j, lo, peer in (
            (0, 2 * (1 - self.y) + self.x, 0, self.yn),
            (1, 2 * self.y + 1 - self.x, half, self.xn),
        ):
            self.go(
                a,
                2,
                side,
                self.block(a, j, self.c, lo, half),
                self.two.at[a % 2, side, pl.ds(0, half)],
                peer,
            )

        def body(t, carry):
            self.core_copy(a, t).wait_send()
            return carry

        lax.fori_loop(0, 4, body, 0)

    def out_copy(self, a):
        shard, dst = self.arrays[a][0], self.arrays[a][4]
        return pltpu.make_async_copy(self.out.at[a % 2, pl.ds(0, shard)], dst, self.out_sem.at[a % 2])

    def add_two(self, a):
        half = self.arrays[a][0] // 2
        piece = 48
        for side in range(2):
            self.copies[a][2, side].wait_recv()
            ref = self.block(a, 2 * self.y + self.x, self.c, side * half, half)

            def body(i, carry, side=side, ref=ref):
                at = rows_at(i * piece, piece)
                to = rows_at(side * half + i * piece, piece)
                self.out[a % 2, to] = ref[at].astype(F32) + self.two[a % 2, side, at].astype(F32)
                return carry

            lax.fori_loop(0, half // piece, body, 0)
        self.out_copy(a).start()
        for k in range(4):
            self.copies[a][1, k].wait_send()

    def retire(self, a):
        for k in range(2):
            self.copies[a][2, k].wait_send()
        self.out_copy(a).wait()

    def step(self, between=None):
        s, count = self.now, len(self.arrays)
        self.now += 1
        for lag, stage in ((4, self.retire), (3, self.add_two), (2, self.add_one), (1, self.add_core)):
            if 0 <= s - lag < count:
                stage(s - lag)
        if s < count:
            self.compute(s, between or (lambda t: None))


FWD_LINES = 4


def forward_kernel(
    n,
    dp,
    tokens,
    context,
    tables,
    key_bias,
    text_bias,
    vec,
    s_qkv,
    s_small,
    s_ckv,
    s_out,
    s_in,
    w_qkv,
    w_small,
    w_out,
    w_in,
    o_gv,
    o_h1,
    o_q,
    o_k,
    o_v,
    o_p,
    o_so,
    o_x1,
    o_h2,
    o_cq,
    o_tkv,
    o_pc,
    o_co,
    o_x2,
    o_h3,
    v_vec,
    gv,
    v_qkv,
    v_small,
    v_ckv,
    tok,
    ctx,
    tab,
    kb,
    tb,
    h1,
    q,
    k,
    v,
    probs,
    so,
    x1,
    h2,
    cq,
    tkv,
    pc,
    co,
    x2,
    h3,
    own,
    got,
    g_send,
    g_recv,
    g_local,
    v_send,
    v_recv,
    k_send,
    k_recv,
    fs,
    fr,
    bs,
    br,
    moves,
):
    d = lax.axis_index("dp")
    z = lax.axis_index("mp")
    rows = tokens.shape[0]
    group = rows // 2
    cols = so.shape[1]
    pairs = cols // 128
    half = lax.rem(d, 2)
    mv = Moves(moves)
    ld_tok = mv.start(tokens, tok)
    ld_small = [
        mv.start(a, b) for a, b in ((context, ctx), (tables, tab), (key_bias, kb), (text_bias, tb))
    ]
    ld_vec = mv.start(vec, v_vec.at[d])
    greet_all(d, z, n, dp)
    vec_copies = []
    for j in range(1, dp):
        peer = (jnp.bitwise_xor(d, j), z)
        cp = send(vec, v_vec.at[d], v_send.at[j], v_recv.at[j], peer)
        cp.start()
        vec_copies.append(cp)
    gathers = [
        Gather(d, z, shard, full, g_send, g_recv, g_local, a)
        for a, (shard, full) in enumerate(
            ((s_qkv, v_qkv), (s_ckv, v_ckv), (s_small, v_small), (s_out, w_out), (s_in, w_in))
        )
    ]
    g_qkv, g_ckv, g_small, g_out, g_in = gathers
    g_qkv.begin()
    ld_tok.wait()
    ld_vec.wait()
    for j in range(1, dp):
        b = jnp.bitwise_xor(d, j)
        send(v_vec.at[b], v_vec.at[b], v_send.at[j], v_recv.at[j], (b, z)).wait_recv()
    width = s_qkv.shape[0]
    for b in range(dp):
        gv[:, b * width : (b + 1) * width] = v_vec[b][:8, :width].astype(F32)

    def norm_rows(i, carry):
        at = rows_at(i * CH, CH)
        nrm, _ = normal(tok[at].astype(F32))
        h1[at] = (nrm * gv[0:1]).astype(BF)
        return carry

    lax.fori_loop(0, rows // CH // 2, norm_rows, 0)
    g_qkv.near()
    g_ckv.begin()
    g_small.begin()
    lax.fori_loop(rows // CH // 2, rows // CH, norm_rows, 0)
    st = [mv.start(h1, o_h1)]
    g_qkv.far()
    g_qkv.last()
    for ld in ld_small:
        ld.wait()
    my_rows = half * rows

    def project(g, carry):
        at = rows_at(g * group, group)
        mine = rows_at(my_rows + g * group, group)
        x = h1[at]
        for part in (1, 2, 0):
            u = dot_nn(x, v_qkv[:, part * cols : (part + 1) * cols])
            if part == 2:
                v[mine] = u.astype(BF)
                continue
            for j in range(pairs):
                r = turn(u[:, j * 128 : (j + 1) * 128], tab[0, at], tab[1, at], tab[2, at])
                if part:
                    k[mine, j * 128 : (j + 1) * 128] = r.astype(BF)
                else:
                    q[at, j * 128 : (j + 1) * 128] = (r * HD ** (-0.5)).astype(BF)
        return carry

    lax.fori_loop(0, 2, project, 0)
    core = (jnp.bitwise_xor(d, 1), z)
    mine, theirs = rows_at(my_rows, rows), rows_at((1 - half) * rows, rows)
    kv = [send(r.at[mine], r.at[mine], k_send.at[i], k_recv.at[i], core) for i, r in enumerate((k, v))]
    for cp in kv:
        cp.start()
    g_ckv.near()
    g_small.near()
    g_out.begin()
    g_ckv.far()
    g_ckv.last()
    g_small.far()
    g_in.begin()
    text = ctx.shape[0]
    t_mine, t_theirs = rows_at(half * text, text), rows_at((1 - half) * text, text)
    tkv[t_mine] = dot_nn(ctx[...], v_ckv[...]).astype(BF)
    kv.append(send(tkv.at[t_mine], tkv.at[t_mine], k_send.at[2], k_recv.at[2], core))
    kv[2].start()
    for i, (r, at) in enumerate(((k, theirs), (v, theirs))):
        send(r.at[at], r.at[at], k_send.at[i], k_recv.at[i], core).wait_recv()
    st += [mv.start(v_qkv, w_qkv), mv.start(q, o_q), mv.start(k, o_k), mv.start(v, o_v)]

    def attend(g, queries, keys, key_lo, values, value_lo, bias, save, out, between):
        at = rows_at(g * group, group)

        def head(h, carry):
            j, e = h // 2, lax.rem(h, 2)
            lo = pl.multiple_of(j * 128, 128)
            mask = half_mask(group, e)
            qb = jnp.where(mask, queries[at, pl.ds(lo, 128)], jnp.zeros((), BF))
            s = dot_nt(qb, keys[:, pl.ds(pl.multiple_of(key_lo + lo, 128), 128)]) + bias[0:1]
            p = softmax(s).astype(BF)
            save[h, at] = p
            o = dot_nn(p, values[:, pl.ds(pl.multiple_of(value_lo + lo, 128), 128)])
            out[at, pl.ds(lo, 128)] = jnp.where(mask, o.astype(BF), out[at, pl.ds(lo, 128)])
            between(h)
            return carry

        lax.fori_loop(0, 2 * pairs, head, 0)

    def quiet(h):
        pass

    def with_line(line, every):
        first = line.next

        def between(h):
            if every == 1:
                line.slot(first + h)
            else:

                @pl.when(lax.rem(h, every) == 0)
                def _():
                    line.slot(first + h // every)

        line.next += -(-2 * pairs // every)
        return between

    sems = (fs, fr, bs, br)

    def finish_one(g):
        def fin(lo, total):
            at = rows_at(g * group + lo, CH)
            mine = rows_at(g * group // 2 + lax.rem(lo, group // 2), CH)
            x = tok[at].astype(F32) + total
            x1[mine] = x
            h2[at] = (normal(x)[0] * gv[1:2]).astype(BF)

        return fin

    def finish_two(g):
        def fin(lo, total):
            at = rows_at(g * group + lo, CH)
            mine = rows_at(g * group // 2 + lax.rem(lo, group // 2), CH)
            x = x1[mine] + total
            x2[mine] = x
            h3[at] = (normal(x)[0] * gv[2:3]).astype(BF)

        return fin

    one = [
        Line(d, z, n, own.at[g], got.at[g], h2, g * group, sems, g, finish_one(g)) for g in range(2)
    ]
    two = [
        Line(d, z, n, own.at[2 + g], got.at[2 + g], h3, g * group, sems, 2 + g, finish_two(g))
        for g in range(2)
    ]

    def self_part(g):
        at = rows_at(g * group, group)
        own[g] = dot_nt(so[at], v_small[:, 0:cols]).astype(BF)

    def cross_project(g):
        at = rows_at(g * group, group)
        cq[at] = (dot_nn(h2[at], v_small[:, cols : 2 * cols]) ).astype(BF) * jnp.asarray(HD ** (-0.5), BF)

    def cross_part(g):
        at = rows_at(g * group, group)
        own[2 + g] = dot_nt(co[at], v_small[:, 2 * cols :]).astype(BF)

    attend(0, q, k, 0, v, 0, kb, probs, so, quiet)
    g_small.last()
    st.append(mv.start(v_small, w_small))
    self_part(0)
    st.append(mv.start(probs.at[:, rows_at(0, group)], o_p.at[:, rows_at(0, group)]))
    attend(1, q, k, 0, v, 0, kb, probs, so, with_line(one[0], 2))
    self_part(1)
    st.append(mv.start(probs.at[:, rows_at(group, group)], o_p.at[:, rows_at(group, group)]))
    st.append(mv.start(so, o_so))
    run(one[0].left(), one[0], one[1])
    send(tkv.at[t_theirs], tkv.at[t_theirs], k_send.at[2], k_recv.at[2], core).wait_recv()
    st.append(mv.start(tkv, o_tkv))
    cross_project(0)
    attend(0, cq, tkv, 0, tkv, cols, tb, pc, co, with_line(one[1], 6))
    cross_part(0)
    g_out.near()
    g_in.near()
    run(one[1].left(), one[1], two[0])
    cross_project(1)
    attend(1, cq, tkv, 0, tkv, cols, tb, pc, co, with_line(two[0], 3))
    cross_part(1)
    st += [mv.start(h2, o_h2), mv.start(x1, o_x1), mv.start(cq, o_cq), mv.start(pc, o_pc), mv.start(co, o_co)]
    run(4, two[0], two[1])
    g_out.far()
    g_in.far()
    run(two[0].left(), two[0], two[1])
    run(two[1].left(), two[1])
    st += [mv.start(h3, o_h3), mv.start(x2, o_x2), mv.start(gv, o_gv)]
    g_out.last()
    g_in.last()
    for g in gathers:
        g.drain()
    for cp in vec_copies + kv:
        cp.wait_send()
    for line in one + two:
        line.drain()
    for cp in st:
        cp.wait()


def run_forward(n, dp, tokens, context, tables, key_bias, text_bias, vec, s_qkv, s_small, s_ckv, s_out, s_in):
    rows, width = tokens.shape
    cols3 = s_qkv.shape[1]
    cols = cols3 // 3
    heads = cols // HD
    text = context.shape[0]
    half_rows = rows // 2
    sds = jax.ShapeDtypeStruct
    outs = [
        sds((width, cols3), BF),
        sds((width, cols3), BF),
        sds((width, s_out.shape[1]), BF),
        sds((width, s_in.shape[1]), BF),
        sds((8, width), F32),
        sds((rows, width), BF),
        sds((rows, cols), BF),
        sds((2 * rows, cols), BF),
        sds((2 * rows, cols), BF),
        sds((heads, rows, 2 * rows), BF),
        sds((rows, cols), BF),
        sds((half_rows, width), F32),
        sds((rows, width), BF),
        sds((rows, cols), BF),
        sds((2 * text, 2 * cols), BF),
        sds((heads, rows, 2 * text), BF),
        sds((rows, cols), BF),
        sds((half_rows, width), F32),
        sds((rows, width), BF),
    ]
    vm = pltpu.VMEM
    chunks = rows // 4 // CH
    saved = [vm(o.shape, o.dtype) for o in outs[5:]]
    scratch = [
        vm((dp,) + vec.shape, BF),
        vm((8, width), F32),
        vm((width, cols3), BF),
        vm((width, cols3), BF),
        vm((s_ckv.shape[0] * dp, s_ckv.shape[1]), BF),
        vm(tokens.shape, BF),
        vm(context.shape, BF),
        vm(tables.shape, F32),
        vm(key_bias.shape, F32),
        vm(text_bias.shape, F32),
        *saved,
        vm((4, half_rows, width), BF),
        vm((4, half_rows, width), BF),
        DMA((5, 9)),
        DMA((5, 9)),
        DMA((5,)),
        DMA((dp,)),
        DMA((dp,)),
        DMA((3,)),
        DMA((3,)),
        *[DMA((FWD_LINES, 2, chunks))] * 4,
        DMA((32,)),
    ]
    return pl.pallas_call(
        functools.partial(forward_kernel, n, dp),
        out_shape=outs,
        in_specs=[HBM] * 11,
        out_specs=[HBM] * len(outs),
        scratch_shapes=scratch,
        compiler_params=pltpu.CompilerParams(
            collective_id=0, has_side_effects=True, vmem_limit_bytes=58 * 2**20
        ),
        name="forward",
    )(tokens, context, tables, key_bias, text_bias, vec, s_qkv, s_small, s_ckv, s_out, s_in)


def backward_kernel(
    n,
    dp,
    tokens,
    context,
    cotangent,
    tables,
    w_qkv,
    w_small,
    w_out,
    w_in,
    i_gv,
    i_h1,
    i_q,
    i_k,
    i_v,
    i_p,
    i_so,
    i_x1,
    i_h2,
    i_cq,
    i_tkv,
    i_pc,
    i_co,
    i_x2,
    i_h3,
    o_mixed,
    o_gt,
    o_gg,
    o_out,
    o_in,
    o_mid,
    o_ckv,
    o_last,
    gv,
    win,
    wout,
    wsmall,
    h2,
    h3,
    dy,
    hid,
    dgu,
    dx2r,
    dx1r,
    x1,
    x2,
    dx,
    q,
    k,
    v,
    so,
    co,
    cq,
    dco,
    dcq,
    dso,
    dqkv,
    tkv,
    dtkv,
    pc,
    pst,
    dk,
    dv,
    ctx,
    tab,
    gg,
    own,
    got,
    krv,
    tst,
    trv,
    s_got,
    s_one,
    s_two,
    s_out,
    ggs,
    ggr,
    ggz,
    ggo,
    k_send,
    k_recv,
    fs,
    fr,
    bs,
    br,
    p_sem,
    c_send,
    c_recv,
    a_send,
    a_recv,
    b_send,
    b_recv,
    s_sem,
    v_send,
    v_recv,
    moves,
):
    d = lax.axis_index("dp")
    z = lax.axis_index("mp")
    rows, width = tokens.shape
    group = rows // 2
    cols = so.shape[1]
    units = hid.shape[1]
    pairs = cols // 128
    half = lax.rem(d, 2)
    core = (jnp.bitwise_xor(d, 1), z)
    mixed, gt = dy, dx2r
    mv = Moves(moves)
    first = [mv.start(a, b) for a, b in ((cotangent, dy), (i_gv, gv), (i_h3, h3))]
    pieces = 2
    piece = units // pieces
    w_loads = []
    for i in range(pieces):
        at = slice(i * piece, (i + 1) * piece)
        up = slice(units + i * piece, units + (i + 1) * piece)
        w_loads.append(
            [
                mv.start(w_in.at[:, at], win.at[:, at]),
                mv.start(w_in.at[:, up], win.at[:, up]),
                mv.start(w_out.at[:, at], wout.at[:, at]),
            ]
        )
    later = [
        mv.start(a, b)
        for a, b in (
            (i_x2, x2),
            (w_small, wsmall),
            (i_x1, x1),
            (i_h2, h2),
            (i_co, co),
            (i_cq, cq),
            (i_tkv, tkv),
            (i_pc, pc),
            (i_q, q),
            (i_k, k),
            (i_v, v),
            (i_so, so),
            (context, ctx),
            (tables, tab),
        )
    ]
    greet_all(d, z, n, dp)
    gg[...] = jnp.zeros_like(gg)
    dtkv[...] = jnp.zeros_like(dtkv)

    def clear(i, carry):
        at = rows_at(i * CH, CH)
        dk[at] = jnp.zeros((CH, cols), F32)
        dv[at] = jnp.zeros((CH, cols), F32)
        return carry

    lax.fori_loop(0, 2 * rows // CH, clear, 0)
    for cp in first:
        cp.wait()

    def bias_sum(i, carry):
        gg[5:6] += jnp.sum(dy[rows_at(i * CH, CH)].astype(F32), axis=0, keepdims=True)
        return carry

    lax.fori_loop(0, rows // CH, bias_sum, 0)
    tile = 256

    def feed(g, lo, count, between):
        at = rows_at(g * group, group)

        def step(i, carry):
            u = pl.multiple_of(i * tile, tile)
            us, ups = pl.ds(u, tile), pl.ds(pl.multiple_of(units + u, tile), tile)
            x = h3[at]
            gate = dot_nn(x, win[:, us]) + gv[3:4, us]
            up = dot_nn(x, win[:, ups]) + gv[4:5, us]
            dh = dot_nn(dy[at], wout[:, us])
            sig = jax.nn.sigmoid(gate)
            act = gate * sig
            hid[at, us] = (act * up).astype(BF)
            d_gate = (dh * up * (sig * (1.0 + gate * (1.0 - sig)))).astype(BF)
            d_up = (dh * act).astype(BF)
            dgu[at, us] = d_gate
            dgu[at, ups] = d_up
            gg[3:4, us] += jnp.sum(d_gate.astype(F32), axis=0, keepdims=True)
            gg[4:5, us] += jnp.sum(d_up.astype(F32), axis=0, keepdims=True)
            between(i)
            return carry

        lax.fori_loop(lo, lo + count, step, 0)

    def norm_back(x, dn, gain, row):
        nrm, r = normal(x)
        gg[row : row + 1] += jnp.sum(dn * nrm, axis=0, keepdims=True)
        e = dn * gain
        return r * (
            e
            - jnp.mean(e, axis=-1, keepdims=True)
            - nrm * jnp.mean(e * nrm, axis=-1, keepdims=True)
        )

    def places(g, lo):
        return rows_at(g * group + lo, CH), rows_at(
            g * group // 2 + lax.rem(lo, group // 2), CH
        )

    def finish_mixed(g):
        def fin(lo, total):
            at, mine = places(g, lo)
            mixed[at] = (x2[mine] + total + gv[5:6]).astype(BF)

        return fin

    def finish_three(g):
        def fin(lo, total):
            at, mine = places(g, lo)
            x = dy[at].astype(F32) + norm_back(x2[mine], total, gv[2:3], 2)
            dx[mine] = x
            dx2r[at] = x.astype(BF)

        return fin

    def finish_two(g):
        def fin(lo, total):
            at, mine = places(g, lo)
            x = dx[mine] + norm_back(x1[mine], total, gv[1:2], 1)
            dx[mine] = x
            dx1r[at] = x.astype(BF)

        return fin

    def finish_one(g):
        def fin(lo, total):
            at, mine = places(g, lo)
            x = dx[mine] + norm_back(h3[at].astype(F32), total, gv[0:1], 0)
            gt[at] = x.astype(BF)

        return fin

    sems = (fs, fr, bs, br)

    def lines(dst, slot, index, fin):
        return [
            Line(
                d, z, n, own.at[slot + g], got.at[slot + g], dst, g * group, sems, index + g, fin(g)
            )
            for g in range(2)
        ]

    mix = lines(mixed, 2, 0, finish_mixed)
    three = lines(dx2r, 0, 2, finish_three)
    two = lines(dx1r, 0, 4, finish_two)
    one = lines(gt, 0, 6, finish_one)

    def quiet(i):
        pass

    def with_lines(total, every, *ls):
        ls = [line for line in ls if line.next < line.slots]
        starts = [line.next for line in ls]

        def between(i):
            def go():
                for line, s in zip(ls, starts):
                    line.slot(s + i // every)

            if every == 1:
                go()
            else:
                pl.when(lax.rem(i, every) == 0)(go)

        for line in ls:
            line.next += -(-total // every)
        return between

    tiles = units // tile
    per = tiles // pieces

    sc = Scatter(
        d, z, s_got, s_one, s_two, s_out, ((c_send, c_recv), (a_send, a_recv), (b_send, b_recv)), s_sem
    )
    shard = width // dp
    wide = s_got.shape[-1]

    def part_of(buf, lane, size, *terms):
        def tile_at(t):
            at = rows_at(t * 2 * size, 2 * size)
            to = lane
            for left, right, lo, count in terms:
                cols_at = pl.ds(pl.multiple_of(t * 2 * size, 128), 2 * size)
                buf[at, to : to + count] = dot_tn(left[:, cols_at], right[:, lo : lo + count]).astype(BF)
                to += count

        return tile_at

    def add_array(buf, lane, dst, *terms):
        sc.add(
            shard,
            buf,
            lambda j: (j * 2 * shard, lane),
            part_of(buf, lane, shard, *terms),
            dst,
        )

    def text_tile(j):
        left = ctx[...]
        t = text_width // 4
        g = dot_tn(left, tst[...]).astype(BF)
        for i in range(4):

            @pl.when(j == i)
            def _():
                dgu[0:t, i * wide : (i + 1) * wide] = g[i * t : (i + 1) * t]

    text_width = ctx.shape[1]
    for i in range(2):
        add_array(wout, i * wide, o_out.at[:, pl.ds(i * wide, wide)], (dy, hid, i * wide, wide))
    for i in range(4):
        add_array(win, i * wide, o_in.at[:, pl.ds(i * wide, wide)], (h3, dgu, i * wide, wide))
    add_array(wout, 0, o_mid, (dx2r, co, 0, cols), (h2, dcq, 0, cols))
    sc.add(text_width // dp, dgu, lambda j: (0, j * wide), text_tile, o_ckv)
    add_array(wout, wide, o_last.at[:, pl.ds(0, wide)], (dx1r, so, 0, cols), (hid, dqkv, 0, cols))
    add_array(win, 2 * wide, o_last.at[:, pl.ds(wide, wide)], (hid, dqkv, cols, wide))

    def attend_back(g, d_out, queries, keys, key_lo, values, value_lo, probs, dkr, dk_lo, dvr, dv_lo, dq, between):
        at = rows_at(g * group, group)

        def head(h, carry):
            j, e = h // 2, lax.rem(h, 2)
            lo = pl.multiple_of(j * 128, 128)
            here = pl.ds(lo, 128)
            mask = half_mask(group, e)
            zero = jnp.zeros((), BF)
            do = jnp.where(mask, d_out[at, here], zero)
            qb = jnp.where(mask, queries[at, here], zero)
            p = probs(h)
            pf = p.astype(F32)
            dp_ = dot_nt(do, values[:, pl.ds(pl.multiple_of(value_lo + lo, 128), 128)])
            ds = (pf * (dp_ - jnp.sum(pf * dp_, axis=-1, keepdims=True))).astype(BF)
            g_q = dot_nn(ds, keys[:, pl.ds(pl.multiple_of(key_lo + lo, 128), 128)]) * HD ** (-0.5)
            dkr[:, pl.ds(pl.multiple_of(dk_lo + lo, 128), 128)] += dot_tn(ds, qb)
            dvr[:, pl.ds(pl.multiple_of(dv_lo + lo, 128), 128)] += dot_tn(p, do)
            dq(h, at, here, mask, g_q)
            between(h)
            return carry

        lax.fori_loop(0, 2 * pairs, head, 0)

    def cross_back(g, between):
        at = rows_at(g * group, group)
        dco[at] = dot_nn(dx2r[at], wsmall[:, 2 * cols :]).astype(BF)

        def dq(h, at, here, mask, g_q):
            dcq[at, here] = jnp.where(mask, g_q.astype(BF), dcq[at, here])

        attend_back(
            g, dco, cq, tkv, 0, tkv, cols, lambda h: pc[h, at], dtkv, 0, dtkv, cols, dq, between
        )

    def self_back(g, between):
        at = rows_at(g * group, group)

        def load(h):
            slot = lax.rem(h, 2)
            return pltpu.make_async_copy(i_p.at[h, at], pst.at[slot], p_sem.at[slot])

        load(0).start()
        dso[at] = dot_nn(dx1r[at], wsmall[:, 0:cols]).astype(BF)

        def probs(h):
            @pl.when(h + 1 < 2 * pairs)
            def _():
                load(h + 1).start()

            load(h).wait()
            return pst[lax.rem(h, 2)]

        def dq(h, at, here, mask, g_q):
            r = turn(g_q, tab[0, at], -tab[1, at], -tab[2, at]).astype(BF)
            dqkv[at, here] = jnp.where(mask, r, dqkv[at, here])

        attend_back(g, dso, q, k, 0, v, 0, probs, dk, 0, dv, 0, dq, between)

    def three_part(g):
        at = rows_at(g * group, group)
        own[g] = dot_nt(dgu[at], win[...]).astype(BF)

    def down_part(g):
        at = rows_at(g * group, group)
        own[2 + g] = dot_nt(hid[at], wout[...]).astype(BF)

    def two_part(g):
        at = rows_at(g * group, group)
        own[g] = dot_nt(dcq[at], wsmall[:, cols : 2 * cols]).astype(BF)

    def one_part(g):
        at = rows_at(g * group, group)
        own[g] = dot_nt(dqkv[at], win[:, 0 : 3 * cols]).astype(BF)

    for i in range(pieces):
        for cp in w_loads[i]:
            cp.wait()
        feed(0, i * per, per, quiet)
    three_part(0)
    for cp in later:
        cp.wait()
    feed(1, 0, tiles, with_lines(tiles, 1, three[0]))
    three_part(1)
    down_part(0)
    run(1, three[0], three[1])
    down_part(1)
    run(1, three[0], three[1])
    sc.step(with_lines(4, 1, three[0], three[1]))
    sc.step(with_lines(4, 1, three[0], three[1]))
    ld_h1 = mv.start(i_h1, hid)
    run(three[0].left(), three[0], three[1])
    cross_back(0, with_lines(6, 3, three[1]))
    three[0].drain()
    two_part(0)
    sc.step(with_lines(4, 1, three[1], two[0]))
    run(three[1].left(), three[1], two[0])
    cross_back(1, with_lines(6, 3, two[0]))
    three[1].drain()
    two_part(1)
    text = ctx.shape[0]
    t_mine, t_theirs = rows_at(half * text, text), rows_at((1 - half) * text, text)
    tst[...] = dtkv[t_theirs].astype(BF)
    t_copy = send(tst, trv, k_send.at[2], k_recv.at[2], core)
    t_copy.start()
    sc.step(with_lines(4, 1, two[0], two[1]))
    sc.step(with_lines(4, 1, two[0], two[1]))
    run(two[0].left(), two[0], two[1])
    self_back(0, with_lines(6, 1, two[1]))
    two[0].drain()
    sc.step(with_lines(4, 1, two[1]))
    ld_tok = mv.start(tokens, h3)
    run(two[1].left(), two[1])
    sc.step(with_lines(4, 1, mix[0], mix[1]))
    self_back(1, with_lines(6, 1, mix[0], mix[1]))
    two[1].drain()
    mine, theirs = rows_at(half * rows, rows), rows_at((1 - half) * rows, rows)
    dco[...] = dk[theirs].astype(BF)
    k_copy = send(dco, krv.at[0], k_send.at[0], k_recv.at[0], core)
    k_copy.start()
    dcq[...] = dv[theirs].astype(BF)
    v_copy = send(dcq, krv.at[1], k_send.at[1], k_recv.at[1], core)
    v_copy.start()
    t_copy.wait()
    tst[...] = (dtkv[t_mine] + trv[...].astype(F32)).astype(BF)
    sc.step(with_lines(4, 1, mix[0], mix[1]))
    ld_qkv = mv.start(w_qkv, win.at[:, pl.ds(0, 3 * cols)])
    k_copy.wait_recv()
    ld_h1.wait()
    ld_tok.wait()
    for g in range(2):
        at = slice(g * group, (g + 1) * group)
        own_at = rows_at(half * rows + g * group, group)
        for j in range(pairs):
            here = slice(j * 128, (j + 1) * 128)
            u = dk[own_at, here] + krv[0, at, here].astype(F32)
            dqkv[at, cols + j * 128 : cols + (j + 1) * 128] = turn(
                u, tab[0, at], -tab[1, at], -tab[2, at]
            ).astype(BF)
        if g == 0:
            v_copy.wait_recv()
        dqkv[at, 2 * cols :] = (dv[own_at] + krv[1, at].astype(F32)).astype(BF)
        if g == 0:
            ld_qkv.wait()
        one_part(g)
        if g == 0:
            run(2, one[0], mix[0], mix[1])
    sc.step(with_lines(4, 1, one[0], one[1], mix[0], mix[1]))
    sc.step(with_lines(4, 1, one[0], one[1], mix[0], mix[1]))
    run(2, one[0], one[1], mix[0], mix[1])
    sc.step()
    run(2, one[0], one[1], mix[0], mix[1])
    sc.step()
    run(max(one[1].left(), mix[0].left(), mix[1].left()), one[0], one[1], mix[0], mix[1])
    st = [mv.start(mixed, o_mixed), mv.start(gt, o_gt)]
    ggs[...] = jnp.zeros_like(ggs)
    for b in range(dp):
        ggs[b, :, 0:shard] = gg[:, b * shard : (b + 1) * shard]
    sums = []
    for b in range(1, dp):
        to = jnp.bitwise_xor(d, b)
        cp = send(ggs.at[to], ggr.at[b], v_send.at[b], v_recv.at[b], (to, z))
        cp.start()
        sums.append(cp)
    sc.step()
    total = ggs[d]
    for b, cp in enumerate(sums):
        cp.wait_recv()
        total = total + ggr[b + 1]
    ggo[...] = total
    line_sums = []
    for j in range(1, n):
        cp = send(
            ggo, ggz.at[j], v_send.at[dp + j - 1], v_recv.at[dp + j - 1], (d, lax.rem(z + j, n))
        )
        cp.start()
        line_sums.append(cp)
    sc.step()
    for j, cp in enumerate(line_sums):
        cp.wait_recv()
        total = total + ggz[j + 1]
    ggz[0, 0:3] = total[0:3]
    ggz[0, 3:8] = ggo[3:8]
    st.append(mv.start(ggz.at[0], o_gg))
    for cp in sums + line_sums + [k_copy, v_copy]:
        cp.wait_send()
    for line in mix + one:
        line.drain()
    for cp in st:
        cp.wait()


def run_backward(n, dp, tokens, context, cotangent, tables, saved):
    rows, width = tokens.shape
    w_qkv, w_in = saved[0], saved[3]
    cols = w_qkv.shape[1] // 3
    units = w_in.shape[1] // 2
    heads = cols // HD
    text, text_width = context.shape
    shard = width // dp
    half_rows = rows // 2
    sds = jax.ShapeDtypeStruct
    outs = [
        sds((rows, width), BF),
        sds((rows, width), BF),
        sds((8, 256), F32),
        sds((width // dp, units), F32),
        sds((width // dp, 2 * units), F32),
        sds((width // dp, 2 * cols), F32),
        sds((text_width // dp, 2 * cols), F32),
        sds((width // dp, 4 * cols), F32),
    ]
    vm = pltpu.VMEM
    chunks = rows // 4 // CH
    full, head, own_x = vm((rows, width), BF), vm((rows, cols), BF), vm((half_rows, width), F32)
    keys = vm((2 * rows, cols), BF)
    scratch = [
        vm((8, width), F32),
        vm((width, 2 * units), BF),
        vm((width, units), BF),
        vm((width, 3 * cols), BF),
        full,
        full,
        full,
        vm((rows, units), BF),
        vm((rows, 2 * units), BF),
        full,
        full,
        own_x,
        own_x,
        own_x,
        head,
        keys,
        keys,
        head,
        head,
        head,
        head,
        head,
        head,
        vm((rows, 3 * cols), BF),
        vm((2 * text, 2 * cols), BF),
        vm((2 * text, 2 * cols), F32),
        vm((heads, rows, 2 * text), BF),
        vm((2, half_rows, 2 * rows), BF),
        vm((2 * rows, cols), F32),
        vm((2 * rows, cols), F32),
        vm(context.shape, BF),
        vm(tables.shape, F32),
        vm((8, width), F32),
        vm((4, half_rows, width), BF),
        vm((4, half_rows, width), BF),
        vm((2, rows, cols), BF),
        vm((text, 2 * cols), BF),
        vm((text, 2 * cols), BF),
        vm((2, 4, shard, 2 * cols), BF),
        vm((2, 2, 2, shard // 2, 2 * cols), BF),
        vm((2, 2, shard // 2, 2 * cols), BF),
        vm((2, shard, 2 * cols), F32),
        vm((dp, 8, 256), F32),
        vm((dp, 8, 256), F32),
        vm((n, 8, 256), F32),
        vm((8, 256), F32),
        DMA((3,)),
        DMA((3,)),
        *[DMA((8, 2, chunks))] * 4,
        DMA((2,)),
        DMA((2, 4)),
        DMA((2, 4)),
        DMA((2, 4)),
        DMA((2, 4)),
        DMA((2, 2)),
        DMA((2, 2)),
        DMA((2,)),
        DMA((dp + n - 1,)),
        DMA((dp + n - 1,)),
        DMA((40,)),
    ]
    ins = (tokens, context, cotangent, tables, *saved)
    return pl.pallas_call(
        functools.partial(backward_kernel, n, dp),
        out_shape=outs,
        in_specs=[HBM] * len(ins),
        out_specs=[HBM] * len(outs),
        scratch_shapes=scratch,
        compiler_params=pltpu.CompilerParams(
            collective_id=1, has_side_effects=True, vmem_limit_bytes=63 * 2**20
        ),
        name="backward",
    )(*ins)


def prepare(tokens, context, frame_counts, text_counts, w_qkv, w_attn_out, w_cross_q, w_cross_kv, w_cross_out, w_in, w_out, norm_gains, b_in, b_out):
    shard, _, cols = w_qkv.shape
    rows = tokens.shape[0]
    text = context.shape[0]
    vec = jnp.concatenate([norm_gains, b_in, b_out[None]], axis=0)
    vec = jnp.pad(vec, ((0, 16 - vec.shape[0]), (0, 256 - shard)))
    d = lax.axis_index("dp")
    clip, half = d // 2, d % 2
    frames = lax.dynamic_index_in_dim(frame_counts, clip, 0, keepdims=False)
    texts = lax.dynamic_index_in_dim(text_counts, clip, 0, keepdims=False)
    key_bias = jnp.where(jnp.arange(2 * rows) <= frames, 0.0, -1e30).astype(F32)[None]
    text_bias = jnp.where(jnp.arange(2 * text) < texts, 0.0, -1e30).astype(F32)[None]
    m = HD // 4
    lane = jnp.arange(128) % HD
    frequency = 10000.0 ** (-(lane % m).astype(F32) / m)
    angle = (half * rows + jnp.arange(rows)).astype(F32)[:, None] * frequency[None]
    sine = jnp.sin(angle)
    tables = jnp.stack(
        [
            jnp.where(lane < 2 * m, jnp.cos(angle), 1.0),
            jnp.where(lane < m, -sine, 0.0),
            jnp.where((lane >= m) & (lane < 2 * m), sine, 0.0),
        ]
    )
    return (
        tables,
        jnp.broadcast_to(key_bias, (8, 2 * rows)),
        jnp.broadcast_to(text_bias, (8, 2 * text)),
        vec,
        w_qkv.reshape(shard, 3 * cols),
        jnp.concatenate([w_attn_out.T, w_cross_q, w_cross_out.T], axis=1),
        w_cross_kv.reshape(w_cross_kv.shape[0], 2 * cols),
        w_out.T,
        w_in.reshape(shard, -1),
    )


def from_partner(block, axis, stride):
    count = lax.axis_size(axis)
    route = []
    for low in range(count):
        high = low | 1 << stride
        if high != low and high < count:
            route += [(low, high), (high, low)]
    return lax.ppermute(block, axis, route)


def layer_norm(values, gain_row):
    centered = values - jnp.mean(values, axis=-1, keepdims=True)
    spread = jnp.mean(centered * centered, axis=-1, keepdims=True)
    return centered * lax.rsqrt(spread + epsilon) * gain_row


def rotate(tensor, positions):
    quarter = tensor.shape[-1] // 4
    frequency = 10000.0 ** (-jnp.arange(quarter, dtype=jnp.float32) / quarter)
    angles = positions[:, None] * frequency[None, :]
    cosine = jnp.cos(angles)[:, None, :]
    sine_part = jnp.sin(angles)[:, None, :]
    first_part = tensor[..., :quarter]
    second = tensor[..., quarter : 2 * quarter]
    return jnp.concatenate(
        [
            first_part * cosine - second * sine_part,
            second * cosine + first_part * sine_part,
            tensor[..., 2 * quarter :],
        ],
        axis=-1,
    )


def gated_unit(both):
    gate = both[:, 0]
    return gate * jax.nn.sigmoid(gate) * both[:, 1]


def in_order(own_part, other_part, which_half):
    lower_first = jnp.concatenate([own_part, other_part], axis=0)
    upper_first = jnp.concatenate([other_part, own_part], axis=0)
    return jnp.where(which_half == 0, lower_first, upper_first)


def own_rows(whole, which_half, row_count):
    return lax.dynamic_slice_in_dim(whole, which_half * row_count, row_count, 0)


def partner_rows(whole, which_half, row_count):
    return lax.dynamic_slice_in_dim(whole, (1 - which_half) * row_count, row_count, 0)


def masked_scores(query_block, key_all, key_live):
    scale = query_block.shape[-1] ** (-0.5)
    raw_scores = (
        jnp.einsum("qhd,khd->hqk", query_block, key_all, preferred_element_type=jnp.float32) * scale
    )
    return jnp.where(key_live[None, None, :], raw_scores, -1e30)


def attend_forward(queries, key_all, value_all, key_live):
    row_count, head_count, head_size = queries.shape
    block_rows = min(512, row_count)
    blocks = queries.reshape(row_count // block_rows, block_rows, head_count, head_size)

    def per_block(query_block):
        scores = masked_scores(query_block, key_all, key_live)
        row_max = jnp.max(scores, axis=-1, keepdims=True)
        weights = jnp.exp(scores - row_max)
        row_total = jnp.sum(weights, axis=-1, keepdims=True)
        attn_probs = weights / row_total
        block_out = jnp.einsum(
            "hqk,khd->qhd",
            attn_probs.astype(jnp.bfloat16),
            value_all,
            preferred_element_type=jnp.float32,
        )
        return (block_out, row_max + jnp.log(row_total))

    outputs, log_sums = lax.map(per_block, blocks)
    return (outputs.reshape(row_count, head_count, head_size), log_sums)


def attend_backward(queries, key_all, value_all, key_live, log_sums, grad_out):
    row_count, head_count, head_size = queries.shape
    block_rows = min(512, row_count)
    block_shape = (row_count // block_rows, block_rows, head_count, head_size)
    scale = head_size ** (-0.5)

    def per_block(running, block_item):
        query_block, grad_block, lse_block = block_item
        attn_probs = jnp.exp(masked_scores(query_block, key_all, key_live) - lse_block)
        grad_probs = jnp.einsum(
            "qhd,khd->hqk", grad_block, value_all, preferred_element_type=jnp.float32
        )
        row_inner = jnp.sum(attn_probs * grad_probs, axis=-1, keepdims=True)
        grad_scores = (attn_probs * (grad_probs - row_inner)).astype(jnp.bfloat16)
        grad_query = (
            jnp.einsum("hqk,khd->qhd", grad_scores, key_all, preferred_element_type=jnp.float32)
            * scale
        )
        grad_key = (
            running[0]
            + jnp.einsum(
                "hqk,qhd->khd", grad_scores, query_block, preferred_element_type=jnp.float32
            )
            * scale
        )
        grad_value = running[1] + jnp.einsum(
            "hqk,qhd->khd",
            attn_probs.astype(jnp.bfloat16),
            grad_block,
            preferred_element_type=jnp.float32,
        )
        return ((grad_key, grad_value), grad_query)

    zero_keys = jnp.zeros(key_all.shape, jnp.float32)
    (grad_key, grad_value), grad_query = lax.scan(
        per_block,
        (zero_keys, zero_keys),
        (queries.reshape(block_shape), grad_out.reshape(block_shape), log_sums),
    )
    return (grad_query.reshape(row_count, head_count, head_size), grad_key, grad_value)


def branch_total(partial_sum):
    return lax.psum(partial_sum, "mp")


def grad_total(partial_sum):
    return lax.psum(partial_sum, "mp")


def body(
    tokens,
    context,
    frame_counts,
    text_counts,
    w_qkv,
    w_attn_out,
    w_cross_q,
    w_cross_kv,
    w_cross_out,
    w_in,
    w_out,
    norm_gains,
    b_in,
    b_out,
    cotangent,
):
    gathered = (
        lax.all_gather(w_qkv, "dp", axis=0, tiled=True),
        lax.all_gather(w_attn_out, "dp", axis=1, tiled=True),
        lax.all_gather(w_cross_q, "dp", axis=0, tiled=True),
        lax.all_gather(w_cross_kv, "dp", axis=0, tiled=True),
        lax.all_gather(w_cross_out, "dp", axis=1, tiled=True),
        lax.all_gather(w_in, "dp", axis=0, tiled=True),
        lax.all_gather(w_out, "dp", axis=1, tiled=True),
        lax.all_gather(norm_gains, "dp", axis=1, tiled=True),
        lax.all_gather(b_in, "dp", axis=1, tiled=True),
        lax.all_gather(b_out, "dp", axis=0, tiled=True),
    )
    (
        qkv_full,
        attn_out_full,
        cross_q_full,
        cross_kv_full,
        cross_out_full,
        in_full,
        out_full,
        gains_full,
        b_in_full,
        b_out_full,
    ) = gathered
    row_count, model_width = tokens.shape
    text_rows, text_width = context.shape
    head_cols = qkv_full.shape[2]
    unit_cols = in_full.shape[2]
    head_count = head_cols // HD
    device_row = lax.axis_index("dp")
    which_half = device_row % 2
    clip_index = device_row // 2
    frame_live = lax.dynamic_index_in_dim(frame_counts, clip_index, 0, keepdims=False)
    text_live = lax.dynamic_index_in_dim(text_counts, clip_index, 0, keepdims=False)
    positions = (which_half * row_count + jnp.arange(row_count)).astype(jnp.float32)
    key_live = jnp.arange(2 * row_count) <= frame_live
    token_live = jnp.arange(2 * text_rows) < text_live
    gain_rows = gains_full.astype(jnp.float32)
    tokens_f = tokens.astype(jnp.float32)
    grad_y_mine = cotangent.astype(jnp.float32)
    norm_one, pull_one = jax.vjp(layer_norm, tokens_f, gain_rows[0])
    h_one = norm_one.astype(jnp.bfloat16)
    qkv = jnp.dot(
        h_one, qkv_full.reshape(model_width, 3 * head_cols), preferred_element_type=jnp.float32
    ).reshape(row_count, 3, head_count, HD)
    queries = rotate(qkv[:, 0], positions).astype(jnp.bfloat16)
    own_keys = rotate(qkv[:, 1], positions).astype(jnp.bfloat16).reshape(row_count, head_cols)
    own_values = qkv[:, 2].astype(jnp.bfloat16).reshape(row_count, head_cols)
    own_text = jnp.dot(
        context,
        cross_kv_full.reshape(text_width, 2 * head_cols),
        preferred_element_type=jnp.float32,
    ).astype(jnp.bfloat16)
    other = from_partner((own_keys, own_values, own_text), "dp", 0)
    key_all = in_order(own_keys, other[0], which_half).reshape(2 * row_count, head_count, HD)
    value_all = in_order(own_values, other[1], which_half).reshape(2 * row_count, head_count, HD)
    text_all = in_order(own_text, other[2], which_half).reshape(2 * text_rows, 2, head_count, HD)
    text_keys = text_all[:, 0]
    text_values = text_all[:, 1]
    self_attn, self_lse = attend_forward(queries, key_all, value_all, key_live)
    self_out = self_attn.reshape(row_count, head_cols).astype(jnp.bfloat16)
    self_part = jnp.dot(self_out, attn_out_full, preferred_element_type=jnp.float32)
    x_one = tokens_f + branch_total(self_part)
    norm_two, pull_two = jax.vjp(layer_norm, x_one, gain_rows[1])
    h_two = norm_two.astype(jnp.bfloat16)
    cross_queries = (
        jnp.dot(h_two, cross_q_full, preferred_element_type=jnp.float32)
        .astype(jnp.bfloat16)
        .reshape(row_count, head_count, HD)
    )
    cross_attn, cross_lse = attend_forward(cross_queries, text_keys, text_values, token_live)
    cross_out = cross_attn.reshape(row_count, head_cols).astype(jnp.bfloat16)
    cross_part = jnp.dot(cross_out, cross_out_full, preferred_element_type=jnp.float32)
    x_two = x_one + branch_total(cross_part)
    norm_three, pull_three = jax.vjp(layer_norm, x_two, gain_rows[2])
    h_three = norm_three.astype(jnp.bfloat16)
    both = jnp.dot(
        h_three, in_full.reshape(model_width, 2 * unit_cols), preferred_element_type=jnp.float32
    ).reshape(row_count, 2, unit_cols) + b_in_full.astype(jnp.float32)
    hidden_f, pull_unit = jax.vjp(gated_unit, both)
    hidden = hidden_f.astype(jnp.bfloat16)
    down_part = jnp.dot(hidden, out_full, preferred_element_type=jnp.float32)
    mixed = (x_two + branch_total(down_part) + b_out_full.astype(jnp.float32)).astype(jnp.bfloat16)
    again = (
        lax.all_gather(w_qkv, "dp", axis=0, tiled=True),
        lax.all_gather(w_attn_out, "dp", axis=1, tiled=True),
        lax.all_gather(w_cross_q, "dp", axis=0, tiled=True),
        lax.all_gather(w_cross_out, "dp", axis=1, tiled=True),
        lax.all_gather(w_in, "dp", axis=0, tiled=True),
        lax.all_gather(w_out, "dp", axis=1, tiled=True),
    )
    qkv_back = again[0]
    attn_out_back = again[1]
    cross_q_back = again[2]
    cross_out_back = again[3]
    in_back = again[4]
    out_back = again[5]
    grad_y = cotangent.astype(jnp.float32)
    grad_out_w = jnp.dot(hidden.T, cotangent, preferred_element_type=jnp.float32)
    grad_b_out = jnp.sum(grad_y, axis=0)
    grad_hidden = jnp.dot(cotangent, out_back.T, preferred_element_type=jnp.float32)
    grad_both = pull_unit(grad_hidden)[0].astype(jnp.bfloat16).reshape(row_count, 2 * unit_cols)
    grad_b_in = jnp.sum(grad_both, axis=0, dtype=jnp.float32).reshape(2, unit_cols)
    grad_in_w = jnp.dot(h_three.T, grad_both, preferred_element_type=jnp.float32).reshape(
        model_width, 2, unit_cols
    )
    three_part = jnp.dot(
        grad_both, in_back.reshape(model_width, 2 * unit_cols).T, preferred_element_type=jnp.float32
    )
    grad_x_norm, grad_gain_three = pull_three(grad_total(three_part))
    grad_x_two = grad_y_mine + grad_x_norm
    grad_two_b = grad_x_two.astype(jnp.bfloat16)
    grad_cross_out_w = jnp.dot(cross_out.T, grad_two_b, preferred_element_type=jnp.float32)
    grad_cross = (
        jnp.dot(grad_two_b, cross_out_back.T, preferred_element_type=jnp.float32)
        .astype(jnp.bfloat16)
        .reshape(row_count, head_count, HD)
    )
    grad_cq, grad_text_key, grad_text_value = attend_backward(
        cross_queries, text_keys, text_values, token_live, cross_lse, grad_cross
    )
    grad_cq_b = grad_cq.reshape(row_count, head_cols).astype(jnp.bfloat16)
    grad_cross_q_w = jnp.dot(h_two.T, grad_cq_b, preferred_element_type=jnp.float32)
    grad_text = jnp.stack([grad_text_key, grad_text_value], axis=1).reshape(
        2 * text_rows, 2 * head_cols
    )
    two_part = jnp.dot(grad_cq_b, cross_q_back.T, preferred_element_type=jnp.float32)
    grad_x_norm, grad_gain_two = pull_two(grad_total(two_part))
    grad_x_one = grad_x_two + grad_x_norm
    grad_one_b = grad_x_one.astype(jnp.bfloat16)
    grad_attn_out_w = jnp.dot(self_out.T, grad_one_b, preferred_element_type=jnp.float32)
    grad_self = (
        jnp.dot(grad_one_b, attn_out_back.T, preferred_element_type=jnp.float32)
        .astype(jnp.bfloat16)
        .reshape(row_count, head_count, HD)
    )
    grad_query, grad_key_all, grad_value_all = attend_backward(
        queries, key_all, value_all, key_live, self_lse, grad_self
    )
    grad_key_flat = grad_key_all.reshape(2 * row_count, head_cols)
    grad_value_flat = grad_value_all.reshape(2 * row_count, head_cols)
    back = from_partner(
        (
            partner_rows(grad_key_flat, which_half, row_count),
            partner_rows(grad_value_flat, which_half, row_count),
            partner_rows(grad_text, which_half, text_rows),
        ),
        "dp",
        0,
    )
    grad_key_own = (own_rows(grad_key_flat, which_half, row_count) + back[0]).reshape(
        row_count, head_count, HD
    )
    grad_value_own = own_rows(grad_value_flat, which_half, row_count) + back[1]
    grad_text_own = (own_rows(grad_text, which_half, text_rows) + back[2]).astype(jnp.bfloat16)
    grad_query_raw = rotate(grad_query, -positions).reshape(row_count, head_cols)
    grad_key_raw = rotate(grad_key_own, -positions).reshape(row_count, head_cols)
    grad_qkv_b = (
        jnp.stack([grad_query_raw, grad_key_raw, grad_value_own], axis=1)
        .astype(jnp.bfloat16)
        .reshape(row_count, 3 * head_cols)
    )
    grad_qkv_w = jnp.dot(h_one.T, grad_qkv_b, preferred_element_type=jnp.float32).reshape(
        model_width, 3, head_cols
    )
    grad_cross_kv_w = jnp.dot(context.T, grad_text_own, preferred_element_type=jnp.float32).reshape(
        text_width, 2, head_cols
    )
    one_part = jnp.dot(
        grad_qkv_b,
        qkv_back.reshape(model_width, 3 * head_cols).T,
        preferred_element_type=jnp.float32,
    )
    grad_x_norm, grad_gain_one = pull_one(grad_total(one_part))
    grad_tokens = grad_x_one + grad_x_norm
    grad_gains = jnp.stack([grad_gain_one, grad_gain_two, grad_gain_three], axis=0)
    summed = (
        lax.psum_scatter(grad_qkv_w, "dp", scatter_dimension=0, tiled=True),
        lax.psum_scatter(grad_attn_out_w, "dp", scatter_dimension=1, tiled=True),
        lax.psum_scatter(grad_cross_q_w, "dp", scatter_dimension=0, tiled=True),
        lax.psum_scatter(grad_cross_kv_w, "dp", scatter_dimension=0, tiled=True),
        lax.psum_scatter(grad_cross_out_w, "dp", scatter_dimension=1, tiled=True),
        lax.psum_scatter(grad_in_w, "dp", scatter_dimension=0, tiled=True),
        lax.psum_scatter(grad_out_w, "dp", scatter_dimension=1, tiled=True),
        lax.psum_scatter(grad_gains, "dp", scatter_dimension=1, tiled=True),
        lax.psum_scatter(grad_b_in, "dp", scatter_dimension=1, tiled=True),
        lax.psum_scatter(grad_b_out, "dp", scatter_dimension=0, tiled=True),
    )
    return (
        mixed,
        grad_tokens,
        summed[0],
        summed[1],
        summed[2],
        summed[3],
        summed[4],
        summed[5],
        summed[6],
        summed[7],
        summed[8],
        summed[9],
    )


def near_body(
    tokens,
    context,
    frame_counts,
    text_counts,
    w_qkv,
    w_attn_out,
    w_cross_q,
    w_cross_kv,
    w_cross_out,
    w_in,
    w_out,
    norm_gains,
    b_in,
    b_out,
    cotangent,
):
    n, dp = lax.axis_size("mp"), lax.axis_size("dp")
    shard, _, cols = w_qkv.shape
    tables, key_bias, text_bias, vec, *shards = prepare(
        tokens,
        context,
        frame_counts,
        text_counts,
        w_qkv,
        w_attn_out,
        w_cross_q,
        w_cross_kv,
        w_cross_out,
        w_in,
        w_out,
        norm_gains,
        b_in,
        b_out,
    )
    saved = run_forward(n, dp, tokens, context, tables, key_bias, text_bias, vec, *shards)
    mixed, gt, gg, *parts = run_backward(n, dp, tokens, context, cotangent, tables, saved)
    g_out, g_in, g_mid, g_ckv, g_last = parts
    return (
        mixed,
        gt.astype(F32),
        g_last[:, cols:].reshape(shard, 3, cols),
        g_last[:, :cols].T,
        g_mid[:, cols:],
        g_ckv.reshape(-1, 2, cols),
        g_mid[:, :cols].T,
        g_in.reshape(shard, 2, -1),
        g_out.T,
        gg[:3, :shard],
        gg[3:5, :shard],
        gg[5, :shard],
    )


def solution(mesh):
    in_specs = (
        P("dp", None),
        P("dp", None),
        P(),
        P(),
        P("dp", None, "mp"),
        P("mp", "dp"),
        P("dp", "mp"),
        P("dp", None, "mp"),
        P("mp", "dp"),
        P("dp", None, "mp"),
        P("mp", "dp"),
        P(None, "dp"),
        P(None, ("mp", "dp")),
        P("dp"),
        P("dp", None),
    )
    out_specs = (
        P("dp", None),
        P("dp", None),
        P("dp", None, "mp"),
        P("mp", "dp"),
        P("dp", "mp"),
        P("dp", None, "mp"),
        P("mp", "dp"),
        P("dp", None, "mp"),
        P("mp", "dp"),
        P(None, "dp"),
        P(None, ("mp", "dp")),
        P("dp"),
    )
    near = mesh.shape["dp"] == 8
    return jax.shard_map(
        near_body if near else body,
        mesh=mesh,
        in_specs=in_specs,
        out_specs=out_specs,
        check_vma=False,
    )
```

```python
import functools

import jax
import jax.numpy as jnp
from jax import lax
from jax.experimental import pallas as pl
from jax.experimental.pallas import tpu as pltpu
from jax.sharding import PartitionSpec as P

HD = 64
MESH = pl.DeviceIdType.MESH
HBM = pl.BlockSpec(memory_space=pl.ANY)
BF = jnp.bfloat16
F32 = jnp.float32
epsilon = 1e-05
CH = 16
NR = 32
LAG = 2
DMA = pltpu.SemaphoreType.DMA
WHOLE = (0, 0)


def dot_nn(a, b):
    return lax.dot_general(a, b, (((1,), (0,)), ((), ())), preferred_element_type=F32)


def dot_nt(a, b):
    return lax.dot_general(a, b, (((1,), (1,)), ((), ())), preferred_element_type=F32)


def dot_tn(a, b):
    return lax.dot_general(a, b, (((0,), (0,)), ((), ())), preferred_element_type=F32)


def send(src, dst, send_sem, recv_sem, peer):
    return pltpu.make_async_remote_copy(
        src_ref=src,
        dst_ref=dst,
        send_sem=send_sem,
        recv_sem=recv_sem,
        device_id=peer,
        device_id_type=MESH,
    )


def rows_at(start, size):
    return pl.ds(pl.multiple_of(start, 16), size)


def greet_all(d, z, n, dp):
    barrier = pltpu.get_barrier_semaphore()
    for k in range(1, dp):
        pl.semaphore_signal(barrier, inc=1, device_id=(jnp.bitwise_xor(d, k), z), device_id_type=MESH)
    for k in range(1, n):
        pl.semaphore_signal(barrier, inc=1, device_id=(d, lax.rem(z + k, n)), device_id_type=MESH)
    pl.semaphore_wait(barrier, dp + n - 2)


def normal(x):
    centered = x - jnp.mean(x, axis=-1, keepdims=True)
    r = lax.rsqrt(jnp.mean(centered * centered, axis=-1, keepdims=True) + epsilon)
    return centered * r, r


class Line:
    def __init__(self, d, z, n, own, got, dst, base, sems, k, fin):
        self.d, self.z, self.n = d, z, n
        self.own, self.got, self.dst, self.base = own, got, dst, base
        self.sems, self.k, self.fin = sems, k, fin
        self.half = own.shape[0] // 2
        self.chunks = self.half // CH
        self.slots = self.chunks + 2 * LAG * (n - 1)
        self.next = 0

    def place(self, f):
        z, n = self.z, self.n
        return (z, z + 1, z - 1) if f else (n - 1 - z, z - 1, z + 1)

    def fore(self, f, c, nxt):
        at = rows_at(f * self.half + c * CH, CH)
        s, r = self.sems[0], self.sems[1]
        return send(
            self.own.at[at], self.got.at[at], s.at[self.k, f, c], r.at[self.k, f, c], (self.d, nxt)
        )

    def back(self, f, c, prv):
        at = rows_at(self.base + f * self.half + c * CH, CH)
        s, r = self.sems[2], self.sems[3]
        return send(
            self.dst.at[at], self.dst.at[at], s.at[self.k, f, c], r.at[self.k, f, c], (self.d, prv)
        )

    def slot(self, s):
        n = self.n
        for f in range(2):
            p, nxt, prv = self.place(f)
            c = s - LAG * p
            valid = (c >= 0) & (c < self.chunks)

            @pl.when(valid & (p == 0))
            def _():
                self.fore(f, c, nxt).start()

            @pl.when(valid & (p > 0) & (p < n - 1))
            def _():
                at = rows_at(f * self.half + c * CH, CH)
                self.fore(f, c, nxt).wait_recv()
                self.own[at] = self.own[at] + self.got[at]
                self.fore(f, c, nxt).start()

            @pl.when(valid & (p == n - 1))
            def _():
                at = rows_at(f * self.half + c * CH, CH)
                self.fore(f, c, nxt).wait_recv()
                self.fin(f * self.half + c * CH, self.own[at].astype(F32) + self.got[at].astype(F32))
                self.back(f, c, prv).start()

            b = s - LAG * (2 * (n - 1) - p)

            @pl.when((b >= 0) & (b < self.chunks) & (p < n - 1))
            def _():
                self.back(f, b, prv).wait_recv()

                @pl.when(p > 0)
                def _():
                    self.back(f, b, prv).start()

    def step(self):
        self.slot(self.next)
        self.next += 1

    def left(self):
        return self.slots - self.next

    def drain(self):
        def body(c, carry):
            for f in range(2):
                p, nxt, prv = self.place(f)

                @pl.when(p < self.n - 1)
                def _():
                    self.fore(f, c, nxt).wait_send()

                @pl.when(p > 0)
                def _():
                    self.back(f, c, prv).wait_send()

            return carry

        lax.fori_loop(0, self.chunks, body, 0)


def run(count, *lines):
    lines = [line for line in lines if line.next < line.slots]
    count = max(count, 0)
    first = [line.next for line in lines]

    def body(s, carry):
        for line, at in zip(lines, first):
            line.slot(at + s)
        return carry

    lax.fori_loop(0, count, body, 0)
    for line in lines:
        line.next += count


class Gather:
    def __init__(self, d, z, shard, full, send_sems, recv_sems, local_sems, a):
        self.d, self.z, self.shard, self.full, self.a = d, z, shard, full, a
        self.send_sems, self.recv_sems, self.local = send_sems, recv_sems, local_sems
        self.size = shard.shape[0]
        self.core, self.xn, self.yn = [(jnp.bitwise_xor(d, k), z) for k in (1, 2, 4)]
        self.bx, self.by, self.bd = [jnp.bitwise_xor(d, k) for k in (2, 4, 6)]
        half = self.size // 2
        self.top, self.bottom = (0, half), (half, half)
        self.started = []

    def part(self, block, rows):
        lo, size = rows
        return self.full.at[rows_at(block * self.size + lo, size or self.size)]

    def copy(self, k, block, rows, peer):
        part = self.part(block, rows)
        return send(part, part, self.send_sems.at[self.a, k], self.recv_sems.at[self.a, k], peer)

    def go(self, k, block, rows, peer):
        cp = self.copy(k, block, rows, peer)
        cp.start()
        self.started.append(cp)

    def got(self, k, block, rows, peer):
        self.copy(k, block, rows, peer).wait_recv()

    def begin(self):
        for k, peer in ((0, self.xn), (1, self.yn), (2, self.core)):
            cp = send(
                self.shard,
                self.part(self.d, WHOLE),
                self.send_sems.at[self.a, k],
                self.recv_sems.at[self.a, k],
                peer,
            )
            cp.start()
            self.started.append(cp)
        self.mine = pltpu.make_async_copy(self.shard, self.part(self.d, WHOLE), self.local.at[self.a])
        self.mine.start()

    def near(self):
        self.got(0, self.bx, WHOLE, self.xn)
        self.go(3, self.bx, self.top, self.yn)
        self.go(5, self.bx, WHOLE, self.core)
        self.got(1, self.by, WHOLE, self.yn)
        self.go(4, self.by, self.bottom, self.xn)
        self.go(6, self.by, WHOLE, self.core)

    def far(self):
        self.got(3, self.bd, self.top, self.yn)
        self.go(7, self.bd, self.top, self.core)
        self.got(4, self.bd, self.bottom, self.xn)
        self.go(8, self.bd, self.bottom, self.core)

    def last(self):
        o = [jnp.bitwise_xor(b, 1) for b in (self.d, self.bx, self.by, self.bd)]
        self.got(2, o[0], WHOLE, self.core)
        self.got(5, o[1], WHOLE, self.core)
        self.got(6, o[2], WHOLE, self.core)
        self.got(7, o[3], self.top, self.core)
        self.got(8, o[3], self.bottom, self.core)
        self.mine.wait()

    def drain(self):
        for cp in self.started:
            cp.wait_send()


class Moves:
    def __init__(self, sems):
        self.sems, self.used = sems, 0

    def start(self, src, dst):
        cp = pltpu.make_async_copy(src, dst, self.sems.at[self.used])
        self.used += 1
        cp.start()
        return cp


def turn(u, cosine, low, high):
    return u * cosine + pltpu.roll(u, 112, 1) * low + pltpu.roll(u, 16, 1) * high


def half_mask(rows, e):
    lane = lax.broadcasted_iota(jnp.int32, (rows, 128), 1)
    return (lane >= 64) == (e == 1)


def softmax(s):
    w = jnp.exp(s - jnp.max(s, axis=-1, keepdims=True))
    return w * (1.0 / jnp.sum(w, axis=-1, keepdims=True))


class Scatter:
    def __init__(self, d, z, got, one, two, out, sems, out_sem):
        self.d, self.z = d, z
        self.got, self.one, self.two, self.out = got, one, two, out
        self.sems, self.out_sem = sems, out_sem
        self.c, self.x, self.y = lax.rem(d, 2), lax.rem(d // 2, 2), d // 4
        self.core, self.xn, self.yn = [(jnp.bitwise_xor(d, k), z) for k in (1, 2, 4)]
        self.arrays, self.copies, self.now = [], [], 0

    def add(self, size, buf, place, compute, dst):
        self.arrays.append((size, buf, place, compute, dst))
        self.copies.append({})

    def block(self, a, j, c, lo=0, size=None):
        shard, buf, place, _, _ = self.arrays[a]
        row, lane = place(j)
        width = self.got.shape[-1]
        return buf.at[rows_at(row + c * shard + lo, size or shard), pl.ds(pl.multiple_of(lane, 128), width)]

    def go(self, a, stage, k, src, dst, peer):
        sd, rv = self.sems[stage]
        cp = send(src, dst, sd.at[a % 2, k], rv.at[a % 2, k], peer)
        cp.start()
        self.copies[a][stage, k] = cp

    def core_copy(self, a, t):
        sd, rv = self.sems[0]
        shard = self.arrays[a][0]
        return send(
            self.block(a, t, 1 - self.c),
            self.got.at[a % 2, t, pl.ds(0, shard)],
            sd.at[a % 2, t],
            rv.at[a % 2, t],
            self.core,
        )

    def compute(self, a, between):
        _, buf, place, tile, _ = self.arrays[a]

        def step(t, carry):
            tile(t)
            self.core_copy(a, t).start()
            between(t)
            return carry

        lax.fori_loop(0, 4, step, 0)

    def plus(self, ref, part):
        piece = 48

        def body(i, carry):
            at = rows_at(i * piece, piece)
            ref[at] = ref[at] + part[at]
            return carry

        lax.fori_loop(0, ref.shape[0] // piece, body, 0)

    def add_core(self, a):
        shard = self.arrays[a][0]
        half = shard // 2

        def body(j, carry):
            self.core_copy(a, j).wait_recv()
            self.plus(self.block(a, j, self.c), self.got.at[a % 2, j])
            return carry

        lax.fori_loop(0, 4, body, 0)
        for b in range(2):
            for side, j, lo, peer in (
                (0, 2 * b + 1 - self.x, 0, self.xn),
                (1, 2 * (1 - self.y) + b, half, self.yn),
            ):
                self.go(
                    a,
                    1,
                    2 * side + b,
                    self.block(a, j, self.c, lo, half),
                    self.one.at[a % 2, side, b, pl.ds(0, half)],
                    peer,
                )

    def add_one(self, a):
        half = self.arrays[a][0] // 2
        for b in range(2):
            for side, j, lo in ((0, 2 * b + self.x, 0), (1, 2 * self.y + b, half)):
                self.copies[a][1, 2 * side + b].wait_recv()
                self.plus(self.block(a, j, self.c, lo, half), self.one.at[a % 2, side, b])
        for side, j, lo, peer in (
            (0, 2 * (1 - self.y) + self.x, 0, self.yn),
            (1, 2 * self.y + 1 - self.x, half, self.xn),
        ):
            self.go(
                a,
                2,
                side,
                self.block(a, j, self.c, lo, half),
                self.two.at[a % 2, side, pl.ds(0, half)],
                peer,
            )

        def body(t, carry):
            self.core_copy(a, t).wait_send()
            return carry

        lax.fori_loop(0, 4, body, 0)

    def out_copy(self, a):
        shard, dst = self.arrays[a][0], self.arrays[a][4]
        return pltpu.make_async_copy(self.out.at[a % 2, pl.ds(0, shard)], dst, self.out_sem.at[a % 2])

    def add_two(self, a):
        half = self.arrays[a][0] // 2
        piece = 48
        for side in range(2):
            self.copies[a][2, side].wait_recv()
            ref = self.block(a, 2 * self.y + self.x, self.c, side * half, half)

            def body(i, carry, side=side, ref=ref):
                at = rows_at(i * piece, piece)
                to = rows_at(side * half + i * piece, piece)
                self.out[a % 2, to] = ref[at].astype(F32) + self.two[a % 2, side, at].astype(F32)
                return carry

            lax.fori_loop(0, half // piece, body, 0)
        self.out_copy(a).start()
        for k in range(4):
            self.copies[a][1, k].wait_send()

    def retire(self, a):
        for k in range(2):
            self.copies[a][2, k].wait_send()
        self.out_copy(a).wait()

    def step(self, between=None):
        s, count = self.now, len(self.arrays)
        self.now += 1
        for lag, stage in ((4, self.retire), (3, self.add_two), (2, self.add_one), (1, self.add_core)):
            if 0 <= s - lag < count:
                stage(s - lag)
        if s < count:
            self.compute(s, between or (lambda t: None))


def block_kernel(
    n,
    dp,
    tokens,
    context,
    cotangent,
    tables,
    counts,
    vec,
    s_qkv,
    s_small,
    s_ckv,
    s_out,
    s_in,
    w_qkv,
    w_out,
    w_in,
    o_h1,
    o_p,
    o_mixed,
    o_gt,
    o_gg,
    o_out,
    o_in,
    o_mid,
    o_ckv,
    o_last,
    v_vec,
    gv,
    win,
    wout,
    wsmall,
    h2,
    h3,
    dy,
    hid,
    dgu,
    dx2r,
    dx1r,
    x1,
    x2,
    dx,
    q,
    k,
    v,
    so,
    co,
    cq,
    dco,
    dcq,
    dso,
    dqkv,
    tkv,
    dtkv,
    pc,
    pst,
    dk,
    dv,
    ctx,
    tab,
    cnt,
    gg,
    own,
    got,
    krv,
    tst,
    trv,
    s_got,
    s_one,
    s_two,
    s_out_v,
    ggs,
    ggr,
    ggz,
    ggo,
    g_send,
    g_recv,
    g_local,
    e_send,
    e_recv,
    f_send,
    f_recv,
    k_send,
    k_recv,
    fs,
    fr,
    bs,
    br,
    p_sem,
    c_send,
    c_recv,
    a_send,
    a_recv,
    b_send,
    b_recv,
    s_sem,
    v_send,
    v_recv,
    moves,
):
    d = lax.axis_index("dp")
    z = lax.axis_index("mp")
    rows, width = tokens.shape
    group = rows // 2
    cols = so.shape[1]
    units = hid.shape[1]
    pairs = cols // 128
    half = lax.rem(d, 2)
    core = (jnp.bitwise_xor(d, 1), z)
    tok, mixed, gt, h1 = dy, dy, dx2r, hid
    v_qkv = win.at[:, pl.ds(0, 3 * cols)]
    v_ckv = wout.at[pl.ds(0, s_ckv.shape[0] * dp), pl.ds(0, 2 * cols)]
    mv = Moves(moves)
    ld_tok = mv.start(tokens, tok)
    ld_small = [mv.start(a, b) for a, b in ((context, ctx), (tables, tab), (counts, cnt))]
    ld_vec = mv.start(vec, v_vec.at[d])
    greet_all(d, z, n, dp)
    vec_copies = []
    for j in range(1, dp):
        peer = (jnp.bitwise_xor(d, j), z)
        cp = send(vec, v_vec.at[d], e_send.at[j], e_recv.at[j], peer)
        cp.start()
        vec_copies.append(cp)
    gathers = [
        Gather(d, z, shard_ref, full, g_send, g_recv, g_local, a)
        for a, (shard_ref, full) in enumerate(
            ((s_qkv, v_qkv), (s_ckv, v_ckv), (s_small, wsmall), (s_out, w_out), (s_in, w_in))
        )
    ]
    g_qkv, g_ckv, g_small, g_out, g_in = gathers
    g_qkv.begin()
    gg[...] = jnp.zeros_like(gg)
    dtkv[...] = jnp.zeros_like(dtkv)

    def clear(i, carry):
        at = rows_at(i * NR, NR)
        dk[at] = jnp.zeros((NR, cols), F32)
        dv[at] = jnp.zeros((NR, cols), F32)
        return carry

    ld_tok.wait()
    ld_vec.wait()
    for j in range(1, dp):
        b = jnp.bitwise_xor(d, j)
        send(v_vec.at[b], v_vec.at[b], e_send.at[j], e_recv.at[j], (b, z)).wait_recv()
    shard = width // dp
    for b in range(dp):
        gv[:, b * shard : (b + 1) * shard] = v_vec[b][:8, :shard].astype(F32)

    def norm_rows(i, carry):
        at = rows_at(i * NR, NR)
        h1[at] = (normal(tok[at].astype(F32))[0] * gv[0:1]).astype(BF)
        return carry

    lax.fori_loop(0, rows // NR // 2, norm_rows, 0)
    g_qkv.near()
    g_ckv.begin()
    g_small.begin()
    lax.fori_loop(rows // NR // 2, rows // NR, norm_rows, 0)
    st_h1 = mv.start(h1, o_h1)
    lax.fori_loop(0, 2 * rows // NR, clear, 0)
    for ld in ld_small:
        ld.wait()
    lane = lax.broadcasted_iota(jnp.int32, (1, 128), 1)
    clip = d // 2
    frames = jnp.sum(jnp.where(lane == clip, cnt[0:1], 0.0), axis=1, keepdims=True)
    texts = jnp.sum(jnp.where(lane == clip, cnt[1:2], 0.0), axis=1, keepdims=True)
    key_at = lax.broadcasted_iota(jnp.int32, (1, 2 * rows), 1).astype(F32)
    text = ctx.shape[0]
    text_at = lax.broadcasted_iota(jnp.int32, (1, 2 * text), 1).astype(F32)
    key_bias = jnp.where(key_at <= frames, 0.0, -1e30)
    text_bias = jnp.where(text_at < texts, 0.0, -1e30)
    g_qkv.far()
    g_qkv.last()
    my_rows = half * rows

    def project(g, carry):
        at = rows_at(g * group, group)
        mine = rows_at(my_rows + g * group, group)
        x = h1[at]
        for part in (1, 2, 0):
            u = dot_nn(x, win[:, part * cols : (part + 1) * cols])
            if part == 2:
                v[mine] = u.astype(BF)
                continue
            for j in range(pairs):
                r = turn(u[:, j * 128 : (j + 1) * 128], tab[0, at], tab[1, at], tab[2, at])
                if part:
                    k[mine, j * 128 : (j + 1) * 128] = r.astype(BF)
                else:
                    q[at, j * 128 : (j + 1) * 128] = (r * HD ** (-0.5)).astype(BF)
        return carry

    lax.fori_loop(0, 2, project, 0)
    mine, theirs = rows_at(my_rows, rows), rows_at((1 - half) * rows, rows)
    kv = [send(r.at[mine], r.at[mine], f_send.at[i], f_recv.at[i], core) for i, r in enumerate((k, v))]
    for cp in kv:
        cp.start()
    st_qkv = mv.start(v_qkv, w_qkv)
    g_ckv.near()
    g_small.near()
    g_out.begin()
    g_ckv.far()
    g_ckv.last()
    g_small.far()
    g_in.begin()
    t_mine, t_theirs = rows_at(half * text, text), rows_at((1 - half) * text, text)
    tkv[t_mine] = dot_nn(ctx[...], v_ckv[...]).astype(BF)
    kv.append(send(tkv.at[t_mine], tkv.at[t_mine], f_send.at[2], f_recv.at[2], core))
    kv[2].start()
    for i, r in enumerate((k, v)):
        send(r.at[theirs], r.at[theirs], f_send.at[i], f_recv.at[i], core).wait_recv()

    tile = 256

    def feed(g, lo, count, between):
        at = rows_at(g * group, group)

        def step(i, carry):
            u = pl.multiple_of(i * tile, tile)
            us, ups = pl.ds(u, tile), pl.ds(pl.multiple_of(units + u, tile), tile)
            x = h3[at]
            gate = dot_nn(x, win[:, us]) + gv[3:4, us]
            up = dot_nn(x, win[:, ups]) + gv[4:5, us]
            dh = dot_nn(dy[at], wout[:, us])
            sig = jax.nn.sigmoid(gate)
            act = gate * sig
            hid[at, us] = (act * up).astype(BF)
            d_gate = (dh * up * (sig * (1.0 + gate * (1.0 - sig)))).astype(BF)
            d_up = (dh * act).astype(BF)
            dgu[at, us] = d_gate
            dgu[at, ups] = d_up
            gg[3:4, us] += jnp.sum(d_gate.astype(F32), axis=0, keepdims=True)
            gg[4:5, us] += jnp.sum(d_up.astype(F32), axis=0, keepdims=True)
            between(i - lo)
            return carry

        lax.fori_loop(lo, lo + count, step, 0)

    def norm_back(x, dn, gain, row):
        nrm, r = normal(x)
        gg[row : row + 1] += jnp.sum(dn * nrm, axis=0, keepdims=True)
        e = dn * gain
        return r * (
            e
            - jnp.mean(e, axis=-1, keepdims=True)
            - nrm * jnp.mean(e * nrm, axis=-1, keepdims=True)
        )

    def places(g, lo):
        return rows_at(g * group + lo, CH), rows_at(
            g * group // 2 + lax.rem(lo, group // 2), CH
        )

    def start_two(g):
        def fin(lo, total):
            at, mine = places(g, lo)
            x = tok[at].astype(F32) + total
            x1[mine] = x
            h2[at] = (normal(x)[0] * gv[1:2]).astype(BF)

        return fin

    def start_three(g):
        def fin(lo, total):
            at, mine = places(g, lo)
            x = x1[mine] + total
            x2[mine] = x
            h3[at] = (normal(x)[0] * gv[2:3]).astype(BF)

        return fin

    def finish_mixed(g):
        def fin(lo, total):
            at, mine = places(g, lo)
            mixed[at] = (x2[mine] + total + gv[5:6]).astype(BF)

        return fin

    def finish_three(g):
        def fin(lo, total):
            at, mine = places(g, lo)
            x = dy[at].astype(F32) + norm_back(x2[mine], total, gv[2:3], 2)
            dx[mine] = x
            dx2r[at] = x.astype(BF)

        return fin

    def finish_two(g):
        def fin(lo, total):
            at, mine = places(g, lo)
            x = dx[mine] + norm_back(x1[mine], total, gv[1:2], 1)
            dx[mine] = x
            dx1r[at] = x.astype(BF)

        return fin

    def finish_one(g):
        def fin(lo, total):
            at, mine = places(g, lo)
            x = dx[mine] + norm_back(h3[at].astype(F32), total, gv[0:1], 0)
            gt[at] = x.astype(BF)

        return fin

    sems = (fs, fr, bs, br)

    def lines(dst, slot, index, fin):
        return [
            Line(
                d, z, n, own.at[slot + g], got.at[slot + g], dst, g * group, sems, index + g, fin(g)
            )
            for g in range(2)
        ]

    fore_one = lines(h2, 0, 0, start_two)
    fore_two = lines(h3, 2, 2, start_three)
    mix = lines(mixed, 2, 4, finish_mixed)
    three = lines(dx2r, 0, 6, finish_three)
    two = lines(dx1r, 0, 8, finish_two)
    one = lines(gt, 0, 10, finish_one)

    def quiet(i):
        pass

    def with_lines(total, every, *ls):
        ls = [line for line in ls if line.next < line.slots]
        starts = [line.next for line in ls]

        def between(i):
            def go():
                for line, s in zip(ls, starts):
                    line.slot(s + i // every)

            if every == 1:
                go()
            else:
                pl.when(lax.rem(i, every) == 0)(go)

        for line in ls:
            line.next += -(-total // every)
        return between

    tiles = units // tile
    pieces = 2
    per = tiles // pieces
    piece = units // pieces

    sc = Scatter(
        d, z, s_got, s_one, s_two, s_out_v, ((c_send, c_recv), (a_send, a_recv), (b_send, b_recv)), s_sem
    )
    wide = s_got.shape[-1]

    def part_of(buf, lane, size, *terms):
        def tile_at(t):
            at = rows_at(t * 2 * size, 2 * size)
            to = lane
            for left, right, lo, count in terms:
                cols_at = pl.ds(pl.multiple_of(t * 2 * size, 128), 2 * size)
                buf[at, to : to + count] = dot_tn(left[:, cols_at], right[:, lo : lo + count]).astype(BF)
                to += count

        return tile_at

    def add_array(buf, lane, dst, *terms):
        sc.add(
            shard,
            buf,
            lambda j: (j * 2 * shard, lane),
            part_of(buf, lane, shard, *terms),
            dst,
        )

    def text_tile(j):
        left = ctx[...]
        t = text_width // 4
        g = dot_tn(left, tst[...]).astype(BF)
        for i in range(4):

            @pl.when(j == i)
            def _():
                dgu[0:t, i * wide : (i + 1) * wide] = g[i * t : (i + 1) * t]

    text_width = ctx.shape[1]
    for i in range(2):
        add_array(wout, i * wide, o_out.at[:, pl.ds(i * wide, wide)], (dy, hid, i * wide, wide))
    for i in range(4):
        add_array(win, i * wide, o_in.at[:, pl.ds(i * wide, wide)], (h3, dgu, i * wide, wide))
    add_array(wout, 0, o_mid, (dx2r, co, 0, cols), (h2, dcq, 0, cols))
    sc.add(text_width // dp, dgu, lambda j: (0, j * wide), text_tile, o_ckv)
    add_array(wout, wide, o_last.at[:, pl.ds(0, wide)], (dx1r, so, 0, cols), (hid, dqkv, 0, cols))
    add_array(win, 2 * wide, o_last.at[:, pl.ds(wide, wide)], (hid, dqkv, cols, wide))

    def attend(g, queries, keys, key_lo, values, value_lo, bias, save, out, between):
        at = rows_at(g * group, group)

        def head(h, carry):
            j, e = h // 2, lax.rem(h, 2)
            lo = pl.multiple_of(j * 128, 128)
            mask = half_mask(group, e)
            qb = jnp.where(mask, queries[at, pl.ds(lo, 128)], jnp.zeros((), BF))
            s = dot_nt(qb, keys[:, pl.ds(pl.multiple_of(key_lo + lo, 128), 128)]) + bias
            p = softmax(s).astype(BF)
            save(h, p)
            o = dot_nn(p, values[:, pl.ds(pl.multiple_of(value_lo + lo, 128), 128)])
            out[at, pl.ds(lo, 128)] = jnp.where(mask, o.astype(BF), out[at, pl.ds(lo, 128)])
            between(h)
            return carry

        lax.fori_loop(0, 2 * pairs, head, 0)

    def self_forward(g, between):
        at = rows_at(g * group, group)

        def keep(h):
            slot = lax.rem(h, 2)
            return pltpu.make_async_copy(pst.at[slot], o_p.at[h, at], p_sem.at[slot])

        def save(h, p):
            @pl.when(h >= 2)
            def _():
                keep(h - 2).wait()

            pst[lax.rem(h, 2)] = p
            keep(h).start()

        attend(g, q, k, 0, v, 0, key_bias, save, so, between)
        for h in (2 * pairs - 2, 2 * pairs - 1):
            keep(h).wait()
        own[g] = dot_nt(so[at], wsmall[:, 0:cols]).astype(BF)

    def cross_forward(g, between):
        at = rows_at(g * group, group)
        cq[at] = dot_nn(h2[at], wsmall[:, cols : 2 * cols]).astype(BF) * jnp.asarray(HD ** (-0.5), BF)

        def save(h, p):
            pc[h, at] = p

        attend(g, cq, tkv, 0, tkv, cols, text_bias, save, co, between)
        own[2 + g] = dot_nt(co[at], wsmall[:, 2 * cols :]).astype(BF)

    def attend_back(g, d_out, queries, keys, key_lo, values, value_lo, probs, dkr, dk_lo, dvr, dv_lo, dq, between):
        at = rows_at(g * group, group)

        def head(h, carry):
            j, e = h // 2, lax.rem(h, 2)
            lo = pl.multiple_of(j * 128, 128)
            here = pl.ds(lo, 128)
            mask = half_mask(group, e)
            zero = jnp.zeros((), BF)
            do = jnp.where(mask, d_out[at, here], zero)
            qb = jnp.where(mask, queries[at, here], zero)
            p = probs(h)
            pf = p.astype(F32)
            dp_ = dot_nt(do, values[:, pl.ds(pl.multiple_of(value_lo + lo, 128), 128)])
            ds = (pf * (dp_ - jnp.sum(pf * dp_, axis=-1, keepdims=True))).astype(BF)
            g_q = dot_nn(ds, keys[:, pl.ds(pl.multiple_of(key_lo + lo, 128), 128)]) * HD ** (-0.5)
            dkr[:, pl.ds(pl.multiple_of(dk_lo + lo, 128), 128)] += dot_tn(ds, qb)
            dvr[:, pl.ds(pl.multiple_of(dv_lo + lo, 128), 128)] += dot_tn(p, do)
            dq(h, at, here, mask, g_q)
            between(h)
            return carry

        lax.fori_loop(0, 2 * pairs, head, 0)

    def cross_back(g, between):
        at = rows_at(g * group, group)
        dco[at] = dot_nn(dx2r[at], wsmall[:, 2 * cols :]).astype(BF)

        def dq(h, at, here, mask, g_q):
            dcq[at, here] = jnp.where(mask, g_q.astype(BF), dcq[at, here])

        attend_back(
            g, dco, cq, tkv, 0, tkv, cols, lambda h: pc[h, at], dtkv, 0, dtkv, cols, dq, between
        )

    def self_back(g, between):
        at = rows_at(g * group, group)

        def load(h):
            slot = lax.rem(h, 2)
            return pltpu.make_async_copy(o_p.at[h, at], pst.at[slot], p_sem.at[slot])

        load(0).start()
        dso[at] = dot_nn(dx1r[at], wsmall[:, 0:cols]).astype(BF)

        def probs(h):
            @pl.when(h + 1 < 2 * pairs)
            def _():
                load(h + 1).start()

            load(h).wait()
            return pst[lax.rem(h, 2)]

        def dq(h, at, here, mask, g_q):
            r = turn(g_q, tab[0, at], -tab[1, at], -tab[2, at]).astype(BF)
            dqkv[at, here] = jnp.where(mask, r, dqkv[at, here])

        attend_back(g, dso, q, k, 0, v, 0, probs, dk, 0, dv, 0, dq, between)

    def three_part(g):
        at = rows_at(g * group, group)
        own[g] = dot_nt(dgu[at], win[...]).astype(BF)

    def down_part(g):
        at = rows_at(g * group, group)
        own[2 + g] = dot_nt(hid[at], wout[...]).astype(BF)

    def two_part(g):
        at = rows_at(g * group, group)
        own[g] = dot_nt(dcq[at], wsmall[:, cols : 2 * cols]).astype(BF)

    def one_part(g):
        at = rows_at(g * group, group)
        own[g] = dot_nt(dqkv[at], win[:, 0 : 3 * cols]).astype(BF)

    g_small.last()
    self_forward(0, quiet)
    self_forward(1, with_lines(6, 1, fore_one[0]))
    run(2, fore_one[0])
    run(fore_one[0].left(), fore_one[0], fore_one[1])
    send(tkv.at[t_theirs], tkv.at[t_theirs], f_send.at[2], f_recv.at[2], core).wait_recv()
    cross_forward(0, with_lines(6, 6, fore_one[1]))
    g_out.near()
    g_in.near()
    run(fore_one[1].left(), fore_one[1], fore_two[0])
    ld_dy = mv.start(cotangent, dy)
    cross_forward(1, with_lines(6, 2, fore_two[0]))
    run(5, fore_two[0], fore_two[1])
    g_out.far()
    g_in.far()
    st_qkv.wait()
    run(6, fore_two[0], fore_two[1])
    g_out.last()
    g_in.last()
    g_qkv.drain()
    g_ckv.drain()
    w_loads = []
    for i in range(pieces):
        at = slice(i * piece, (i + 1) * piece)
        up = slice(units + i * piece, units + (i + 1) * piece)
        w_loads.append(
            [
                mv.start(w_in.at[:, at], win.at[:, at]),
                mv.start(w_in.at[:, up], win.at[:, up]),
                mv.start(w_out.at[:, at], wout.at[:, at]),
            ]
        )
    run(fore_two[0].left(), fore_two[0], fore_two[1])
    ld_dy.wait()
    st_h1.wait()

    def bias_sum(i, carry):
        gg[5:6] += jnp.sum(dy[rows_at(i * NR, NR)].astype(F32), axis=0, keepdims=True)
        return carry

    for i in range(pieces):
        for cp in w_loads[i]:
            cp.wait()
        feed(0, i * per, per, with_lines(per, 1, fore_two[1]))
    fore_one[0].drain()
    three_part(0)
    run(fore_two[1].left(), fore_two[1], three[0])
    lax.fori_loop(0, rows // NR, bias_sum, 0)
    for line in (fore_one[1], fore_two[0], fore_two[1]):
        line.drain()
    feed(1, 0, tiles, with_lines(tiles, 1, three[0]))
    three_part(1)
    down_part(0)
    run(2, three[0], three[1])
    down_part(1)
    run(2, three[0], three[1])
    sc.step(with_lines(4, 1, three[0], three[1]))
    sc.step(with_lines(4, 1, three[0], three[1]))
    ld_h1 = mv.start(o_h1, hid)
    run(three[0].left(), three[0], three[1])
    cross_back(0, with_lines(6, 2, three[1]))
    three[0].drain()
    two_part(0)
    sc.step(with_lines(4, 1, three[1], two[0]))
    run(three[1].left(), three[1], two[0])
    cross_back(1, with_lines(6, 1, two[0]))
    three[1].drain()
    two_part(1)
    tst[...] = dtkv[t_theirs].astype(BF)
    t_copy = send(tst, trv, k_send.at[2], k_recv.at[2], core)
    t_copy.start()
    sc.step(with_lines(4, 1, two[0], two[1]))
    sc.step(with_lines(4, 1, two[0], two[1]))
    run(two[0].left(), two[0], two[1])
    self_back(0, with_lines(6, 1, two[1], mix[0]))
    two[0].drain()
    sc.step(with_lines(4, 1, two[1], mix[0]))
    ld_tok = mv.start(tokens, h3)
    run(two[1].left(), two[1])
    sc.step(with_lines(4, 1, mix[0], mix[1]))
    self_back(1, with_lines(6, 1, mix[0], mix[1]))
    two[1].drain()
    dco[...] = dk[theirs].astype(BF)
    k_copy = send(dco, krv.at[0], k_send.at[0], k_recv.at[0], core)
    k_copy.start()
    dcq[...] = dv[theirs].astype(BF)
    v_copy = send(dcq, krv.at[1], k_send.at[1], k_recv.at[1], core)
    v_copy.start()
    t_copy.wait()
    tst[...] = (dtkv[t_mine] + trv[...].astype(F32)).astype(BF)
    sc.step(with_lines(4, 1, mix[0], mix[1]))
    ld_qkv = mv.start(w_qkv, win.at[:, pl.ds(0, 3 * cols)])
    k_copy.wait_recv()
    ld_h1.wait()
    ld_tok.wait()
    for g in range(2):
        at = slice(g * group, (g + 1) * group)
        own_at = rows_at(half * rows + g * group, group)
        for j in range(pairs):
            here = slice(j * 128, (j + 1) * 128)
            u = dk[own_at, here] + krv[0, at, here].astype(F32)
            dqkv[at, cols + j * 128 : cols + (j + 1) * 128] = turn(
                u, tab[0, at], -tab[1, at], -tab[2, at]
            ).astype(BF)
        if g == 0:
            v_copy.wait_recv()
        dqkv[at, 2 * cols :] = (dv[own_at] + krv[1, at].astype(F32)).astype(BF)
        if g == 0:
            ld_qkv.wait()
        one_part(g)
        if g == 0:
            run(8, one[0], mix[0], mix[1])
    sc.step(with_lines(4, 1, one[0], one[1], mix[0], mix[1]))
    sc.step(with_lines(4, 1, one[0], one[1], mix[0], mix[1]))
    run(2, one[0], one[1], mix[0], mix[1])
    sc.step()
    run(2, one[0], one[1], mix[0], mix[1])
    sc.step()
    run(max(one[1].left(), mix[0].left(), mix[1].left()), one[0], one[1], mix[0], mix[1])
    st = [mv.start(mixed, o_mixed), mv.start(gt, o_gt)]
    ggs[...] = jnp.zeros_like(ggs)
    for b in range(dp):
        ggs[b, :, 0:shard] = gg[:, b * shard : (b + 1) * shard]
    sums = []
    for b in range(1, dp):
        to = jnp.bitwise_xor(d, b)
        cp = send(ggs.at[to], ggr.at[b], v_send.at[b], v_recv.at[b], (to, z))
        cp.start()
        sums.append(cp)
    sc.step()
    total = ggs[d]
    for b, cp in enumerate(sums):
        cp.wait_recv()
        total = total + ggr[b + 1]
    ggo[...] = total
    line_sums = []
    for j in range(1, n):
        cp = send(
            ggo, ggz.at[j], v_send.at[dp + j - 1], v_recv.at[dp + j - 1], (d, lax.rem(z + j, n))
        )
        cp.start()
        line_sums.append(cp)
    sc.step()
    for j, cp in enumerate(line_sums):
        cp.wait_recv()
        total = total + ggz[j + 1]
    ggz[0, 0:3] = total[0:3]
    ggz[0, 3:8] = ggo[3:8]
    st.append(mv.start(ggz.at[0], o_gg))
    for cp in sums + line_sums + [k_copy, v_copy] + kv + vec_copies:
        cp.wait_send()
    for g in (g_small, g_out, g_in):
        g.drain()
    for line in mix + one:
        line.drain()
    for cp in st:
        cp.wait()


def run_block(n, dp, tokens, context, cotangent, tables, counts, vec, s_qkv, s_small, s_ckv, s_out, s_in):
    rows, width = tokens.shape
    cols = s_qkv.shape[1] // 3
    units = s_out.shape[1]
    heads = cols // HD
    text, text_width = context.shape
    shard = width // dp
    half_rows = rows // 2
    sds = jax.ShapeDtypeStruct
    outs = [
        sds((width, 3 * cols), BF),
        sds((width, units), BF),
        sds((width, 2 * units), BF),
        sds((rows, width), BF),
        sds((heads, rows, 2 * rows), BF),
        sds((rows, width), BF),
        sds((rows, width), BF),
        sds((8, 256), F32),
        sds((shard, units), F32),
        sds((shard, 2 * units), F32),
        sds((shard, 2 * cols), F32),
        sds((text_width // dp, 2 * cols), F32),
        sds((shard, 4 * cols), F32),
    ]
    vm = pltpu.VMEM
    chunks = rows // 4 // CH
    full, head, own_x = vm((rows, width), BF), vm((rows, cols), BF), vm((half_rows, width), F32)
    keys = vm((2 * rows, cols), BF)
    scratch = [
        vm((dp,) + vec.shape, BF),
        vm((8, width), F32),
        vm((width, 2 * units), BF),
        vm((width, units), BF),
        vm((width, 3 * cols), BF),
        full,
        full,
        full,
        vm((rows, units), BF),
        vm((rows, 2 * units), BF),
        full,
        full,
        own_x,
        own_x,
        own_x,
        head,
        keys,
        keys,
        head,
        head,
        head,
        head,
        head,
        head,
        vm((rows, 3 * cols), BF),
        vm((2 * text, 2 * cols), BF),
        vm((2 * text, 2 * cols), F32),
        vm((heads, rows, 2 * text), BF),
        vm((2, half_rows, 2 * rows), BF),
        vm((2 * rows, cols), F32),
        vm((2 * rows, cols), F32),
        vm(context.shape, BF),
        vm(tables.shape, F32),
        vm(counts.shape, F32),
        vm((8, width), F32),
        vm((4, half_rows, width), BF),
        vm((4, half_rows, width), BF),
        vm((2, rows, cols), BF),
        vm((text, 2 * cols), BF),
        vm((text, 2 * cols), BF),
        vm((2, 4, shard, 2 * cols), BF),
        vm((2, 2, 2, shard // 2, 2 * cols), BF),
        vm((2, 2, shard // 2, 2 * cols), BF),
        vm((2, shard, 2 * cols), F32),
        vm((dp, 8, 256), F32),
        vm((dp, 8, 256), F32),
        vm((n, 8, 256), F32),
        vm((8, 256), F32),
        DMA((5, 9)),
        DMA((5, 9)),
        DMA((5,)),
        DMA((dp,)),
        DMA((dp,)),
        DMA((3,)),
        DMA((3,)),
        DMA((3,)),
        DMA((3,)),
        *[DMA((12, 2, chunks))] * 4,
        DMA((2,)),
        DMA((2, 4)),
        DMA((2, 4)),
        DMA((2, 4)),
        DMA((2, 4)),
        DMA((2, 2)),
        DMA((2, 2)),
        DMA((2,)),
        DMA((dp + n - 1,)),
        DMA((dp + n - 1,)),
        DMA((32,)),
    ]
    ins = (tokens, context, cotangent, tables, counts, vec, s_qkv, s_small, s_ckv, s_out, s_in)
    return pl.pallas_call(
        functools.partial(block_kernel, n, dp),
        out_shape=outs,
        in_specs=[HBM] * len(ins),
        out_specs=[HBM] * len(outs),
        scratch_shapes=scratch,
        compiler_params=pltpu.CompilerParams(
            collective_id=0, has_side_effects=True, vmem_limit_bytes=63 * 2**20
        ),
        name="block",
    )(*ins)[5:]


def prepare(tokens, context, frame_counts, text_counts, w_qkv, w_attn_out, w_cross_q, w_cross_kv, w_cross_out, w_in, w_out, norm_gains, b_in, b_out):
    shard, _, cols = w_qkv.shape
    rows = tokens.shape[0]
    vec = jnp.concatenate([norm_gains, b_in, b_out[None]], axis=0)
    vec = jnp.pad(vec, ((0, 16 - vec.shape[0]), (0, 256 - shard)))
    d = lax.axis_index("dp")
    half = d % 2
    counts = jnp.stack([frame_counts, text_counts]).astype(F32)
    counts = jnp.pad(counts, ((0, 6), (0, 128 - counts.shape[1])))
    m = HD // 4
    lane = jnp.arange(128) % HD
    frequency = 10000.0 ** (-(lane % m).astype(F32) / m)
    angle = (half * rows + jnp.arange(rows)).astype(F32)[:, None] * frequency[None]
    sine = jnp.sin(angle)
    tables = jnp.stack(
        [
            jnp.where(lane < 2 * m, jnp.cos(angle), 1.0),
            jnp.where(lane < m, -sine, 0.0),
            jnp.where((lane >= m) & (lane < 2 * m), sine, 0.0),
        ]
    )
    return (
        tables,
        counts,
        vec,
        w_qkv.reshape(shard, 3 * cols),
        jnp.concatenate([w_attn_out.T, w_cross_q, w_cross_out.T], axis=1),
        w_cross_kv.reshape(w_cross_kv.shape[0], 2 * cols),
        w_out.T,
        w_in.reshape(shard, -1),
    )


def from_partner(block, axis, stride):
    count = lax.axis_size(axis)
    route = []
    for low in range(count):
        high = low | 1 << stride
        if high != low and high < count:
            route += [(low, high), (high, low)]
    return lax.ppermute(block, axis, route)


def layer_norm(values, gain_row):
    centered = values - jnp.mean(values, axis=-1, keepdims=True)
    spread = jnp.mean(centered * centered, axis=-1, keepdims=True)
    return centered * lax.rsqrt(spread + epsilon) * gain_row


def rotate(tensor, positions):
    quarter = tensor.shape[-1] // 4
    frequency = 10000.0 ** (-jnp.arange(quarter, dtype=jnp.float32) / quarter)
    angles = positions[:, None] * frequency[None, :]
    cosine = jnp.cos(angles)[:, None, :]
    sine_part = jnp.sin(angles)[:, None, :]
    first_part = tensor[..., :quarter]
    second = tensor[..., quarter : 2 * quarter]
    return jnp.concatenate(
        [
            first_part * cosine - second * sine_part,
            second * cosine + first_part * sine_part,
            tensor[..., 2 * quarter :],
        ],
        axis=-1,
    )


def gated_unit(both):
    gate = both[:, 0]
    return gate * jax.nn.sigmoid(gate) * both[:, 1]


def in_order(own_part, other_part, which_half):
    lower_first = jnp.concatenate([own_part, other_part], axis=0)
    upper_first = jnp.concatenate([other_part, own_part], axis=0)
    return jnp.where(which_half == 0, lower_first, upper_first)


def own_rows(whole, which_half, row_count):
    return lax.dynamic_slice_in_dim(whole, which_half * row_count, row_count, 0)


def partner_rows(whole, which_half, row_count):
    return lax.dynamic_slice_in_dim(whole, (1 - which_half) * row_count, row_count, 0)


def masked_scores(query_block, key_all, key_live):
    scale = query_block.shape[-1] ** (-0.5)
    raw_scores = (
        jnp.einsum("qhd,khd->hqk", query_block, key_all, preferred_element_type=jnp.float32) * scale
    )
    return jnp.where(key_live[None, None, :], raw_scores, -1e30)


def attend_forward(queries, key_all, value_all, key_live):
    row_count, head_count, head_size = queries.shape
    block_rows = min(512, row_count)
    blocks = queries.reshape(row_count // block_rows, block_rows, head_count, head_size)

    def per_block(query_block):
        scores = masked_scores(query_block, key_all, key_live)
        row_max = jnp.max(scores, axis=-1, keepdims=True)
        weights = jnp.exp(scores - row_max)
        row_total = jnp.sum(weights, axis=-1, keepdims=True)
        attn_probs = weights / row_total
        block_out = jnp.einsum(
            "hqk,khd->qhd",
            attn_probs.astype(jnp.bfloat16),
            value_all,
            preferred_element_type=jnp.float32,
        )
        return (block_out, row_max + jnp.log(row_total))

    outputs, log_sums = lax.map(per_block, blocks)
    return (outputs.reshape(row_count, head_count, head_size), log_sums)


def attend_backward(queries, key_all, value_all, key_live, log_sums, grad_out):
    row_count, head_count, head_size = queries.shape
    block_rows = min(512, row_count)
    block_shape = (row_count // block_rows, block_rows, head_count, head_size)
    scale = head_size ** (-0.5)

    def per_block(running, block_item):
        query_block, grad_block, lse_block = block_item
        attn_probs = jnp.exp(masked_scores(query_block, key_all, key_live) - lse_block)
        grad_probs = jnp.einsum(
            "qhd,khd->hqk", grad_block, value_all, preferred_element_type=jnp.float32
        )
        row_inner = jnp.sum(attn_probs * grad_probs, axis=-1, keepdims=True)
        grad_scores = (attn_probs * (grad_probs - row_inner)).astype(jnp.bfloat16)
        grad_query = (
            jnp.einsum("hqk,khd->qhd", grad_scores, key_all, preferred_element_type=jnp.float32)
            * scale
        )
        grad_key = (
            running[0]
            + jnp.einsum(
                "hqk,qhd->khd", grad_scores, query_block, preferred_element_type=jnp.float32
            )
            * scale
        )
        grad_value = running[1] + jnp.einsum(
            "hqk,qhd->khd",
            attn_probs.astype(jnp.bfloat16),
            grad_block,
            preferred_element_type=jnp.float32,
        )
        return ((grad_key, grad_value), grad_query)

    zero_keys = jnp.zeros(key_all.shape, jnp.float32)
    (grad_key, grad_value), grad_query = lax.scan(
        per_block,
        (zero_keys, zero_keys),
        (queries.reshape(block_shape), grad_out.reshape(block_shape), log_sums),
    )
    return (grad_query.reshape(row_count, head_count, head_size), grad_key, grad_value)


def branch_total(partial_sum):
    return lax.psum(partial_sum, "mp")


def grad_total(partial_sum):
    return lax.psum(partial_sum, "mp")


def body(
    tokens,
    context,
    frame_counts,
    text_counts,
    w_qkv,
    w_attn_out,
    w_cross_q,
    w_cross_kv,
    w_cross_out,
    w_in,
    w_out,
    norm_gains,
    b_in,
    b_out,
    cotangent,
):
    gathered = (
        lax.all_gather(w_qkv, "dp", axis=0, tiled=True),
        lax.all_gather(w_attn_out, "dp", axis=1, tiled=True),
        lax.all_gather(w_cross_q, "dp", axis=0, tiled=True),
        lax.all_gather(w_cross_kv, "dp", axis=0, tiled=True),
        lax.all_gather(w_cross_out, "dp", axis=1, tiled=True),
        lax.all_gather(w_in, "dp", axis=0, tiled=True),
        lax.all_gather(w_out, "dp", axis=1, tiled=True),
        lax.all_gather(norm_gains, "dp", axis=1, tiled=True),
        lax.all_gather(b_in, "dp", axis=1, tiled=True),
        lax.all_gather(b_out, "dp", axis=0, tiled=True),
    )
    (
        qkv_full,
        attn_out_full,
        cross_q_full,
        cross_kv_full,
        cross_out_full,
        in_full,
        out_full,
        gains_full,
        b_in_full,
        b_out_full,
    ) = gathered
    row_count, model_width = tokens.shape
    text_rows, text_width = context.shape
    head_cols = qkv_full.shape[2]
    unit_cols = in_full.shape[2]
    head_count = head_cols // HD
    device_row = lax.axis_index("dp")
    which_half = device_row % 2
    clip_index = device_row // 2
    frame_live = lax.dynamic_index_in_dim(frame_counts, clip_index, 0, keepdims=False)
    text_live = lax.dynamic_index_in_dim(text_counts, clip_index, 0, keepdims=False)
    positions = (which_half * row_count + jnp.arange(row_count)).astype(jnp.float32)
    key_live = jnp.arange(2 * row_count) <= frame_live
    token_live = jnp.arange(2 * text_rows) < text_live
    gain_rows = gains_full.astype(jnp.float32)
    tokens_f = tokens.astype(jnp.float32)
    grad_y_mine = cotangent.astype(jnp.float32)
    norm_one, pull_one = jax.vjp(layer_norm, tokens_f, gain_rows[0])
    h_one = norm_one.astype(jnp.bfloat16)
    qkv = jnp.dot(
        h_one, qkv_full.reshape(model_width, 3 * head_cols), preferred_element_type=jnp.float32
    ).reshape(row_count, 3, head_count, HD)
    queries = rotate(qkv[:, 0], positions).astype(jnp.bfloat16)
    own_keys = rotate(qkv[:, 1], positions).astype(jnp.bfloat16).reshape(row_count, head_cols)
    own_values = qkv[:, 2].astype(jnp.bfloat16).reshape(row_count, head_cols)
    own_text = jnp.dot(
        context,
        cross_kv_full.reshape(text_width, 2 * head_cols),
        preferred_element_type=jnp.float32,
    ).astype(jnp.bfloat16)
    other = from_partner((own_keys, own_values, own_text), "dp", 0)
    key_all = in_order(own_keys, other[0], which_half).reshape(2 * row_count, head_count, HD)
    value_all = in_order(own_values, other[1], which_half).reshape(2 * row_count, head_count, HD)
    text_all = in_order(own_text, other[2], which_half).reshape(2 * text_rows, 2, head_count, HD)
    text_keys = text_all[:, 0]
    text_values = text_all[:, 1]
    self_attn, self_lse = attend_forward(queries, key_all, value_all, key_live)
    self_out = self_attn.reshape(row_count, head_cols).astype(jnp.bfloat16)
    self_part = jnp.dot(self_out, attn_out_full, preferred_element_type=jnp.float32)
    x_one = tokens_f + branch_total(self_part)
    norm_two, pull_two = jax.vjp(layer_norm, x_one, gain_rows[1])
    h_two = norm_two.astype(jnp.bfloat16)
    cross_queries = (
        jnp.dot(h_two, cross_q_full, preferred_element_type=jnp.float32)
        .astype(jnp.bfloat16)
        .reshape(row_count, head_count, HD)
    )
    cross_attn, cross_lse = attend_forward(cross_queries, text_keys, text_values, token_live)
    cross_out = cross_attn.reshape(row_count, head_cols).astype(jnp.bfloat16)
    cross_part = jnp.dot(cross_out, cross_out_full, preferred_element_type=jnp.float32)
    x_two = x_one + branch_total(cross_part)
    norm_three, pull_three = jax.vjp(layer_norm, x_two, gain_rows[2])
    h_three = norm_three.astype(jnp.bfloat16)
    both = jnp.dot(
        h_three, in_full.reshape(model_width, 2 * unit_cols), preferred_element_type=jnp.float32
    ).reshape(row_count, 2, unit_cols) + b_in_full.astype(jnp.float32)
    hidden_f, pull_unit = jax.vjp(gated_unit, both)
    hidden = hidden_f.astype(jnp.bfloat16)
    down_part = jnp.dot(hidden, out_full, preferred_element_type=jnp.float32)
    mixed = (x_two + branch_total(down_part) + b_out_full.astype(jnp.float32)).astype(jnp.bfloat16)
    again = (
        lax.all_gather(w_qkv, "dp", axis=0, tiled=True),
        lax.all_gather(w_attn_out, "dp", axis=1, tiled=True),
        lax.all_gather(w_cross_q, "dp", axis=0, tiled=True),
        lax.all_gather(w_cross_out, "dp", axis=1, tiled=True),
        lax.all_gather(w_in, "dp", axis=0, tiled=True),
        lax.all_gather(w_out, "dp", axis=1, tiled=True),
    )
    qkv_back = again[0]
    attn_out_back = again[1]
    cross_q_back = again[2]
    cross_out_back = again[3]
    in_back = again[4]
    out_back = again[5]
    grad_y = cotangent.astype(jnp.float32)
    grad_out_w = jnp.dot(hidden.T, cotangent, preferred_element_type=jnp.float32)
    grad_b_out = jnp.sum(grad_y, axis=0)
    grad_hidden = jnp.dot(cotangent, out_back.T, preferred_element_type=jnp.float32)
    grad_both = pull_unit(grad_hidden)[0].astype(jnp.bfloat16).reshape(row_count, 2 * unit_cols)
    grad_b_in = jnp.sum(grad_both, axis=0, dtype=jnp.float32).reshape(2, unit_cols)
    grad_in_w = jnp.dot(h_three.T, grad_both, preferred_element_type=jnp.float32).reshape(
        model_width, 2, unit_cols
    )
    three_part = jnp.dot(
        grad_both, in_back.reshape(model_width, 2 * unit_cols).T, preferred_element_type=jnp.float32
    )
    grad_x_norm, grad_gain_three = pull_three(grad_total(three_part))
    grad_x_two = grad_y_mine + grad_x_norm
    grad_two_b = grad_x_two.astype(jnp.bfloat16)
    grad_cross_out_w = jnp.dot(cross_out.T, grad_two_b, preferred_element_type=jnp.float32)
    grad_cross = (
        jnp.dot(grad_two_b, cross_out_back.T, preferred_element_type=jnp.float32)
        .astype(jnp.bfloat16)
        .reshape(row_count, head_count, HD)
    )
    grad_cq, grad_text_key, grad_text_value = attend_backward(
        cross_queries, text_keys, text_values, token_live, cross_lse, grad_cross
    )
    grad_cq_b = grad_cq.reshape(row_count, head_cols).astype(jnp.bfloat16)
    grad_cross_q_w = jnp.dot(h_two.T, grad_cq_b, preferred_element_type=jnp.float32)
    grad_text = jnp.stack([grad_text_key, grad_text_value], axis=1).reshape(
        2 * text_rows, 2 * head_cols
    )
    two_part = jnp.dot(grad_cq_b, cross_q_back.T, preferred_element_type=jnp.float32)
    grad_x_norm, grad_gain_two = pull_two(grad_total(two_part))
    grad_x_one = grad_x_two + grad_x_norm
    grad_one_b = grad_x_one.astype(jnp.bfloat16)
    grad_attn_out_w = jnp.dot(self_out.T, grad_one_b, preferred_element_type=jnp.float32)
    grad_self = (
        jnp.dot(grad_one_b, attn_out_back.T, preferred_element_type=jnp.float32)
        .astype(jnp.bfloat16)
        .reshape(row_count, head_count, HD)
    )
    grad_query, grad_key_all, grad_value_all = attend_backward(
        queries, key_all, value_all, key_live, self_lse, grad_self
    )
    grad_key_flat = grad_key_all.reshape(2 * row_count, head_cols)
    grad_value_flat = grad_value_all.reshape(2 * row_count, head_cols)
    back = from_partner(
        (
            partner_rows(grad_key_flat, which_half, row_count),
            partner_rows(grad_value_flat, which_half, row_count),
            partner_rows(grad_text, which_half, text_rows),
        ),
        "dp",
        0,
    )
    grad_key_own = (own_rows(grad_key_flat, which_half, row_count) + back[0]).reshape(
        row_count, head_count, HD
    )
    grad_value_own = own_rows(grad_value_flat, which_half, row_count) + back[1]
    grad_text_own = (own_rows(grad_text, which_half, text_rows) + back[2]).astype(jnp.bfloat16)
    grad_query_raw = rotate(grad_query, -positions).reshape(row_count, head_cols)
    grad_key_raw = rotate(grad_key_own, -positions).reshape(row_count, head_cols)
    grad_qkv_b = (
        jnp.stack([grad_query_raw, grad_key_raw, grad_value_own], axis=1)
        .astype(jnp.bfloat16)
        .reshape(row_count, 3 * head_cols)
    )
    grad_qkv_w = jnp.dot(h_one.T, grad_qkv_b, preferred_element_type=jnp.float32).reshape(
        model_width, 3, head_cols
    )
    grad_cross_kv_w = jnp.dot(context.T, grad_text_own, preferred_element_type=jnp.float32).reshape(
        text_width, 2, head_cols
    )
    one_part = jnp.dot(
        grad_qkv_b,
        qkv_back.reshape(model_width, 3 * head_cols).T,
        preferred_element_type=jnp.float32,
    )
    grad_x_norm, grad_gain_one = pull_one(grad_total(one_part))
    grad_tokens = grad_x_one + grad_x_norm
    grad_gains = jnp.stack([grad_gain_one, grad_gain_two, grad_gain_three], axis=0)
    summed = (
        lax.psum_scatter(grad_qkv_w, "dp", scatter_dimension=0, tiled=True),
        lax.psum_scatter(grad_attn_out_w, "dp", scatter_dimension=1, tiled=True),
        lax.psum_scatter(grad_cross_q_w, "dp", scatter_dimension=0, tiled=True),
        lax.psum_scatter(grad_cross_kv_w, "dp", scatter_dimension=0, tiled=True),
        lax.psum_scatter(grad_cross_out_w, "dp", scatter_dimension=1, tiled=True),
        lax.psum_scatter(grad_in_w, "dp", scatter_dimension=0, tiled=True),
        lax.psum_scatter(grad_out_w, "dp", scatter_dimension=1, tiled=True),
        lax.psum_scatter(grad_gains, "dp", scatter_dimension=1, tiled=True),
        lax.psum_scatter(grad_b_in, "dp", scatter_dimension=1, tiled=True),
        lax.psum_scatter(grad_b_out, "dp", scatter_dimension=0, tiled=True),
    )
    return (
        mixed,
        grad_tokens,
        summed[0],
        summed[1],
        summed[2],
        summed[3],
        summed[4],
        summed[5],
        summed[6],
        summed[7],
        summed[8],
        summed[9],
    )


def near_body(
    tokens,
    context,
    frame_counts,
    text_counts,
    w_qkv,
    w_attn_out,
    w_cross_q,
    w_cross_kv,
    w_cross_out,
    w_in,
    w_out,
    norm_gains,
    b_in,
    b_out,
    cotangent,
):
    n, dp = lax.axis_size("mp"), lax.axis_size("dp")
    shard, _, cols = w_qkv.shape
    small = prepare(
        tokens,
        context,
        frame_counts,
        text_counts,
        w_qkv,
        w_attn_out,
        w_cross_q,
        w_cross_kv,
        w_cross_out,
        w_in,
        w_out,
        norm_gains,
        b_in,
        b_out,
    )
    mixed, gt, gg, *parts = run_block(n, dp, tokens, context, cotangent, *small)
    g_out, g_in, g_mid, g_ckv, g_last = parts
    return (
        mixed,
        gt.astype(F32),
        g_last[:, cols:].reshape(shard, 3, cols),
        g_last[:, :cols].T,
        g_mid[:, cols:],
        g_ckv.reshape(-1, 2, cols),
        g_mid[:, :cols].T,
        g_in.reshape(shard, 2, -1),
        g_out.T,
        gg[:3, :shard],
        gg[3:5, :shard],
        gg[5, :shard],
    )


def solution(mesh):
    in_specs = (
        P("dp", None),
        P("dp", None),
        P(),
        P(),
        P("dp", None, "mp"),
        P("mp", "dp"),
        P("dp", "mp"),
        P("dp", None, "mp"),
        P("mp", "dp"),
        P("dp", None, "mp"),
        P("mp", "dp"),
        P(None, "dp"),
        P(None, ("mp", "dp")),
        P("dp"),
        P("dp", None),
    )
    out_specs = (
        P("dp", None),
        P("dp", None),
        P("dp", None, "mp"),
        P("mp", "dp"),
        P("dp", "mp"),
        P("dp", None, "mp"),
        P("mp", "dp"),
        P("dp", None, "mp"),
        P("mp", "dp"),
        P(None, "dp"),
        P(None, ("mp", "dp")),
        P("dp"),
    )
    near = mesh.shape["dp"] == 8
    return jax.shard_map(
        near_body if near else body,
        mesh=mesh,
        in_specs=in_specs,
        out_specs=out_specs,
        check_vma=False,
    )
```

```python
import functools

import jax
import jax.numpy as jnp
from jax import lax
from jax.experimental import pallas as pl
from jax.experimental.pallas import tpu as pltpu
from jax.sharding import PartitionSpec as P

HD = 64
MESH = pl.DeviceIdType.MESH
HBM = pl.BlockSpec(memory_space=pl.ANY)
BF = jnp.bfloat16
F32 = jnp.float32
epsilon = 1e-05
CH = 16
NR = 32
LAG = 3
DMA = pltpu.SemaphoreType.DMA
WHOLE = (0, 0)


def dot_nn(a, b):
    return lax.dot_general(a, b, (((1,), (0,)), ((), ())), preferred_element_type=F32)


def dot_nt(a, b):
    return lax.dot_general(a, b, (((1,), (1,)), ((), ())), preferred_element_type=F32)


def dot_tn(a, b):
    return lax.dot_general(a, b, (((0,), (0,)), ((), ())), preferred_element_type=F32)


def send(src, dst, send_sem, recv_sem, peer):
    return pltpu.make_async_remote_copy(
        src_ref=src,
        dst_ref=dst,
        send_sem=send_sem,
        recv_sem=recv_sem,
        device_id=peer,
        device_id_type=MESH,
    )


def rows_at(start, size):
    return pl.ds(pl.multiple_of(start, 16), size)


def greet_all(d, z, n, dp):
    barrier = pltpu.get_barrier_semaphore()
    for k in range(1, dp):
        pl.semaphore_signal(barrier, inc=1, device_id=(jnp.bitwise_xor(d, k), z), device_id_type=MESH)
    for k in range(1, n):
        pl.semaphore_signal(barrier, inc=1, device_id=(d, lax.rem(z + k, n)), device_id_type=MESH)
    pl.semaphore_wait(barrier, dp + n - 2)


def normal(x):
    centered = x - jnp.mean(x, axis=-1, keepdims=True)
    r = lax.rsqrt(jnp.mean(centered * centered, axis=-1, keepdims=True) + epsilon)
    return centered * r, r


class Line:
    def __init__(self, d, z, n, own, got, dst, base, sems, k, fin):
        self.d, self.z, self.n = d, z, n
        self.own, self.got, self.dst, self.base = own, got, dst, base
        self.sems, self.k, self.fin = sems, k, fin
        self.half = own.shape[0] // 2
        self.chunks = self.half // CH
        self.slots = self.chunks + 2 * LAG * (n - 1)
        self.next = 0

    def place(self, f):
        z, n = self.z, self.n
        return (z, z + 1, z - 1) if f else (n - 1 - z, z - 1, z + 1)

    def fore(self, f, c, nxt):
        at = rows_at(f * self.half + c * CH, CH)
        s, r = self.sems[0], self.sems[1]
        return send(
            self.own.at[at], self.got.at[at], s.at[self.k, f, c], r.at[self.k, f, c], (self.d, nxt)
        )

    def back(self, f, c, prv):
        at = rows_at(self.base + f * self.half + c * CH, CH)
        s, r = self.sems[2], self.sems[3]
        return send(
            self.dst.at[at], self.dst.at[at], s.at[self.k, f, c], r.at[self.k, f, c], (self.d, prv)
        )

    def slot(self, s):
        n = self.n
        for f in range(2):
            p, nxt, prv = self.place(f)
            c = s - LAG * p
            valid = (c >= 0) & (c < self.chunks)

            @pl.when(valid & (p == 0))
            def _():
                self.fore(f, c, nxt).start()

            @pl.when(valid & (p > 0) & (p < n - 1))
            def _():
                at = rows_at(f * self.half + c * CH, CH)
                self.fore(f, c, nxt).wait_recv()
                self.own[at] = self.own[at] + self.got[at]
                self.fore(f, c, nxt).start()

            @pl.when(valid & (p == n - 1))
            def _():
                at = rows_at(f * self.half + c * CH, CH)
                self.fore(f, c, nxt).wait_recv()
                self.fin(f * self.half + c * CH, self.own[at].astype(F32) + self.got[at].astype(F32))
                self.back(f, c, prv).start()

            b = s - LAG * (2 * (n - 1) - p)

            @pl.when((b >= 0) & (b < self.chunks) & (p < n - 1))
            def _():
                self.back(f, b, prv).wait_recv()

                @pl.when(p > 0)
                def _():
                    self.back(f, b, prv).start()

    def step(self):
        self.slot(self.next)
        self.next += 1

    def left(self):
        return self.slots - self.next

    def drain(self):
        def body(c, carry):
            for f in range(2):
                p, nxt, prv = self.place(f)

                @pl.when(p < self.n - 1)
                def _():
                    self.fore(f, c, nxt).wait_send()

                @pl.when(p > 0)
                def _():
                    self.back(f, c, prv).wait_send()

            return carry

        lax.fori_loop(0, self.chunks, body, 0)


def run(count, *lines):
    lines = [line for line in lines if line.next < line.slots]
    count = max(count, 0)
    first = [line.next for line in lines]

    def body(s, carry):
        for line, at in zip(lines, first):
            line.slot(at + s)
        return carry

    lax.fori_loop(0, count, body, 0)
    for line in lines:
        line.next += count


class Gather:
    def __init__(self, d, z, shard, full, send_sems, recv_sems, local_sems, a):
        self.d, self.z, self.shard, self.full, self.a = d, z, shard, full, a
        self.send_sems, self.recv_sems, self.local = send_sems, recv_sems, local_sems
        self.size = shard.shape[0]
        self.core, self.xn, self.yn = [(jnp.bitwise_xor(d, k), z) for k in (1, 2, 4)]
        self.bx, self.by, self.bd = [jnp.bitwise_xor(d, k) for k in (2, 4, 6)]
        half = self.size // 2
        self.top, self.bottom = (0, half), (half, half)
        self.started = []

    def part(self, block, rows):
        lo, size = rows
        return self.full.at[rows_at(block * self.size + lo, size or self.size)]

    def copy(self, k, block, rows, peer):
        part = self.part(block, rows)
        return send(part, part, self.send_sems.at[self.a, k], self.recv_sems.at[self.a, k], peer)

    def go(self, k, block, rows, peer):
        cp = self.copy(k, block, rows, peer)
        cp.start()
        self.started.append(cp)

    def got(self, k, block, rows, peer):
        self.copy(k, block, rows, peer).wait_recv()

    def begin(self):
        for k, peer in ((0, self.xn), (1, self.yn), (2, self.core)):
            cp = send(
                self.shard,
                self.part(self.d, WHOLE),
                self.send_sems.at[self.a, k],
                self.recv_sems.at[self.a, k],
                peer,
            )
            cp.start()
            self.started.append(cp)
        self.mine = pltpu.make_async_copy(self.shard, self.part(self.d, WHOLE), self.local.at[self.a])
        self.mine.start()

    def near(self):
        self.got(0, self.bx, WHOLE, self.xn)
        self.go(3, self.bx, self.top, self.yn)
        self.go(5, self.bx, WHOLE, self.core)
        self.got(1, self.by, WHOLE, self.yn)
        self.go(4, self.by, self.bottom, self.xn)
        self.go(6, self.by, WHOLE, self.core)

    def far(self):
        self.got(3, self.bd, self.top, self.yn)
        self.go(7, self.bd, self.top, self.core)
        self.got(4, self.bd, self.bottom, self.xn)
        self.go(8, self.bd, self.bottom, self.core)

    def last(self):
        o = [jnp.bitwise_xor(b, 1) for b in (self.d, self.bx, self.by, self.bd)]
        self.got(2, o[0], WHOLE, self.core)
        self.got(5, o[1], WHOLE, self.core)
        self.got(6, o[2], WHOLE, self.core)
        self.got(7, o[3], self.top, self.core)
        self.got(8, o[3], self.bottom, self.core)
        self.mine.wait()

    def drain(self):
        for cp in self.started:
            cp.wait_send()


class Moves:
    def __init__(self, sems):
        self.sems, self.used = sems, 0

    def start(self, src, dst):
        cp = pltpu.make_async_copy(src, dst, self.sems.at[self.used])
        self.used += 1
        cp.start()
        return cp


def turn(u, cosine, low, high):
    return u * cosine + pltpu.roll(u, 112, 1) * low + pltpu.roll(u, 16, 1) * high


def half_mask(rows, e):
    lane = lax.broadcasted_iota(jnp.int32, (rows, 128), 1)
    return (lane >= 64) == (e == 1)


def softmax(s):
    w = jnp.exp(s - jnp.max(s, axis=-1, keepdims=True))
    return w * (1.0 / jnp.sum(w, axis=-1, keepdims=True))


class Scatter:
    def __init__(self, d, z, got, one, two, out, sems, out_sem):
        self.d, self.z = d, z
        self.got, self.one, self.two, self.out = got, one, two, out
        self.sems, self.out_sem = sems, out_sem
        self.c, self.x, self.y = lax.rem(d, 2), lax.rem(d // 2, 2), d // 4
        self.core, self.xn, self.yn = [(jnp.bitwise_xor(d, k), z) for k in (1, 2, 4)]
        self.arrays, self.copies, self.now = [], [], 0

    def add(self, size, buf, place, compute, dst):
        self.arrays.append((size, buf, place, compute, dst))
        self.copies.append({})

    def block(self, a, j, c, lo=0, size=None):
        shard, buf, place, _, _ = self.arrays[a]
        row, lane = place(j)
        width = self.got.shape[-1]
        return buf.at[rows_at(row + c * shard + lo, size or shard), pl.ds(pl.multiple_of(lane, 128), width)]

    def go(self, a, stage, k, src, dst, peer):
        sd, rv = self.sems[stage]
        cp = send(src, dst, sd.at[a % 2, k], rv.at[a % 2, k], peer)
        cp.start()
        self.copies[a][stage, k] = cp

    def core_copy(self, a, t):
        sd, rv = self.sems[0]
        shard = self.arrays[a][0]
        return send(
            self.block(a, t, 1 - self.c),
            self.got.at[a % 2, t, pl.ds(0, shard)],
            sd.at[a % 2, t],
            rv.at[a % 2, t],
            self.core,
        )

    def compute(self, a, between):
        _, buf, place, tile, _ = self.arrays[a]

        def step(t, carry):
            tile(t)
            self.core_copy(a, t).start()
            between(t)
            return carry

        lax.fori_loop(0, 4, step, 0)

    def plus(self, ref, part):
        piece = 48

        def body(i, carry):
            at = rows_at(i * piece, piece)
            ref[at] = ref[at] + part[at]
            return carry

        lax.fori_loop(0, ref.shape[0] // piece, body, 0)

    def add_core(self, a):
        shard = self.arrays[a][0]
        half = shard // 2

        def body(j, carry):
            self.core_copy(a, j).wait_recv()
            self.plus(self.block(a, j, self.c), self.got.at[a % 2, j])
            return carry

        lax.fori_loop(0, 4, body, 0)
        for b in range(2):
            for side, j, lo, peer in (
                (0, 2 * b + 1 - self.x, 0, self.xn),
                (1, 2 * (1 - self.y) + b, half, self.yn),
            ):
                self.go(
                    a,
                    1,
                    2 * side + b,
                    self.block(a, j, self.c, lo, half),
                    self.one.at[a % 2, side, b, pl.ds(0, half)],
                    peer,
                )

    def add_one(self, a):
        half = self.arrays[a][0] // 2
        for b in range(2):
            for side, j, lo in ((0, 2 * b + self.x, 0), (1, 2 * self.y + b, half)):
                self.copies[a][1, 2 * side + b].wait_recv()
                self.plus(self.block(a, j, self.c, lo, half), self.one.at[a % 2, side, b])
        for side, j, lo, peer in (
            (0, 2 * (1 - self.y) + self.x, 0, self.yn),
            (1, 2 * self.y + 1 - self.x, half, self.xn),
        ):
            self.go(
                a,
                2,
                side,
                self.block(a, j, self.c, lo, half),
                self.two.at[a % 2, side, pl.ds(0, half)],
                peer,
            )

        def body(t, carry):
            self.core_copy(a, t).wait_send()
            return carry

        lax.fori_loop(0, 4, body, 0)

    def out_copy(self, a):
        shard, dst = self.arrays[a][0], self.arrays[a][4]
        return pltpu.make_async_copy(self.out.at[a % 2, pl.ds(0, shard)], dst, self.out_sem.at[a % 2])

    def add_two(self, a):
        half = self.arrays[a][0] // 2
        piece = 48
        for side in range(2):
            self.copies[a][2, side].wait_recv()
            ref = self.block(a, 2 * self.y + self.x, self.c, side * half, half)

            def body(i, carry, side=side, ref=ref):
                at = rows_at(i * piece, piece)
                to = rows_at(side * half + i * piece, piece)
                self.out[a % 2, to] = ref[at].astype(F32) + self.two[a % 2, side, at].astype(F32)
                return carry

            lax.fori_loop(0, half // piece, body, 0)
        self.out_copy(a).start()
        for k in range(4):
            self.copies[a][1, k].wait_send()

    def retire(self, a):
        for k in range(2):
            self.copies[a][2, k].wait_send()
        self.out_copy(a).wait()

    def step(self, pace, make):
        s, count = self.now, len(self.arrays)
        self.now += 1
        for lag, stage in ((4, self.retire), (3, self.add_two), (2, self.add_one), (1, self.add_core)):
            if 0 <= s - lag < count:
                stage(s - lag)
                if lag < 4:
                    pace()
        if s < count:
            self.compute(s, make())


def block_kernel(
    n,
    dp,
    tokens,
    context,
    cotangent,
    tables,
    frame_counts,
    text_counts,
    vec,
    s_qkv,
    s_small,
    s_ckv,
    s_out,
    s_in,
    w_qkv,
    w_out,
    w_in,
    o_h1,
    o_p,
    o_mixed,
    o_gt,
    o_gains,
    o_b_in,
    o_b_out,
    o_out,
    o_in,
    o_mid,
    o_ckv,
    o_last,
    v_vec,
    gv,
    win,
    wout,
    wsmall,
    h2,
    h3,
    dy,
    hid,
    dgu,
    dx2r,
    dx1r,
    x1,
    x2,
    dx,
    q,
    k,
    v,
    so,
    co,
    cq,
    dco,
    dcq,
    dso,
    dqkv,
    tkv,
    dtkv,
    pc,
    pst,
    dk,
    dv,
    ctx,
    tab,
    gg,
    own,
    got,
    krv,
    tst,
    trv,
    s_got,
    s_one,
    s_two,
    s_out_v,
    ggs,
    ggr,
    ggz,
    ggo,
    v_gains,
    v_b_in,
    v_b_out,
    g_send,
    g_recv,
    g_local,
    e_send,
    e_recv,
    f_send,
    f_recv,
    k_send,
    k_recv,
    fs,
    fr,
    bs,
    br,
    p_sem,
    c_send,
    c_recv,
    a_send,
    a_recv,
    b_send,
    b_recv,
    s_sem,
    v_send,
    v_recv,
    moves,
):
    d = lax.axis_index("dp")
    z = lax.axis_index("mp")
    rows, width = tokens.shape
    group = rows // 2
    cols = so.shape[1]
    units = hid.shape[1]
    pairs = cols // 128
    half = lax.rem(d, 2)
    core = (jnp.bitwise_xor(d, 1), z)
    tok, mixed, gt, h1 = dy, dy, dx2r, hid
    v_qkv = win.at[:, pl.ds(0, 3 * cols)]
    v_ckv = wout.at[pl.ds(0, s_ckv.shape[0] * dp), pl.ds(0, 2 * cols)]
    mv = Moves(moves)
    ld_tok = mv.start(tokens, tok)
    ld_small = [mv.start(a, b) for a, b in ((context, ctx), (tables, tab))]
    ld_vec = mv.start(vec, v_vec.at[d])
    greet_all(d, z, n, dp)
    vec_copies = []
    for j in range(1, dp):
        peer = (jnp.bitwise_xor(d, j), z)
        cp = send(vec, v_vec.at[d], e_send.at[j], e_recv.at[j], peer)
        cp.start()
        vec_copies.append(cp)
    gathers = [
        Gather(d, z, shard_ref, full, g_send, g_recv, g_local, a)
        for a, (shard_ref, full) in enumerate(
            ((s_qkv, v_qkv), (s_ckv, v_ckv), (s_small, wsmall), (s_out, w_out), (s_in, w_in))
        )
    ]
    g_qkv, g_ckv, g_small, g_out, g_in = gathers
    g_qkv.begin()
    gg[...] = jnp.zeros_like(gg)
    dtkv[...] = jnp.zeros_like(dtkv)

    def clear(i, carry):
        at = rows_at(i * NR, NR)
        dk[at] = jnp.zeros((NR, cols), F32)
        dv[at] = jnp.zeros((NR, cols), F32)
        return carry

    ld_tok.wait()
    ld_vec.wait()
    for j in range(1, dp):
        b = jnp.bitwise_xor(d, j)
        send(v_vec.at[b], v_vec.at[b], e_send.at[j], e_recv.at[j], (b, z)).wait_recv()
    shard = width // dp
    for b in range(dp):
        gv[:, b * shard : (b + 1) * shard] = v_vec[b][:8, :shard].astype(F32)

    def norm_rows(i, carry):
        at = rows_at(i * NR, NR)
        h1[at] = (normal(tok[at].astype(F32))[0] * gv[0:1]).astype(BF)
        return carry

    lax.fori_loop(0, rows // NR // 2, norm_rows, 0)
    g_qkv.near()
    g_ckv.begin()
    g_small.begin()
    lax.fori_loop(rows // NR // 2, rows // NR, norm_rows, 0)
    st_h1 = mv.start(h1, o_h1)
    lax.fori_loop(0, 2 * rows // NR, clear, 0)
    for ld in ld_small:
        ld.wait()
    clip = d // 2
    text = ctx.shape[0]
    key_at = lax.broadcasted_iota(jnp.int32, (1, 2 * rows), 1)
    text_at = lax.broadcasted_iota(jnp.int32, (1, 2 * text), 1)
    key_bias = jnp.where(key_at <= frame_counts[clip], 0.0, -1e30)
    text_bias = jnp.where(text_at < text_counts[clip], 0.0, -1e30)
    g_qkv.far()
    g_qkv.last()
    my_rows = half * rows

    def project(g, carry):
        at = rows_at(g * group, group)
        mine = rows_at(my_rows + g * group, group)
        x = h1[at]
        for part in (1, 2, 0):
            u = dot_nn(x, win[:, part * cols : (part + 1) * cols])
            if part == 2:
                v[mine] = u.astype(BF)
                continue
            for j in range(pairs):
                r = turn(u[:, j * 128 : (j + 1) * 128], tab[0, at], tab[1, at], tab[2, at])
                if part:
                    k[mine, j * 128 : (j + 1) * 128] = r.astype(BF)
                else:
                    q[at, j * 128 : (j + 1) * 128] = (r * HD ** (-0.5)).astype(BF)
        return carry

    lax.fori_loop(0, 2, project, 0)
    mine, theirs = rows_at(my_rows, rows), rows_at((1 - half) * rows, rows)
    kv = [send(r.at[mine], r.at[mine], f_send.at[i], f_recv.at[i], core) for i, r in enumerate((k, v))]
    for cp in kv:
        cp.start()
    st_qkv = mv.start(v_qkv, w_qkv)
    g_ckv.near()
    g_small.near()
    g_out.begin()
    g_ckv.far()
    g_ckv.last()
    g_small.far()
    g_in.begin()
    t_mine, t_theirs = rows_at(half * text, text), rows_at((1 - half) * text, text)
    tkv[t_mine] = dot_nn(ctx[...], v_ckv[...]).astype(BF)
    kv.append(send(tkv.at[t_mine], tkv.at[t_mine], f_send.at[2], f_recv.at[2], core))
    kv[2].start()
    for i, r in enumerate((k, v)):
        send(r.at[theirs], r.at[theirs], f_send.at[i], f_recv.at[i], core).wait_recv()

    tile = 256

    def feed(g, lo, count, between):
        at = rows_at(g * group, group)

        def step(i, carry):
            u = pl.multiple_of(i * tile, tile)
            us, ups = pl.ds(u, tile), pl.ds(pl.multiple_of(units + u, tile), tile)
            x = h3[at]
            gate = dot_nn(x, win[:, us]) + gv[3:4, us]
            up = dot_nn(x, win[:, ups]) + gv[4:5, us]
            dh = dot_nn(dy[at], wout[:, us])
            sig = jax.nn.sigmoid(gate)
            act = gate * sig
            hid[at, us] = (act * up).astype(BF)
            d_gate = (dh * up * (sig * (1.0 + gate * (1.0 - sig)))).astype(BF)
            d_up = (dh * act).astype(BF)
            dgu[at, us] = d_gate
            dgu[at, ups] = d_up
            gg[3:4, us] += jnp.sum(d_gate.astype(F32), axis=0, keepdims=True)
            gg[4:5, us] += jnp.sum(d_up.astype(F32), axis=0, keepdims=True)
            between(i - lo)
            return carry

        lax.fori_loop(lo, lo + count, step, 0)

    def norm_back(x, dn, gain, row):
        nrm, r = normal(x)
        gg[row : row + 1] += jnp.sum(dn * nrm, axis=0, keepdims=True)
        e = dn * gain
        return r * (
            e
            - jnp.mean(e, axis=-1, keepdims=True)
            - nrm * jnp.mean(e * nrm, axis=-1, keepdims=True)
        )

    def places(g, lo):
        return rows_at(g * group + lo, CH), rows_at(
            g * group // 2 + lax.rem(lo, group // 2), CH
        )

    def start_two(g):
        def fin(lo, total):
            at, mine = places(g, lo)
            x = tok[at].astype(F32) + total
            x1[mine] = x
            h2[at] = (normal(x)[0] * gv[1:2]).astype(BF)

        return fin

    def start_three(g):
        def fin(lo, total):
            at, mine = places(g, lo)
            x = x1[mine] + total
            x2[mine] = x
            h3[at] = (normal(x)[0] * gv[2:3]).astype(BF)

        return fin

    def finish_mixed(g):
        def fin(lo, total):
            at, mine = places(g, lo)
            mixed[at] = (x2[mine] + total + gv[5:6]).astype(BF)

        return fin

    def finish_three(g):
        def fin(lo, total):
            at, mine = places(g, lo)
            x = dy[at].astype(F32) + norm_back(x2[mine], total, gv[2:3], 2)
            dx[mine] = x
            dx2r[at] = x.astype(BF)

        return fin

    def finish_two(g):
        def fin(lo, total):
            at, mine = places(g, lo)
            x = dx[mine] + norm_back(x1[mine], total, gv[1:2], 1)
            dx[mine] = x
            dx1r[at] = x.astype(BF)

        return fin

    def finish_one(g):
        def fin(lo, total):
            at, mine = places(g, lo)
            x = dx[mine] + norm_back(h3[at].astype(F32), total, gv[0:1], 0)
            gt[at] = x.astype(BF)

        return fin

    sems = (fs, fr, bs, br)

    def lines(dst, slot, index, fin):
        return [
            Line(
                d, z, n, own.at[slot + g], got.at[slot + g], dst, g * group, sems, index + g, fin(g)
            )
            for g in range(2)
        ]

    fore_one = lines(h2, 0, 0, start_two)
    fore_two = lines(h3, 2, 2, start_three)
    mix = lines(mixed, 2, 4, finish_mixed)
    three = lines(dx2r, 0, 6, finish_three)
    two = lines(dx1r, 0, 8, finish_two)
    one = lines(gt, 0, 10, finish_one)

    def with_lines(total, every, *ls):
        ls = [line for line in ls if line.next < line.slots]
        starts = [line.next for line in ls]

        def between(i):
            def go():
                for line, s in zip(ls, starts):
                    for e in range(2 if every == 1 else 1):
                        line.slot(s + (2 if every == 1 else 1) * (i // every) + e)

            if every == 1:
                go()
            else:
                pl.when(lax.rem(i, every) == 0)(go)

        for line in ls:
            line.next += -(-total // every) * (2 if every == 1 else 1)
        return between

    tiles = units // tile
    pieces = 2
    per = tiles // pieces
    piece = units // pieces

    sc = Scatter(
        d, z, s_got, s_one, s_two, s_out_v, ((c_send, c_recv), (a_send, a_recv), (b_send, b_recv)), s_sem
    )
    wide = s_got.shape[-1]

    def part_of(buf, lane, size, *terms):
        def tile_at(t):
            at = rows_at(t * 2 * size, 2 * size)
            to = lane
            for left, right, lo, count in terms:
                cols_at = pl.ds(pl.multiple_of(t * 2 * size, 128), 2 * size)
                buf[at, to : to + count] = dot_tn(left[:, cols_at], right[:, lo : lo + count]).astype(BF)
                to += count

        return tile_at

    def add_array(buf, lane, dst, *terms):
        sc.add(
            shard,
            buf,
            lambda j: (j * 2 * shard, lane),
            part_of(buf, lane, shard, *terms),
            dst,
        )

    def text_tile(j):
        left = ctx[...]
        t = text_width // 4
        g = dot_tn(left, tst[...]).astype(BF)
        for i in range(4):

            @pl.when(j == i)
            def _():
                dgu[0:t, i * wide : (i + 1) * wide] = g[i * t : (i + 1) * t]

    text_width = ctx.shape[1]
    for i in range(2):
        add_array(wout, i * wide, o_out.at[:, pl.ds(i * wide, wide)], (dy, hid, i * wide, wide))
    for i in range(4):
        add_array(win, i * wide, o_in.at[:, pl.ds(i * wide, wide)], (h3, dgu, i * wide, wide))
    add_array(wout, 0, o_mid, (dx2r, co, 0, cols), (h2, dcq, 0, cols))
    sc.add(text_width // dp, dgu, lambda j: (0, j * wide), text_tile, o_ckv)
    add_array(wout, wide, o_last.at[:, pl.ds(0, wide)], (dx1r, so, 0, cols), (hid, dqkv, 0, cols))
    add_array(win, 2 * wide, o_last.at[:, pl.ds(wide, wide)], (hid, dqkv, cols, wide))

    def attend(g, queries, keys, key_lo, values, value_lo, bias, save, out, between):
        at = rows_at(g * group, group)

        def head(h, carry):
            j, e = h // 2, lax.rem(h, 2)
            lo = pl.multiple_of(j * 128, 128)
            mask = half_mask(group, e)
            qb = jnp.where(mask, queries[at, pl.ds(lo, 128)], jnp.zeros((), BF))
            s = dot_nt(qb, keys[:, pl.ds(pl.multiple_of(key_lo + lo, 128), 128)]) + bias
            p = softmax(s).astype(BF)
            save(h, p)
            o = dot_nn(p, values[:, pl.ds(pl.multiple_of(value_lo + lo, 128), 128)])
            out[at, pl.ds(lo, 128)] = jnp.where(mask, o.astype(BF), out[at, pl.ds(lo, 128)])
            between(h)
            return carry

        lax.fori_loop(0, 2 * pairs, head, 0)

    def self_forward(g, every, *ls):
        at = rows_at(g * group, group)

        def keep(h):
            slot = lax.rem(h, 2)
            return pltpu.make_async_copy(pst.at[slot], o_p.at[h, at], p_sem.at[slot])

        def save(h, p):
            @pl.when(h >= 2)
            def _():
                keep(h - 2).wait()

            pst[lax.rem(h, 2)] = p
            keep(h).start()

        attend(g, q, k, 0, v, 0, key_bias, save, so, with_lines(6, every, *ls))
        run(1, *ls)
        for h in (2 * pairs - 2, 2 * pairs - 1):
            keep(h).wait()
        own[g] = dot_nt(so[at], wsmall[:, 0:cols]).astype(BF)

    def cross_forward(g, every, *ls):
        at = rows_at(g * group, group)
        cq[at] = dot_nn(h2[at], wsmall[:, cols : 2 * cols]).astype(BF) * jnp.asarray(HD ** (-0.5), BF)

        def save(h, p):
            pc[h, at] = p

        run(1, *ls)
        attend(g, cq, tkv, 0, tkv, cols, text_bias, save, co, with_lines(6, every, *ls))
        run(1, *ls)
        own[2 + g] = dot_nt(co[at], wsmall[:, 2 * cols :]).astype(BF)

    def attend_back(g, d_out, queries, keys, key_lo, values, value_lo, probs, dkr, dk_lo, dvr, dv_lo, dq, between):
        at = rows_at(g * group, group)

        def head(h, carry):
            j, e = h // 2, lax.rem(h, 2)
            lo = pl.multiple_of(j * 128, 128)
            here = pl.ds(lo, 128)
            mask = half_mask(group, e)
            zero = jnp.zeros((), BF)
            do = jnp.where(mask, d_out[at, here], zero)
            qb = jnp.where(mask, queries[at, here], zero)
            p = probs(h)
            pf = p.astype(F32)
            dp_ = dot_nt(do, values[:, pl.ds(pl.multiple_of(value_lo + lo, 128), 128)])
            ds = (pf * (dp_ - jnp.sum(pf * dp_, axis=-1, keepdims=True))).astype(BF)
            g_q = dot_nn(ds, keys[:, pl.ds(pl.multiple_of(key_lo + lo, 128), 128)]) * HD ** (-0.5)
            dkr[:, pl.ds(pl.multiple_of(dk_lo + lo, 128), 128)] += dot_tn(ds, qb)
            dvr[:, pl.ds(pl.multiple_of(dv_lo + lo, 128), 128)] += dot_tn(p, do)
            dq(h, at, here, mask, g_q)
            between(h)
            return carry

        lax.fori_loop(0, 2 * pairs, head, 0)

    def cross_back(g, every, *ls):
        at = rows_at(g * group, group)
        dco[at] = dot_nn(dx2r[at], wsmall[:, 2 * cols :]).astype(BF)
        run(1, *ls)

        def dq(h, at, here, mask, g_q):
            dcq[at, here] = jnp.where(mask, g_q.astype(BF), dcq[at, here])

        attend_back(
            g, dco, cq, tkv, 0, tkv, cols, lambda h: pc[h, at], dtkv, 0, dtkv, cols, dq, with_lines(6, every, *ls)
        )

    def self_back(g, *ls):
        at = rows_at(g * group, group)

        def load(h):
            slot = lax.rem(h, 2)
            return pltpu.make_async_copy(o_p.at[h, at], pst.at[slot], p_sem.at[slot])

        load(0).start()
        dso[at] = dot_nn(dx1r[at], wsmall[:, 0:cols]).astype(BF)
        run(1, *ls)

        def probs(h):
            @pl.when(h + 1 < 2 * pairs)
            def _():
                load(h + 1).start()

            load(h).wait()
            return pst[lax.rem(h, 2)]

        def dq(h, at, here, mask, g_q):
            r = turn(g_q, tab[0, at], -tab[1, at], -tab[2, at]).astype(BF)
            dqkv[at, here] = jnp.where(mask, r, dqkv[at, here])

        attend_back(g, dso, q, k, 0, v, 0, probs, dk, 0, dv, 0, dq, with_lines(6, 1, *ls))

    def three_part(g, *ls):
        at = rows_at(g * group, group)
        step = width // 4
        for i in range(4):
            to = slice(i * step, (i + 1) * step)
            own[g, :, to] = dot_nt(dgu[at], win[to]).astype(BF)
            if i % 2:
                run(1, *ls)

    def gradient(*ls):
        sc.step(lambda: run(1, *ls), lambda: with_lines(4, 2, *ls))

    def down_part(g):
        at = rows_at(g * group, group)
        own[2 + g] = dot_nt(hid[at], wout[...]).astype(BF)

    def two_part(g):
        at = rows_at(g * group, group)
        own[g] = dot_nt(dcq[at], wsmall[:, cols : 2 * cols]).astype(BF)

    def one_part(g):
        at = rows_at(g * group, group)
        own[g] = dot_nt(dqkv[at], win[:, 0 : 3 * cols]).astype(BF)

    g_small.last()
    self_forward(0, 1)
    self_forward(1, 1, fore_one[0])
    run(8, fore_one[0], fore_one[1])
    g_out.near()
    g_in.near()
    run(fore_one[0].left(), fore_one[0], fore_one[1])
    send(tkv.at[t_theirs], tkv.at[t_theirs], f_send.at[2], f_recv.at[2], core).wait_recv()
    cross_forward(0, 3, fore_one[1])
    run(fore_one[1].left(), fore_one[1], fore_two[0])
    ld_dy = mv.start(cotangent, dy)
    cross_forward(1, 3, fore_two[0])
    st_qkv.wait()
    g_out.far()
    g_in.far()
    run(8, fore_two[0], fore_two[1])
    g_out.last()
    g_in.last()
    g_qkv.drain()
    g_ckv.drain()
    w_loads = []
    for i in range(pieces):
        at = slice(i * piece, (i + 1) * piece)
        up = slice(units + i * piece, units + (i + 1) * piece)
        w_loads.append(
            [
                mv.start(w_in.at[:, at], win.at[:, at]),
                mv.start(w_in.at[:, up], win.at[:, up]),
                mv.start(w_out.at[:, at], wout.at[:, at]),
            ]
        )
    run(fore_two[0].left(), fore_two[0], fore_two[1])
    ld_dy.wait()
    st_h1.wait()

    def bias_sum(i, carry):
        gg[5:6] += jnp.sum(dy[rows_at(i * NR, NR)].astype(F32), axis=0, keepdims=True)
        return carry

    for i in range(pieces):
        for cp in w_loads[i]:
            cp.wait()
        feed(0, i * per, per, with_lines(per, 1, fore_two[1]))
    fore_one[0].drain()
    three_part(0, fore_two[1])
    run(fore_two[1].left(), fore_two[1], three[0])
    lax.fori_loop(0, rows // NR, bias_sum, 0)
    for line in (fore_one[1], fore_two[0], fore_two[1]):
        line.drain()
    feed(1, 0, tiles, with_lines(tiles, 1, three[0]))
    three_part(1, three[0])
    down_part(0)
    run(1, three[0], three[1])
    down_part(1)
    run(1, three[0], three[1])
    gradient(three[0], three[1])
    gradient(three[0], three[1])
    ld_h1 = mv.start(o_h1, hid)
    run(three[0].left(), three[0], three[1])
    cross_back(0, 2, three[1])
    three[0].drain()
    two_part(0)
    gradient(three[1], two[0])
    run(three[1].left(), three[1], two[0])
    cross_back(1, 2, two[0])
    three[1].drain()
    two_part(1)
    tst[...] = dtkv[t_theirs].astype(BF)
    t_copy = send(tst, trv, k_send.at[2], k_recv.at[2], core)
    t_copy.start()
    gradient(two[0], two[1])
    run(2, two[0], two[1])
    gradient(two[0], two[1])
    run(two[0].left(), two[0], two[1])
    self_back(0, two[1], mix[0])
    two[0].drain()
    gradient(two[1], mix[0])
    ld_tok = mv.start(tokens, h3)
    run(two[1].left(), two[1], mix[0])
    gradient(mix[0], mix[1])
    self_back(1, mix[0], mix[1])
    two[1].drain()
    dco[...] = dk[theirs].astype(BF)
    k_copy = send(dco, krv.at[0], k_send.at[0], k_recv.at[0], core)
    k_copy.start()
    dcq[...] = dv[theirs].astype(BF)
    v_copy = send(dcq, krv.at[1], k_send.at[1], k_recv.at[1], core)
    v_copy.start()
    t_copy.wait()
    tst[...] = (dtkv[t_mine] + trv[...].astype(F32)).astype(BF)
    gradient(mix[0], mix[1])
    ld_qkv = mv.start(w_qkv, win.at[:, pl.ds(0, 3 * cols)])
    k_copy.wait_recv()
    ld_h1.wait()
    ld_tok.wait()
    for g in range(2):
        at = slice(g * group, (g + 1) * group)
        own_at = rows_at(half * rows + g * group, group)
        for j in range(pairs):
            here = slice(j * 128, (j + 1) * 128)
            u = dk[own_at, here] + krv[0, at, here].astype(F32)
            dqkv[at, cols + j * 128 : cols + (j + 1) * 128] = turn(
                u, tab[0, at], -tab[1, at], -tab[2, at]
            ).astype(BF)
        if g == 0:
            v_copy.wait_recv()
        dqkv[at, 2 * cols :] = (dv[own_at] + krv[1, at].astype(F32)).astype(BF)
        if g == 0:
            ld_qkv.wait()
        one_part(g)
        if g == 0:
            run(4, one[0], mix[0], mix[1])
    gradient(one[0], one[1], mix[0], mix[1])
    run(1, one[0], one[1], mix[0], mix[1])
    gradient(one[0], one[1], mix[0], mix[1])
    run(2, one[0], one[1], mix[0], mix[1])
    gradient(one[0], one[1], mix[0], mix[1])
    run(3, one[0], one[1], mix[0], mix[1])
    gradient(one[0], one[1], mix[0], mix[1])
    run(max(one[1].left(), mix[0].left(), mix[1].left()), one[0], one[1], mix[0], mix[1])
    st = [mv.start(mixed, o_mixed), mv.start(gt, o_gt)]
    ggs[...] = jnp.zeros_like(ggs)
    for b in range(dp):
        ggs[b, :, 0:shard] = gg[:, b * shard : (b + 1) * shard]
    sums = []
    for b in range(1, dp):
        to = jnp.bitwise_xor(d, b)
        cp = send(ggs.at[to], ggr.at[b], v_send.at[b], v_recv.at[b], (to, z))
        cp.start()
        sums.append(cp)
    gradient()
    total = ggs[d]
    for b, cp in enumerate(sums):
        cp.wait_recv()
        total = total + ggr[b + 1]
    ggo[...] = total
    line_sums = []
    for j in range(1, n):
        cp = send(
            ggo, ggz.at[j], v_send.at[dp + j - 1], v_recv.at[dp + j - 1], (d, lax.rem(z + j, n))
        )
        cp.start()
        line_sums.append(cp)
    gradient()
    for j, cp in enumerate(line_sums):
        cp.wait_recv()
        total = total + ggz[j + 1]
    v_gains[...] = total[0:3, 0:shard]
    v_b_in[...] = ggo[3:5, 0:shard]
    v_b_out[...] = ggo[5:6, 0:shard]
    st += [mv.start(a, b) for a, b in ((v_gains, o_gains), (v_b_in, o_b_in), (v_b_out, o_b_out))]
    for cp in sums + line_sums + [k_copy, v_copy] + kv + vec_copies:
        cp.wait_send()
    for g in (g_small, g_out, g_in):
        g.drain()
    for line in mix + one:
        line.drain()
    for cp in st:
        cp.wait()


def run_block(n, dp, tokens, context, cotangent, tables, frame_counts, text_counts, vec, s_qkv, s_small, s_ckv, s_out, s_in):
    rows, width = tokens.shape
    cols = s_qkv.shape[1] // 3
    units = s_out.shape[1]
    heads = cols // HD
    text, text_width = context.shape
    shard = width // dp
    half_rows = rows // 2
    sds = jax.ShapeDtypeStruct
    outs = [
        sds((width, 3 * cols), BF),
        sds((width, units), BF),
        sds((width, 2 * units), BF),
        sds((rows, width), BF),
        sds((heads, rows, 2 * rows), BF),
        sds((rows, width), BF),
        sds((rows, width), BF),
        sds((3, shard), F32),
        sds((2, shard), F32),
        sds((1, shard), F32),
        sds((shard, units), F32),
        sds((shard, 2 * units), F32),
        sds((shard, 2 * cols), F32),
        sds((text_width // dp, 2 * cols), F32),
        sds((shard, 4 * cols), F32),
    ]
    vm = pltpu.VMEM
    chunks = rows // 4 // CH
    full, head, own_x = vm((rows, width), BF), vm((rows, cols), BF), vm((half_rows, width), F32)
    keys = vm((2 * rows, cols), BF)
    scratch = [
        vm((dp,) + vec.shape, BF),
        vm((8, width), F32),
        vm((width, 2 * units), BF),
        vm((width, units), BF),
        vm((width, 3 * cols), BF),
        full,
        full,
        full,
        vm((rows, units), BF),
        vm((rows, 2 * units), BF),
        full,
        full,
        own_x,
        own_x,
        own_x,
        head,
        keys,
        keys,
        head,
        head,
        head,
        head,
        head,
        head,
        vm((rows, 3 * cols), BF),
        vm((2 * text, 2 * cols), BF),
        vm((2 * text, 2 * cols), F32),
        vm((heads, rows, 2 * text), BF),
        vm((2, half_rows, 2 * rows), BF),
        vm((2 * rows, cols), F32),
        vm((2 * rows, cols), F32),
        vm(context.shape, BF),
        vm(tables.shape, F32),
        vm((8, width), F32),
        vm((4, half_rows, width), BF),
        vm((4, half_rows, width), BF),
        vm((2, rows, cols), BF),
        vm((text, 2 * cols), BF),
        vm((text, 2 * cols), BF),
        vm((2, 4, shard, 2 * cols), BF),
        vm((2, 2, 2, shard // 2, 2 * cols), BF),
        vm((2, 2, shard // 2, 2 * cols), BF),
        vm((2, shard, 2 * cols), F32),
        vm((dp, 8, 256), F32),
        vm((dp, 8, 256), F32),
        vm((n, 8, 256), F32),
        vm((8, 256), F32),
        vm((3, shard), F32),
        vm((2, shard), F32),
        vm((1, shard), F32),
        DMA((5, 9)),
        DMA((5, 9)),
        DMA((5,)),
        DMA((dp,)),
        DMA((dp,)),
        DMA((3,)),
        DMA((3,)),
        DMA((3,)),
        DMA((3,)),
        *[DMA((12, 2, chunks))] * 4,
        DMA((2,)),
        DMA((2, 4)),
        DMA((2, 4)),
        DMA((2, 4)),
        DMA((2, 4)),
        DMA((2, 2)),
        DMA((2, 2)),
        DMA((2,)),
        DMA((dp + n - 1,)),
        DMA((dp + n - 1,)),
        DMA((32,)),
    ]
    ins = (tokens, context, cotangent, tables, frame_counts, text_counts, vec, s_qkv, s_small, s_ckv, s_out, s_in)
    scalars = pl.BlockSpec(memory_space=pltpu.SMEM)
    return pl.pallas_call(
        functools.partial(block_kernel, n, dp),
        out_shape=outs,
        in_specs=[HBM] * 4 + [scalars] * 2 + [HBM] * 6,
        out_specs=[HBM] * len(outs),
        scratch_shapes=scratch,
        compiler_params=pltpu.CompilerParams(
            collective_id=0, has_side_effects=True, vmem_limit_bytes=63 * 2**20
        ),
        name="block",
    )(*ins)[5:]


def prepare(tokens, context, frame_counts, text_counts, w_qkv, w_attn_out, w_cross_q, w_cross_kv, w_cross_out, w_in, w_out, norm_gains, b_in, b_out):
    shard, _, cols = w_qkv.shape
    rows = tokens.shape[0]
    vec = jnp.concatenate([norm_gains, b_in, b_out[None]], axis=0)
    vec = jnp.pad(vec, ((0, 16 - vec.shape[0]), (0, 256 - shard)))
    d = lax.axis_index("dp")
    half = d % 2
    m = HD // 4
    lane = jnp.arange(128) % HD
    frequency = 10000.0 ** (-(lane % m).astype(F32) / m)
    angle = (half * rows + jnp.arange(rows)).astype(F32)[:, None] * frequency[None]
    sine = jnp.sin(angle)
    tables = jnp.stack(
        [
            jnp.where(lane < 2 * m, jnp.cos(angle), 1.0),
            jnp.where(lane < m, -sine, 0.0),
            jnp.where((lane >= m) & (lane < 2 * m), sine, 0.0),
        ]
    )
    return (
        tables,
        frame_counts,
        text_counts,
        vec,
        w_qkv.reshape(shard, 3 * cols),
        jnp.concatenate([w_attn_out.T, w_cross_q, w_cross_out.T], axis=1),
        w_cross_kv.reshape(w_cross_kv.shape[0], 2 * cols),
        w_out.T,
        w_in.reshape(shard, -1),
    )


def from_partner(block, axis, stride):
    count = lax.axis_size(axis)
    route = []
    for low in range(count):
        high = low | 1 << stride
        if high != low and high < count:
            route += [(low, high), (high, low)]
    return lax.ppermute(block, axis, route)


def layer_norm(values, gain_row):
    centered = values - jnp.mean(values, axis=-1, keepdims=True)
    spread = jnp.mean(centered * centered, axis=-1, keepdims=True)
    return centered * lax.rsqrt(spread + epsilon) * gain_row


def rotate(tensor, positions):
    quarter = tensor.shape[-1] // 4
    frequency = 10000.0 ** (-jnp.arange(quarter, dtype=jnp.float32) / quarter)
    angles = positions[:, None] * frequency[None, :]
    cosine = jnp.cos(angles)[:, None, :]
    sine_part = jnp.sin(angles)[:, None, :]
    first_part = tensor[..., :quarter]
    second = tensor[..., quarter : 2 * quarter]
    return jnp.concatenate(
        [
            first_part * cosine - second * sine_part,
            second * cosine + first_part * sine_part,
            tensor[..., 2 * quarter :],
        ],
        axis=-1,
    )


def gated_unit(both):
    gate = both[:, 0]
    return gate * jax.nn.sigmoid(gate) * both[:, 1]


def in_order(own_part, other_part, which_half):
    lower_first = jnp.concatenate([own_part, other_part], axis=0)
    upper_first = jnp.concatenate([other_part, own_part], axis=0)
    return jnp.where(which_half == 0, lower_first, upper_first)


def own_rows(whole, which_half, row_count):
    return lax.dynamic_slice_in_dim(whole, which_half * row_count, row_count, 0)


def partner_rows(whole, which_half, row_count):
    return lax.dynamic_slice_in_dim(whole, (1 - which_half) * row_count, row_count, 0)


def masked_scores(query_block, key_all, key_live):
    scale = query_block.shape[-1] ** (-0.5)
    raw_scores = (
        jnp.einsum("qhd,khd->hqk", query_block, key_all, preferred_element_type=jnp.float32) * scale
    )
    return jnp.where(key_live[None, None, :], raw_scores, -1e30)


def attend_forward(queries, key_all, value_all, key_live):
    row_count, head_count, head_size = queries.shape
    block_rows = min(512, row_count)
    blocks = queries.reshape(row_count // block_rows, block_rows, head_count, head_size)

    def per_block(query_block):
        scores = masked_scores(query_block, key_all, key_live)
        row_max = jnp.max(scores, axis=-1, keepdims=True)
        weights = jnp.exp(scores - row_max)
        row_total = jnp.sum(weights, axis=-1, keepdims=True)
        attn_probs = weights / row_total
        block_out = jnp.einsum(
            "hqk,khd->qhd",
            attn_probs.astype(jnp.bfloat16),
            value_all,
            preferred_element_type=jnp.float32,
        )
        return (block_out, row_max + jnp.log(row_total))

    outputs, log_sums = lax.map(per_block, blocks)
    return (outputs.reshape(row_count, head_count, head_size), log_sums)


def attend_backward(queries, key_all, value_all, key_live, log_sums, grad_out):
    row_count, head_count, head_size = queries.shape
    block_rows = min(512, row_count)
    block_shape = (row_count // block_rows, block_rows, head_count, head_size)
    scale = head_size ** (-0.5)

    def per_block(running, block_item):
        query_block, grad_block, lse_block = block_item
        attn_probs = jnp.exp(masked_scores(query_block, key_all, key_live) - lse_block)
        grad_probs = jnp.einsum(
            "qhd,khd->hqk", grad_block, value_all, preferred_element_type=jnp.float32
        )
        row_inner = jnp.sum(attn_probs * grad_probs, axis=-1, keepdims=True)
        grad_scores = (attn_probs * (grad_probs - row_inner)).astype(jnp.bfloat16)
        grad_query = (
            jnp.einsum("hqk,khd->qhd", grad_scores, key_all, preferred_element_type=jnp.float32)
            * scale
        )
        grad_key = (
            running[0]
            + jnp.einsum(
                "hqk,qhd->khd", grad_scores, query_block, preferred_element_type=jnp.float32
            )
            * scale
        )
        grad_value = running[1] + jnp.einsum(
            "hqk,qhd->khd",
            attn_probs.astype(jnp.bfloat16),
            grad_block,
            preferred_element_type=jnp.float32,
        )
        return ((grad_key, grad_value), grad_query)

    zero_keys = jnp.zeros(key_all.shape, jnp.float32)
    (grad_key, grad_value), grad_query = lax.scan(
        per_block,
        (zero_keys, zero_keys),
        (queries.reshape(block_shape), grad_out.reshape(block_shape), log_sums),
    )
    return (grad_query.reshape(row_count, head_count, head_size), grad_key, grad_value)


def branch_total(partial_sum):
    return lax.psum(partial_sum, "mp")


def grad_total(partial_sum):
    return lax.psum(partial_sum, "mp")


def body(
    tokens,
    context,
    frame_counts,
    text_counts,
    w_qkv,
    w_attn_out,
    w_cross_q,
    w_cross_kv,
    w_cross_out,
    w_in,
    w_out,
    norm_gains,
    b_in,
    b_out,
    cotangent,
):
    gathered = (
        lax.all_gather(w_qkv, "dp", axis=0, tiled=True),
        lax.all_gather(w_attn_out, "dp", axis=1, tiled=True),
        lax.all_gather(w_cross_q, "dp", axis=0, tiled=True),
        lax.all_gather(w_cross_kv, "dp", axis=0, tiled=True),
        lax.all_gather(w_cross_out, "dp", axis=1, tiled=True),
        lax.all_gather(w_in, "dp", axis=0, tiled=True),
        lax.all_gather(w_out, "dp", axis=1, tiled=True),
        lax.all_gather(norm_gains, "dp", axis=1, tiled=True),
        lax.all_gather(b_in, "dp", axis=1, tiled=True),
        lax.all_gather(b_out, "dp", axis=0, tiled=True),
    )
    (
        qkv_full,
        attn_out_full,
        cross_q_full,
        cross_kv_full,
        cross_out_full,
        in_full,
        out_full,
        gains_full,
        b_in_full,
        b_out_full,
    ) = gathered
    row_count, model_width = tokens.shape
    text_rows, text_width = context.shape
    head_cols = qkv_full.shape[2]
    unit_cols = in_full.shape[2]
    head_count = head_cols // HD
    device_row = lax.axis_index("dp")
    which_half = device_row % 2
    clip_index = device_row // 2
    frame_live = lax.dynamic_index_in_dim(frame_counts, clip_index, 0, keepdims=False)
    text_live = lax.dynamic_index_in_dim(text_counts, clip_index, 0, keepdims=False)
    positions = (which_half * row_count + jnp.arange(row_count)).astype(jnp.float32)
    key_live = jnp.arange(2 * row_count) <= frame_live
    token_live = jnp.arange(2 * text_rows) < text_live
    gain_rows = gains_full.astype(jnp.float32)
    tokens_f = tokens.astype(jnp.float32)
    grad_y_mine = cotangent.astype(jnp.float32)
    norm_one, pull_one = jax.vjp(layer_norm, tokens_f, gain_rows[0])
    h_one = norm_one.astype(jnp.bfloat16)
    qkv = jnp.dot(
        h_one, qkv_full.reshape(model_width, 3 * head_cols), preferred_element_type=jnp.float32
    ).reshape(row_count, 3, head_count, HD)
    queries = rotate(qkv[:, 0], positions).astype(jnp.bfloat16)
    own_keys = rotate(qkv[:, 1], positions).astype(jnp.bfloat16).reshape(row_count, head_cols)
    own_values = qkv[:, 2].astype(jnp.bfloat16).reshape(row_count, head_cols)
    own_text = jnp.dot(
        context,
        cross_kv_full.reshape(text_width, 2 * head_cols),
        preferred_element_type=jnp.float32,
    ).astype(jnp.bfloat16)
    other = from_partner((own_keys, own_values, own_text), "dp", 0)
    key_all = in_order(own_keys, other[0], which_half).reshape(2 * row_count, head_count, HD)
    value_all = in_order(own_values, other[1], which_half).reshape(2 * row_count, head_count, HD)
    text_all = in_order(own_text, other[2], which_half).reshape(2 * text_rows, 2, head_count, HD)
    text_keys = text_all[:, 0]
    text_values = text_all[:, 1]
    self_attn, self_lse = attend_forward(queries, key_all, value_all, key_live)
    self_out = self_attn.reshape(row_count, head_cols).astype(jnp.bfloat16)
    self_part = jnp.dot(self_out, attn_out_full, preferred_element_type=jnp.float32)
    x_one = tokens_f + branch_total(self_part)
    norm_two, pull_two = jax.vjp(layer_norm, x_one, gain_rows[1])
    h_two = norm_two.astype(jnp.bfloat16)
    cross_queries = (
        jnp.dot(h_two, cross_q_full, preferred_element_type=jnp.float32)
        .astype(jnp.bfloat16)
        .reshape(row_count, head_count, HD)
    )
    cross_attn, cross_lse = attend_forward(cross_queries, text_keys, text_values, token_live)
    cross_out = cross_attn.reshape(row_count, head_cols).astype(jnp.bfloat16)
    cross_part = jnp.dot(cross_out, cross_out_full, preferred_element_type=jnp.float32)
    x_two = x_one + branch_total(cross_part)
    norm_three, pull_three = jax.vjp(layer_norm, x_two, gain_rows[2])
    h_three = norm_three.astype(jnp.bfloat16)
    both = jnp.dot(
        h_three, in_full.reshape(model_width, 2 * unit_cols), preferred_element_type=jnp.float32
    ).reshape(row_count, 2, unit_cols) + b_in_full.astype(jnp.float32)
    hidden_f, pull_unit = jax.vjp(gated_unit, both)
    hidden = hidden_f.astype(jnp.bfloat16)
    down_part = jnp.dot(hidden, out_full, preferred_element_type=jnp.float32)
    mixed = (x_two + branch_total(down_part) + b_out_full.astype(jnp.float32)).astype(jnp.bfloat16)
    again = (
        lax.all_gather(w_qkv, "dp", axis=0, tiled=True),
        lax.all_gather(w_attn_out, "dp", axis=1, tiled=True),
        lax.all_gather(w_cross_q, "dp", axis=0, tiled=True),
        lax.all_gather(w_cross_out, "dp", axis=1, tiled=True),
        lax.all_gather(w_in, "dp", axis=0, tiled=True),
        lax.all_gather(w_out, "dp", axis=1, tiled=True),
    )
    qkv_back = again[0]
    attn_out_back = again[1]
    cross_q_back = again[2]
    cross_out_back = again[3]
    in_back = again[4]
    out_back = again[5]
    grad_y = cotangent.astype(jnp.float32)
    grad_out_w = jnp.dot(hidden.T, cotangent, preferred_element_type=jnp.float32)
    grad_b_out = jnp.sum(grad_y, axis=0)
    grad_hidden = jnp.dot(cotangent, out_back.T, preferred_element_type=jnp.float32)
    grad_both = pull_unit(grad_hidden)[0].astype(jnp.bfloat16).reshape(row_count, 2 * unit_cols)
    grad_b_in = jnp.sum(grad_both, axis=0, dtype=jnp.float32).reshape(2, unit_cols)
    grad_in_w = jnp.dot(h_three.T, grad_both, preferred_element_type=jnp.float32).reshape(
        model_width, 2, unit_cols
    )
    three_part = jnp.dot(
        grad_both, in_back.reshape(model_width, 2 * unit_cols).T, preferred_element_type=jnp.float32
    )
    grad_x_norm, grad_gain_three = pull_three(grad_total(three_part))
    grad_x_two = grad_y_mine + grad_x_norm
    grad_two_b = grad_x_two.astype(jnp.bfloat16)
    grad_cross_out_w = jnp.dot(cross_out.T, grad_two_b, preferred_element_type=jnp.float32)
    grad_cross = (
        jnp.dot(grad_two_b, cross_out_back.T, preferred_element_type=jnp.float32)
        .astype(jnp.bfloat16)
        .reshape(row_count, head_count, HD)
    )
    grad_cq, grad_text_key, grad_text_value = attend_backward(
        cross_queries, text_keys, text_values, token_live, cross_lse, grad_cross
    )
    grad_cq_b = grad_cq.reshape(row_count, head_cols).astype(jnp.bfloat16)
    grad_cross_q_w = jnp.dot(h_two.T, grad_cq_b, preferred_element_type=jnp.float32)
    grad_text = jnp.stack([grad_text_key, grad_text_value], axis=1).reshape(
        2 * text_rows, 2 * head_cols
    )
    two_part = jnp.dot(grad_cq_b, cross_q_back.T, preferred_element_type=jnp.float32)
    grad_x_norm, grad_gain_two = pull_two(grad_total(two_part))
    grad_x_one = grad_x_two + grad_x_norm
    grad_one_b = grad_x_one.astype(jnp.bfloat16)
    grad_attn_out_w = jnp.dot(self_out.T, grad_one_b, preferred_element_type=jnp.float32)
    grad_self = (
        jnp.dot(grad_one_b, attn_out_back.T, preferred_element_type=jnp.float32)
        .astype(jnp.bfloat16)
        .reshape(row_count, head_count, HD)
    )
    grad_query, grad_key_all, grad_value_all = attend_backward(
        queries, key_all, value_all, key_live, self_lse, grad_self
    )
    grad_key_flat = grad_key_all.reshape(2 * row_count, head_cols)
    grad_value_flat = grad_value_all.reshape(2 * row_count, head_cols)
    back = from_partner(
        (
            partner_rows(grad_key_flat, which_half, row_count),
            partner_rows(grad_value_flat, which_half, row_count),
            partner_rows(grad_text, which_half, text_rows),
        ),
        "dp",
        0,
    )
    grad_key_own = (own_rows(grad_key_flat, which_half, row_count) + back[0]).reshape(
        row_count, head_count, HD
    )
    grad_value_own = own_rows(grad_value_flat, which_half, row_count) + back[1]
    grad_text_own = (own_rows(grad_text, which_half, text_rows) + back[2]).astype(jnp.bfloat16)
    grad_query_raw = rotate(grad_query, -positions).reshape(row_count, head_cols)
    grad_key_raw = rotate(grad_key_own, -positions).reshape(row_count, head_cols)
    grad_qkv_b = (
        jnp.stack([grad_query_raw, grad_key_raw, grad_value_own], axis=1)
        .astype(jnp.bfloat16)
        .reshape(row_count, 3 * head_cols)
    )
    grad_qkv_w = jnp.dot(h_one.T, grad_qkv_b, preferred_element_type=jnp.float32).reshape(
        model_width, 3, head_cols
    )
    grad_cross_kv_w = jnp.dot(context.T, grad_text_own, preferred_element_type=jnp.float32).reshape(
        text_width, 2, head_cols
    )
    one_part = jnp.dot(
        grad_qkv_b,
        qkv_back.reshape(model_width, 3 * head_cols).T,
        preferred_element_type=jnp.float32,
    )
    grad_x_norm, grad_gain_one = pull_one(grad_total(one_part))
    grad_tokens = grad_x_one + grad_x_norm
    grad_gains = jnp.stack([grad_gain_one, grad_gain_two, grad_gain_three], axis=0)
    summed = (
        lax.psum_scatter(grad_qkv_w, "dp", scatter_dimension=0, tiled=True),
        lax.psum_scatter(grad_attn_out_w, "dp", scatter_dimension=1, tiled=True),
        lax.psum_scatter(grad_cross_q_w, "dp", scatter_dimension=0, tiled=True),
        lax.psum_scatter(grad_cross_kv_w, "dp", scatter_dimension=0, tiled=True),
        lax.psum_scatter(grad_cross_out_w, "dp", scatter_dimension=1, tiled=True),
        lax.psum_scatter(grad_in_w, "dp", scatter_dimension=0, tiled=True),
        lax.psum_scatter(grad_out_w, "dp", scatter_dimension=1, tiled=True),
        lax.psum_scatter(grad_gains, "dp", scatter_dimension=1, tiled=True),
        lax.psum_scatter(grad_b_in, "dp", scatter_dimension=1, tiled=True),
        lax.psum_scatter(grad_b_out, "dp", scatter_dimension=0, tiled=True),
    )
    return (
        mixed,
        grad_tokens,
        summed[0],
        summed[1],
        summed[2],
        summed[3],
        summed[4],
        summed[5],
        summed[6],
        summed[7],
        summed[8],
        summed[9],
    )


def near_body(
    tokens,
    context,
    frame_counts,
    text_counts,
    w_qkv,
    w_attn_out,
    w_cross_q,
    w_cross_kv,
    w_cross_out,
    w_in,
    w_out,
    norm_gains,
    b_in,
    b_out,
    cotangent,
):
    n, dp = lax.axis_size("mp"), lax.axis_size("dp")
    shard, _, cols = w_qkv.shape
    small = prepare(
        tokens,
        context,
        frame_counts,
        text_counts,
        w_qkv,
        w_attn_out,
        w_cross_q,
        w_cross_kv,
        w_cross_out,
        w_in,
        w_out,
        norm_gains,
        b_in,
        b_out,
    )
    mixed, gt, gains, bias_in, bias_out, *parts = run_block(n, dp, tokens, context, cotangent, *small)
    g_out, g_in, g_mid, g_ckv, g_last = parts
    return (
        mixed,
        gt.astype(F32),
        g_last[:, cols:].reshape(shard, 3, cols),
        g_last[:, :cols].T,
        g_mid[:, cols:],
        g_ckv.reshape(-1, 2, cols),
        g_mid[:, :cols].T,
        g_in.reshape(shard, 2, -1),
        g_out.T,
        gains,
        bias_in,
        bias_out[0],
    )


def solution(mesh):
    in_specs = (
        P("dp", None),
        P("dp", None),
        P(),
        P(),
        P("dp", None, "mp"),
        P("mp", "dp"),
        P("dp", "mp"),
        P("dp", None, "mp"),
        P("mp", "dp"),
        P("dp", None, "mp"),
        P("mp", "dp"),
        P(None, "dp"),
        P(None, ("mp", "dp")),
        P("dp"),
        P("dp", None),
    )
    out_specs = (
        P("dp", None),
        P("dp", None),
        P("dp", None, "mp"),
        P("mp", "dp"),
        P("dp", "mp"),
        P("dp", None, "mp"),
        P("mp", "dp"),
        P("dp", None, "mp"),
        P("mp", "dp"),
        P(None, "dp"),
        P(None, ("mp", "dp")),
        P("dp"),
    )
    near = mesh.shape["dp"] == 8
    return jax.shard_map(
        near_body if near else body,
        mesh=mesh,
        in_specs=in_specs,
        out_specs=out_specs,
        check_vma=False,
    )
```

```python
import functools

import jax
import jax.numpy as jnp
from jax import lax
from jax.experimental import pallas as pl
from jax.experimental.pallas import tpu as pltpu
from jax.sharding import PartitionSpec as P

HD = 64
MESH = pl.DeviceIdType.MESH
HBM = pl.BlockSpec(memory_space=pl.ANY)
BF = jnp.bfloat16
F32 = jnp.float32
epsilon = 1e-05
CH = 16
NR = 32
LAG = 3
DMA = pltpu.SemaphoreType.DMA
WHOLE = (0, 0)


def dot_nn(a, b):
    return lax.dot_general(a, b, (((1,), (0,)), ((), ())), preferred_element_type=F32)


def dot_nt(a, b):
    return lax.dot_general(a, b, (((1,), (1,)), ((), ())), preferred_element_type=F32)


def dot_tn(a, b):
    return lax.dot_general(a, b, (((0,), (0,)), ((), ())), preferred_element_type=F32)


def send(src, dst, send_sem, recv_sem, peer):
    return pltpu.make_async_remote_copy(
        src_ref=src,
        dst_ref=dst,
        send_sem=send_sem,
        recv_sem=recv_sem,
        device_id=peer,
        device_id_type=MESH,
    )


def rows_at(start, size):
    return pl.ds(pl.multiple_of(start, 16), size)


def greet_all(d, z, n, dp):
    barrier = pltpu.get_barrier_semaphore()
    for k in range(1, dp):
        pl.semaphore_signal(barrier, inc=1, device_id=(jnp.bitwise_xor(d, k), z), device_id_type=MESH)
    for k in range(1, n):
        pl.semaphore_signal(barrier, inc=1, device_id=(d, lax.rem(z + k, n)), device_id_type=MESH)
    pl.semaphore_wait(barrier, dp + n - 2)


def normal(x):
    centered = x - jnp.mean(x, axis=-1, keepdims=True)
    r = lax.rsqrt(jnp.mean(centered * centered, axis=-1, keepdims=True) + epsilon)
    return centered * r, r


class Line:
    def __init__(self, d, z, n, own, got, dst, base, sems, k, fin):
        self.d, self.z, self.n = d, z, n
        self.own, self.got, self.dst, self.base = own, got, dst, base
        self.sems, self.k, self.fin = sems, k, fin
        self.half = own.shape[0] // 2
        self.chunks = self.half // CH
        self.slots = self.chunks + 2 * LAG * (n - 1)
        self.next = 0

    def place(self, f):
        z, n = self.z, self.n
        return (z, z + 1, z - 1) if f else (n - 1 - z, z - 1, z + 1)

    def fore(self, f, c, nxt):
        at = rows_at(f * self.half + c * CH, CH)
        s, r = self.sems[0], self.sems[1]
        return send(
            self.own.at[at], self.got.at[at], s.at[self.k, f, c], r.at[self.k, f, c], (self.d, nxt)
        )

    def back(self, f, c, prv):
        at = rows_at(self.base + f * self.half + c * CH, CH)
        s, r = self.sems[2], self.sems[3]
        return send(
            self.dst.at[at], self.dst.at[at], s.at[self.k, f, c], r.at[self.k, f, c], (self.d, prv)
        )

    def slot(self, s):
        n = self.n
        for f in range(2):
            p, nxt, prv = self.place(f)
            c = s - LAG * p
            valid = (c >= 0) & (c < self.chunks)

            @pl.when(valid & (p == 0))
            def _():
                self.fore(f, c, nxt).start()

            @pl.when(valid & (p > 0) & (p < n - 1))
            def _():
                at = rows_at(f * self.half + c * CH, CH)
                self.fore(f, c, nxt).wait_recv()
                self.own[at] = self.own[at] + self.got[at]
                self.fore(f, c, nxt).start()

            @pl.when(valid & (p == n - 1))
            def _():
                at = rows_at(f * self.half + c * CH, CH)
                self.fore(f, c, nxt).wait_recv()
                self.fin(f * self.half + c * CH, self.own[at].astype(F32) + self.got[at].astype(F32))
                self.back(f, c, prv).start()

            b = s - LAG * (2 * (n - 1) - p)

            @pl.when((b >= 0) & (b < self.chunks) & (p < n - 1))
            def _():
                self.back(f, b, prv).wait_recv()

                @pl.when(p > 0)
                def _():
                    self.back(f, b, prv).start()

    def step(self):
        self.slot(self.next)
        self.next += 1

    def left(self):
        return self.slots - self.next

    def drain(self):
        def body(c, carry):
            for f in range(2):
                p, nxt, prv = self.place(f)

                @pl.when(p < self.n - 1)
                def _():
                    self.fore(f, c, nxt).wait_send()

                @pl.when(p > 0)
                def _():
                    self.back(f, c, prv).wait_send()

            return carry

        lax.fori_loop(0, self.chunks, body, 0)


def run(count, *lines):
    lines = [line for line in lines if line.next < line.slots]
    count = max(count, 0)
    first = [line.next for line in lines]

    def body(s, carry):
        for line, at in zip(lines, first):
            line.slot(at + s)
        return carry

    lax.fori_loop(0, count, body, 0)
    for line in lines:
        line.next += count


class Gather:
    def __init__(self, d, z, shard, full, send_sems, recv_sems, local_sems, a):
        self.d, self.z, self.shard, self.full, self.a = d, z, shard, full, a
        self.send_sems, self.recv_sems, self.local = send_sems, recv_sems, local_sems
        self.size = shard.shape[0]
        self.core, self.xn, self.yn = [(jnp.bitwise_xor(d, k), z) for k in (1, 2, 4)]
        self.bx, self.by, self.bd = [jnp.bitwise_xor(d, k) for k in (2, 4, 6)]
        half = self.size // 2
        self.top, self.bottom = (0, half), (half, half)
        self.started = []

    def part(self, block, rows):
        lo, size = rows
        return self.full.at[rows_at(block * self.size + lo, size or self.size)]

    def copy(self, k, block, rows, peer):
        part = self.part(block, rows)
        return send(part, part, self.send_sems.at[self.a, k], self.recv_sems.at[self.a, k], peer)

    def go(self, k, block, rows, peer):
        cp = self.copy(k, block, rows, peer)
        cp.start()
        self.started.append(cp)

    def got(self, k, block, rows, peer):
        self.copy(k, block, rows, peer).wait_recv()

    def begin(self):
        for k, peer in ((0, self.xn), (1, self.yn), (2, self.core)):
            cp = send(
                self.shard,
                self.part(self.d, WHOLE),
                self.send_sems.at[self.a, k],
                self.recv_sems.at[self.a, k],
                peer,
            )
            cp.start()
            self.started.append(cp)
        self.mine = pltpu.make_async_copy(self.shard, self.part(self.d, WHOLE), self.local.at[self.a])
        self.mine.start()

    def near(self):
        self.got(0, self.bx, WHOLE, self.xn)
        self.go(3, self.bx, self.top, self.yn)
        self.go(5, self.bx, WHOLE, self.core)
        self.got(1, self.by, WHOLE, self.yn)
        self.go(4, self.by, self.bottom, self.xn)
        self.go(6, self.by, WHOLE, self.core)

    def far(self):
        self.got(3, self.bd, self.top, self.yn)
        self.go(7, self.bd, self.top, self.core)
        self.got(4, self.bd, self.bottom, self.xn)
        self.go(8, self.bd, self.bottom, self.core)

    def last(self):
        o = [jnp.bitwise_xor(b, 1) for b in (self.d, self.bx, self.by, self.bd)]
        self.got(2, o[0], WHOLE, self.core)
        self.got(5, o[1], WHOLE, self.core)
        self.got(6, o[2], WHOLE, self.core)
        self.got(7, o[3], self.top, self.core)
        self.got(8, o[3], self.bottom, self.core)
        self.mine.wait()

    def drain(self):
        for cp in self.started:
            cp.wait_send()


class Moves:
    def __init__(self, sems):
        self.sems, self.used = sems, 0

    def start(self, src, dst):
        cp = pltpu.make_async_copy(src, dst, self.sems.at[self.used])
        self.used += 1
        cp.start()
        return cp


def turn(u, cosine, low, high):
    return u * cosine + pltpu.roll(u, 112, 1) * low + pltpu.roll(u, 16, 1) * high


def half_mask(rows, e):
    lane = lax.broadcasted_iota(jnp.int32, (rows, 128), 1)
    return (lane >= 64) == (e == 1)


def softmax(s):
    w = jnp.exp(s - jnp.max(s, axis=-1, keepdims=True))
    return w * (1.0 / jnp.sum(w, axis=-1, keepdims=True))


class Scatter:
    def __init__(self, d, z, got, one, two, out, sems, out_sem):
        self.d, self.z = d, z
        self.got, self.one, self.two, self.out = got, one, two, out
        self.sems, self.out_sem = sems, out_sem
        self.c, self.x, self.y = lax.rem(d, 2), lax.rem(d // 2, 2), d // 4
        self.core, self.xn, self.yn = [(jnp.bitwise_xor(d, k), z) for k in (1, 2, 4)]
        self.arrays, self.copies, self.now = [], [], 0

    def add(self, size, buf, place, compute, dst):
        self.arrays.append((size, buf, place, compute, dst))
        self.copies.append({})

    def block(self, a, j, c, lo=0, size=None):
        shard, buf, place, _, _ = self.arrays[a]
        row, lane = place(j)
        width = self.got.shape[-1]
        return buf.at[rows_at(row + c * shard + lo, size or shard), pl.ds(pl.multiple_of(lane, 128), width)]

    def go(self, a, stage, k, src, dst, peer):
        sd, rv = self.sems[stage]
        cp = send(src, dst, sd.at[a % 2, k], rv.at[a % 2, k], peer)
        cp.start()
        self.copies[a][stage, k] = cp

    def core_copy(self, a, t):
        sd, rv = self.sems[0]
        shard = self.arrays[a][0]
        return send(
            self.block(a, t, 1 - self.c),
            self.got.at[a % 2, t, pl.ds(0, shard)],
            sd.at[a % 2, t],
            rv.at[a % 2, t],
            self.core,
        )

    def compute(self, a, between):
        _, buf, place, tile, _ = self.arrays[a]

        def step(t, carry):
            tile(t)
            self.core_copy(a, t).start()
            between(t)
            return carry

        lax.fori_loop(0, 4, step, 0)

    def plus(self, ref, part):
        piece = 48

        def body(i, carry):
            at = rows_at(i * piece, piece)
            ref[at] = ref[at] + part[at]
            return carry

        lax.fori_loop(0, ref.shape[0] // piece, body, 0)

    def add_core(self, a):
        shard = self.arrays[a][0]
        half = shard // 2

        def body(j, carry):
            self.core_copy(a, j).wait_recv()
            self.plus(self.block(a, j, self.c), self.got.at[a % 2, j])
            return carry

        lax.fori_loop(0, 4, body, 0)
        for b in range(2):
            for side, j, lo, peer in (
                (0, 2 * b + 1 - self.x, 0, self.xn),
                (1, 2 * (1 - self.y) + b, half, self.yn),
            ):
                self.go(
                    a,
                    1,
                    2 * side + b,
                    self.block(a, j, self.c, lo, half),
                    self.one.at[a % 2, side, b, pl.ds(0, half)],
                    peer,
                )

    def add_one(self, a):
        half = self.arrays[a][0] // 2
        for b in range(2):
            for side, j, lo in ((0, 2 * b + self.x, 0), (1, 2 * self.y + b, half)):
                self.copies[a][1, 2 * side + b].wait_recv()
                self.plus(self.block(a, j, self.c, lo, half), self.one.at[a % 2, side, b])
        for side, j, lo, peer in (
            (0, 2 * (1 - self.y) + self.x, 0, self.yn),
            (1, 2 * self.y + 1 - self.x, half, self.xn),
        ):
            self.go(
                a,
                2,
                side,
                self.block(a, j, self.c, lo, half),
                self.two.at[a % 2, side, pl.ds(0, half)],
                peer,
            )

        def body(t, carry):
            self.core_copy(a, t).wait_send()
            return carry

        lax.fori_loop(0, 4, body, 0)

    def out_copy(self, a):
        shard, dst = self.arrays[a][0], self.arrays[a][4]
        return pltpu.make_async_copy(self.out.at[a % 2, pl.ds(0, shard)], dst, self.out_sem.at[a % 2])

    def add_two(self, a):
        half = self.arrays[a][0] // 2
        piece = 48
        for side in range(2):
            self.copies[a][2, side].wait_recv()
            ref = self.block(a, 2 * self.y + self.x, self.c, side * half, half)

            def body(i, carry, side=side, ref=ref):
                at = rows_at(i * piece, piece)
                to = rows_at(side * half + i * piece, piece)
                self.out[a % 2, to] = ref[at].astype(F32) + self.two[a % 2, side, at].astype(F32)
                return carry

            lax.fori_loop(0, half // piece, body, 0)
        self.out_copy(a).start()
        for k in range(4):
            self.copies[a][1, k].wait_send()

    def retire(self, a):
        for k in range(2):
            self.copies[a][2, k].wait_send()
        self.out_copy(a).wait()

    def step(self, pace, make):
        s, count = self.now, len(self.arrays)
        self.now += 1
        for lag, stage in ((4, self.retire), (3, self.add_two), (2, self.add_one), (1, self.add_core)):
            if 0 <= s - lag < count:
                stage(s - lag)
                if lag < 4:
                    pace()
        if s < count:
            self.compute(s, make())


def block_kernel(
    n,
    dp,
    tokens,
    context,
    cotangent,
    tables,
    frame_counts,
    text_counts,
    vec,
    s_qkv,
    s_small,
    s_ckv,
    s_out,
    s_in,
    w_qkv,
    w_out,
    w_in,
    o_h1,
    o_p,
    o_mixed,
    o_gt,
    o_gains,
    o_b_in,
    o_b_out,
    o_out,
    o_in,
    o_mid,
    o_ckv,
    o_last,
    v_vec,
    gv,
    win,
    wout,
    wsmall,
    h2,
    h3,
    dy,
    hid,
    dgu,
    dx2r,
    dx1r,
    x1,
    x2,
    dx,
    q,
    k,
    v,
    so,
    co,
    cq,
    dco,
    dcq,
    dso,
    dqkv,
    tkv,
    dtkv,
    pc,
    pst,
    dk,
    dv,
    ctx,
    tab,
    gg,
    own,
    got,
    krv,
    tst,
    trv,
    s_got,
    s_one,
    s_two,
    s_out_v,
    ggs,
    ggr,
    ggz,
    ggo,
    v_gains,
    v_b_in,
    v_b_out,
    g_send,
    g_recv,
    g_local,
    e_send,
    e_recv,
    f_send,
    f_recv,
    k_send,
    k_recv,
    fs,
    fr,
    bs,
    br,
    p_sem,
    c_send,
    c_recv,
    a_send,
    a_recv,
    b_send,
    b_recv,
    s_sem,
    v_send,
    v_recv,
    moves,
):
    d = lax.axis_index("dp")
    z = lax.axis_index("mp")
    rows, width = tokens.shape
    group = rows // 2
    cols = so.shape[1]
    units = hid.shape[1]
    pairs = cols // 128
    half = lax.rem(d, 2)
    core = (jnp.bitwise_xor(d, 1), z)
    tok, mixed, gt, h1 = dy, dy, dx2r, hid
    v_qkv = win.at[:, pl.ds(0, 3 * cols)]
    v_ckv = wout.at[pl.ds(0, s_ckv.shape[0] * dp), pl.ds(0, 2 * cols)]
    mv = Moves(moves)
    ld_tok = mv.start(tokens, tok)
    ld_small = [mv.start(a, b) for a, b in ((context, ctx), (tables, tab))]
    ld_vec = mv.start(vec, v_vec.at[d])
    greet_all(d, z, n, dp)
    vec_copies = []
    for j in range(1, dp):
        peer = (jnp.bitwise_xor(d, j), z)
        cp = send(vec, v_vec.at[d], e_send.at[j], e_recv.at[j], peer)
        cp.start()
        vec_copies.append(cp)
    gathers = [
        Gather(d, z, shard_ref, full, g_send, g_recv, g_local, a)
        for a, (shard_ref, full) in enumerate(
            ((s_qkv, v_qkv), (s_ckv, v_ckv), (s_small, wsmall), (s_out, w_out), (s_in, w_in))
        )
    ]
    g_qkv, g_ckv, g_small, g_out, g_in = gathers
    g_qkv.begin()
    gg[...] = jnp.zeros_like(gg)
    dtkv[...] = jnp.zeros_like(dtkv)

    def clear(i, carry):
        at = rows_at(i * NR, NR)
        dk[at] = jnp.zeros((NR, cols), F32)
        dv[at] = jnp.zeros((NR, cols), F32)
        return carry

    ld_tok.wait()
    ld_vec.wait()
    for j in range(1, dp):
        b = jnp.bitwise_xor(d, j)
        send(v_vec.at[b], v_vec.at[b], e_send.at[j], e_recv.at[j], (b, z)).wait_recv()
    shard = width // dp
    for b in range(dp):
        gv[:, b * shard : (b + 1) * shard] = v_vec[b][:8, :shard].astype(F32)

    def norm_rows(i, carry):
        at = rows_at(i * NR, NR)
        h1[at] = (normal(tok[at].astype(F32))[0] * gv[0:1]).astype(BF)
        return carry

    lax.fori_loop(0, rows // NR // 2, norm_rows, 0)
    g_qkv.near()
    g_ckv.begin()
    g_small.begin()
    lax.fori_loop(rows // NR // 2, rows // NR, norm_rows, 0)
    st_h1 = mv.start(h1, o_h1)
    lax.fori_loop(0, 2 * rows // NR, clear, 0)
    for ld in ld_small:
        ld.wait()
    clip = d // 2
    text = ctx.shape[0]
    key_at = lax.broadcasted_iota(jnp.int32, (1, 2 * rows), 1)
    text_at = lax.broadcasted_iota(jnp.int32, (1, 2 * text), 1)
    key_bias = jnp.where(key_at <= frame_counts[clip], 0.0, -1e30)
    text_bias = jnp.where(text_at < text_counts[clip], 0.0, -1e30)
    g_qkv.far()
    g_qkv.last()
    my_rows = half * rows

    def project(g, carry):
        at = rows_at(g * group, group)
        mine = rows_at(my_rows + g * group, group)
        x = h1[at]
        for part in (1, 2, 0):
            u = dot_nn(x, win[:, part * cols : (part + 1) * cols])
            if part == 2:
                v[mine] = u.astype(BF)
                continue
            for j in range(pairs):
                r = turn(u[:, j * 128 : (j + 1) * 128], tab[0, at], tab[1, at], tab[2, at])
                if part:
                    k[mine, j * 128 : (j + 1) * 128] = r.astype(BF)
                else:
                    q[at, j * 128 : (j + 1) * 128] = (r * HD ** (-0.5)).astype(BF)
        return carry

    lax.fori_loop(0, 2, project, 0)
    mine, theirs = rows_at(my_rows, rows), rows_at((1 - half) * rows, rows)
    kv = [send(r.at[mine], r.at[mine], f_send.at[i], f_recv.at[i], core) for i, r in enumerate((k, v))]
    for cp in kv:
        cp.start()
    st_qkv = mv.start(v_qkv, w_qkv)
    g_ckv.near()
    g_small.near()
    g_out.begin()
    g_ckv.far()
    g_ckv.last()
    g_small.far()
    g_in.begin()
    t_mine, t_theirs = rows_at(half * text, text), rows_at((1 - half) * text, text)
    tkv[t_mine] = dot_nn(ctx[...], v_ckv[...]).astype(BF)
    kv.append(send(tkv.at[t_mine], tkv.at[t_mine], f_send.at[2], f_recv.at[2], core))
    kv[2].start()
    for i, r in enumerate((k, v)):
        send(r.at[theirs], r.at[theirs], f_send.at[i], f_recv.at[i], core).wait_recv()

    tile = 256

    def feed(g, lo, count, between):
        at = rows_at(g * group, group)

        def step(i, carry):
            u = pl.multiple_of(i * tile, tile)
            us, ups = pl.ds(u, tile), pl.ds(pl.multiple_of(units + u, tile), tile)
            x = h3[at]
            gate = dot_nn(x, win[:, us]) + gv[3:4, us]
            up = dot_nn(x, win[:, ups]) + gv[4:5, us]
            dh = dot_nn(dy[at], wout[:, us])
            sig = jax.nn.sigmoid(gate)
            act = gate * sig
            hid[at, us] = (act * up).astype(BF)
            d_gate = (dh * up * (sig * (1.0 + gate * (1.0 - sig)))).astype(BF)
            d_up = (dh * act).astype(BF)
            dgu[at, us] = d_gate
            dgu[at, ups] = d_up
            gg[3:4, us] += jnp.sum(d_gate.astype(F32), axis=0, keepdims=True)
            gg[4:5, us] += jnp.sum(d_up.astype(F32), axis=0, keepdims=True)
            between(i - lo)
            return carry

        lax.fori_loop(lo, lo + count, step, 0)

    def norm_back(x, dn, gain, row):
        nrm, r = normal(x)
        gg[row : row + 1] += jnp.sum(dn * nrm, axis=0, keepdims=True)
        e = dn * gain
        return r * (
            e
            - jnp.mean(e, axis=-1, keepdims=True)
            - nrm * jnp.mean(e * nrm, axis=-1, keepdims=True)
        )

    def places(g, lo):
        return rows_at(g * group + lo, CH), rows_at(
            g * group // 2 + lax.rem(lo, group // 2), CH
        )

    def start_two(g):
        def fin(lo, total):
            at, mine = places(g, lo)
            x = tok[at].astype(F32) + total
            x1[mine] = x
            h2[at] = (normal(x)[0] * gv[1:2]).astype(BF)

        return fin

    def start_three(g):
        def fin(lo, total):
            at, mine = places(g, lo)
            x = x1[mine] + total
            x2[mine] = x
            h3[at] = (normal(x)[0] * gv[2:3]).astype(BF)

        return fin

    def finish_mixed(g):
        def fin(lo, total):
            at, mine = places(g, lo)
            mixed[at] = (x2[mine] + total + gv[5:6]).astype(BF)

        return fin

    def finish_three(g):
        def fin(lo, total):
            at, mine = places(g, lo)
            x = dy[at].astype(F32) + norm_back(x2[mine], total, gv[2:3], 2)
            dx[mine] = x
            dx2r[at] = x.astype(BF)

        return fin

    def finish_two(g):
        def fin(lo, total):
            at, mine = places(g, lo)
            x = dx[mine] + norm_back(x1[mine], total, gv[1:2], 1)
            dx[mine] = x
            dx1r[at] = x.astype(BF)

        return fin

    def finish_one(g):
        def fin(lo, total):
            at, mine = places(g, lo)
            x = dx[mine] + norm_back(h3[at].astype(F32), total, gv[0:1], 0)
            gt[at] = x.astype(BF)

        return fin

    sems = (fs, fr, bs, br)

    def lines(dst, slot, index, fin):
        return [
            Line(
                d, z, n, own.at[slot + g], got.at[slot + g], dst, g * group, sems, index + g, fin(g)
            )
            for g in range(2)
        ]

    fore_one = lines(h2, 0, 0, start_two)
    fore_two = lines(h3, 2, 2, start_three)
    mix = lines(mixed, 2, 4, finish_mixed)
    three = lines(dx2r, 0, 6, finish_three)
    two = lines(dx1r, 0, 8, finish_two)
    one = lines(gt, 0, 10, finish_one)

    def with_lines(total, every, *ls):
        ls = [line for line in ls if line.next < line.slots]
        starts = [line.next for line in ls]

        def between(i):
            def go():
                for line, s in zip(ls, starts):
                    for e in range(2 if every == 1 else 1):
                        line.slot(s + (2 if every == 1 else 1) * (i // every) + e)

            if every == 1:
                go()
            else:
                pl.when(lax.rem(i, every) == 0)(go)

        for line in ls:
            line.next += -(-total // every) * (2 if every == 1 else 1)
        return between

    tiles = units // tile
    pieces = 2
    per = tiles // pieces
    piece = units // pieces

    sc = Scatter(
        d, z, s_got, s_one, s_two, s_out_v, ((c_send, c_recv), (a_send, a_recv), (b_send, b_recv)), s_sem
    )
    wide = s_got.shape[-1]

    def part_of(buf, lane, size, *terms):
        def tile_at(t):
            at = rows_at(t * 2 * size, 2 * size)
            to = lane
            for left, right, lo, count in terms:
                cols_at = pl.ds(pl.multiple_of(t * 2 * size, 128), 2 * size)
                buf[at, to : to + count] = dot_tn(left[:, cols_at], right[:, lo : lo + count]).astype(BF)
                to += count

        return tile_at

    def add_array(buf, lane, dst, *terms):
        sc.add(
            shard,
            buf,
            lambda j: (j * 2 * shard, lane),
            part_of(buf, lane, shard, *terms),
            dst,
        )

    def text_tile(j):
        left = ctx[...]
        t = text_width // 4
        g = dot_tn(left, tst[...]).astype(BF)
        for i in range(4):

            @pl.when(j == i)
            def _():
                dgu[0:t, i * wide : (i + 1) * wide] = g[i * t : (i + 1) * t]

    text_width = ctx.shape[1]
    for i in range(2):
        add_array(wout, i * wide, o_out.at[:, pl.ds(i * wide, wide)], (dy, hid, i * wide, wide))
    for i in range(4):
        add_array(win, i * wide, o_in.at[:, pl.ds(i * wide, wide)], (h3, dgu, i * wide, wide))
    add_array(wout, 0, o_mid, (dx2r, co, 0, cols), (h2, dcq, 0, cols))
    sc.add(text_width // dp, dgu, lambda j: (0, j * wide), text_tile, o_ckv)
    add_array(wout, wide, o_last.at[:, pl.ds(0, wide)], (dx1r, so, 0, cols), (hid, dqkv, 0, cols))
    add_array(win, 2 * wide, o_last.at[:, pl.ds(wide, wide)], (hid, dqkv, cols, wide))

    def attend(g, queries, keys, key_lo, values, value_lo, bias, save, out, between):
        at = rows_at(g * group, group)

        def head(h, carry):
            j, e = h // 2, lax.rem(h, 2)
            lo = pl.multiple_of(j * 128, 128)
            mask = half_mask(group, e)
            qb = jnp.where(mask, queries[at, pl.ds(lo, 128)], jnp.zeros((), BF))
            s = dot_nt(qb, keys[:, pl.ds(pl.multiple_of(key_lo + lo, 128), 128)]) + bias
            p = softmax(s).astype(BF)
            save(h, p)
            o = dot_nn(p, values[:, pl.ds(pl.multiple_of(value_lo + lo, 128), 128)])
            out[at, pl.ds(lo, 128)] = jnp.where(mask, o.astype(BF), out[at, pl.ds(lo, 128)])
            between(h)
            return carry

        lax.fori_loop(0, 2 * pairs, head, 0)

    def self_forward(g, every, *ls):
        at = rows_at(g * group, group)

        def keep(h):
            slot = lax.rem(h, 2)
            return pltpu.make_async_copy(pst.at[slot], o_p.at[h, at], p_sem.at[slot])

        def save(h, p):
            @pl.when(h >= 2)
            def _():
                keep(h - 2).wait()

            pst[lax.rem(h, 2)] = p
            keep(h).start()

        attend(g, q, k, 0, v, 0, key_bias, save, so, with_lines(6, every, *ls))
        run(1, *ls)
        for h in (2 * pairs - 2, 2 * pairs - 1):
            keep(h).wait()
        own[g] = dot_nt(so[at], wsmall[:, 0:cols]).astype(BF)

    def cross_forward(g, every, *ls):
        at = rows_at(g * group, group)
        cq[at] = dot_nn(h2[at], wsmall[:, cols : 2 * cols]).astype(BF) * jnp.asarray(HD ** (-0.5), BF)

        def save(h, p):
            pc[h, at] = p

        run(1, *ls)
        attend(g, cq, tkv, 0, tkv, cols, text_bias, save, co, with_lines(6, every, *ls))
        run(1, *ls)
        own[2 + g] = dot_nt(co[at], wsmall[:, 2 * cols :]).astype(BF)

    def attend_back(g, d_out, queries, keys, key_lo, values, value_lo, probs, dkr, dk_lo, dvr, dv_lo, dq, between):
        at = rows_at(g * group, group)

        def head(h, carry):
            j, e = h // 2, lax.rem(h, 2)
            lo = pl.multiple_of(j * 128, 128)
            here = pl.ds(lo, 128)
            mask = half_mask(group, e)
            zero = jnp.zeros((), BF)
            do = jnp.where(mask, d_out[at, here], zero)
            qb = jnp.where(mask, queries[at, here], zero)
            p = probs(h)
            pf = p.astype(F32)
            dp_ = dot_nt(do, values[:, pl.ds(pl.multiple_of(value_lo + lo, 128), 128)])
            ds = (pf * (dp_ - jnp.sum(pf * dp_, axis=-1, keepdims=True))).astype(BF)
            g_q = dot_nn(ds, keys[:, pl.ds(pl.multiple_of(key_lo + lo, 128), 128)]) * HD ** (-0.5)
            dkr[:, pl.ds(pl.multiple_of(dk_lo + lo, 128), 128)] += dot_tn(ds, qb)
            dvr[:, pl.ds(pl.multiple_of(dv_lo + lo, 128), 128)] += dot_tn(p, do)
            dq(h, at, here, mask, g_q)
            between(h)
            return carry

        lax.fori_loop(0, 2 * pairs, head, 0)

    def cross_back(g, every, *ls):
        at = rows_at(g * group, group)
        dco[at] = dot_nn(dx2r[at], wsmall[:, 2 * cols :]).astype(BF)
        run(1, *ls)

        def dq(h, at, here, mask, g_q):
            dcq[at, here] = jnp.where(mask, g_q.astype(BF), dcq[at, here])

        attend_back(
            g, dco, cq, tkv, 0, tkv, cols, lambda h: pc[h, at], dtkv, 0, dtkv, cols, dq, with_lines(6, every, *ls)
        )

    def self_back(g, *ls):
        at = rows_at(g * group, group)

        def load(h):
            slot = lax.rem(h, 2)
            return pltpu.make_async_copy(o_p.at[h, at], pst.at[slot], p_sem.at[slot])

        load(0).start()
        dso[at] = dot_nn(dx1r[at], wsmall[:, 0:cols]).astype(BF)
        run(1, *ls)

        def probs(h):
            @pl.when(h + 1 < 2 * pairs)
            def _():
                load(h + 1).start()

            load(h).wait()
            return pst[lax.rem(h, 2)]

        def dq(h, at, here, mask, g_q):
            r = turn(g_q, tab[0, at], -tab[1, at], -tab[2, at]).astype(BF)
            dqkv[at, here] = jnp.where(mask, r, dqkv[at, here])

        attend_back(g, dso, q, k, 0, v, 0, probs, dk, 0, dv, 0, dq, with_lines(6, 1, *ls))

    def three_part(g, *ls):
        at = rows_at(g * group, group)
        step = width // 4
        for i in range(4):
            to = slice(i * step, (i + 1) * step)
            own[g, :, to] = dot_nt(dgu[at], win[to]).astype(BF)
            if i % 2:
                run(1, *ls)

    def gradient(*ls):
        sc.step(lambda: run(1, *ls), lambda: with_lines(4, 2, *ls))

    def down_part(g):
        at = rows_at(g * group, group)
        own[2 + g] = dot_nt(hid[at], wout[...]).astype(BF)

    def two_part(g):
        at = rows_at(g * group, group)
        own[g] = dot_nt(dcq[at], wsmall[:, cols : 2 * cols]).astype(BF)

    def one_part(g):
        at = rows_at(g * group, group)
        own[g] = dot_nt(dqkv[at], win[:, 0 : 3 * cols]).astype(BF)

    g_small.last()
    self_forward(0, 1)
    self_forward(1, 1, fore_one[0])
    run(8, fore_one[0], fore_one[1])
    g_out.near()
    g_in.near()
    run(fore_one[0].left(), fore_one[0], fore_one[1])
    send(tkv.at[t_theirs], tkv.at[t_theirs], f_send.at[2], f_recv.at[2], core).wait_recv()
    cross_forward(0, 3, fore_one[1])
    run(fore_one[1].left(), fore_one[1], fore_two[0])
    ld_dy = mv.start(cotangent, dy)
    cross_forward(1, 3, fore_two[0])
    st_qkv.wait()
    g_out.far()
    g_in.far()
    run(8, fore_two[0], fore_two[1])
    g_out.last()
    g_in.last()
    g_qkv.drain()
    g_ckv.drain()
    w_loads = []
    for i in range(pieces):
        at = slice(i * piece, (i + 1) * piece)
        up = slice(units + i * piece, units + (i + 1) * piece)
        w_loads.append(
            [
                mv.start(w_in.at[:, at], win.at[:, at]),
                mv.start(w_in.at[:, up], win.at[:, up]),
                mv.start(w_out.at[:, at], wout.at[:, at]),
            ]
        )
    run(fore_two[0].left(), fore_two[0], fore_two[1])
    ld_dy.wait()
    st_h1.wait()

    def bias_sum(i, carry):
        gg[5:6] += jnp.sum(dy[rows_at(i * NR, NR)].astype(F32), axis=0, keepdims=True)
        return carry

    for i in range(pieces):
        for cp in w_loads[i]:
            cp.wait()
        feed(0, i * per, per, with_lines(per, 1, fore_two[1]))
    fore_one[0].drain()
    three_part(0, fore_two[1])
    run(fore_two[1].left(), fore_two[1], three[0])
    lax.fori_loop(0, rows // NR, bias_sum, 0)
    for line in (fore_one[1], fore_two[0], fore_two[1]):
        line.drain()
    feed(1, 0, tiles, with_lines(tiles, 1, three[0]))
    three_part(1, three[0])
    down_part(0)
    run(1, three[0], three[1])
    down_part(1)
    run(1, three[0], three[1])
    gradient(three[0], three[1])
    gradient(three[0], three[1])
    ld_h1 = mv.start(o_h1, hid)
    run(three[0].left(), three[0], three[1])
    cross_back(0, 2, three[1])
    three[0].drain()
    two_part(0)
    gradient(three[1], two[0])
    run(three[1].left(), three[1], two[0])
    cross_back(1, 2, two[0])
    three[1].drain()
    two_part(1)
    tst[...] = dtkv[t_theirs].astype(BF)
    t_copy = send(tst, trv, k_send.at[2], k_recv.at[2], core)
    t_copy.start()
    gradient(two[0], two[1])
    run(2, two[0], two[1])
    gradient(two[0], two[1])
    run(two[0].left(), two[0], two[1])
    self_back(0, two[1], mix[0])
    two[0].drain()
    gradient(two[1], mix[0])
    ld_tok = mv.start(tokens, h3)
    run(two[1].left(), two[1], mix[0])
    gradient(mix[0], mix[1])
    self_back(1, mix[0], mix[1])
    two[1].drain()
    dco[...] = dk[theirs].astype(BF)
    k_copy = send(dco, krv.at[0], k_send.at[0], k_recv.at[0], core)
    k_copy.start()
    dcq[...] = dv[theirs].astype(BF)
    v_copy = send(dcq, krv.at[1], k_send.at[1], k_recv.at[1], core)
    v_copy.start()
    t_copy.wait()
    tst[...] = (dtkv[t_mine] + trv[...].astype(F32)).astype(BF)
    gradient(mix[0], mix[1])
    ld_qkv = mv.start(w_qkv, win.at[:, pl.ds(0, 3 * cols)])
    k_copy.wait_recv()
    ld_h1.wait()
    ld_tok.wait()
    for g in range(2):
        at = slice(g * group, (g + 1) * group)
        own_at = rows_at(half * rows + g * group, group)
        for j in range(pairs):
            here = slice(j * 128, (j + 1) * 128)
            u = dk[own_at, here] + krv[0, at, here].astype(F32)
            dqkv[at, cols + j * 128 : cols + (j + 1) * 128] = turn(
                u, tab[0, at], -tab[1, at], -tab[2, at]
            ).astype(BF)
        if g == 0:
            v_copy.wait_recv()
        dqkv[at, 2 * cols :] = (dv[own_at] + krv[1, at].astype(F32)).astype(BF)
        if g == 0:
            ld_qkv.wait()
        one_part(g)
        if g == 0:
            run(4, one[0], mix[0], mix[1])
    gradient(one[0], one[1], mix[0], mix[1])
    run(1, one[0], one[1], mix[0], mix[1])
    gradient(one[0], one[1], mix[0], mix[1])
    run(2, one[0], one[1], mix[0], mix[1])
    gradient(one[0], one[1], mix[0], mix[1])
    run(3, one[0], one[1], mix[0], mix[1])
    gradient(one[0], one[1], mix[0], mix[1])
    run(max(one[1].left(), mix[0].left(), mix[1].left()), one[0], one[1], mix[0], mix[1])
    st = [mv.start(mixed, o_mixed)]
    for g, wide_rows in enumerate((x1, x2)):
        at = pl.ds(g * group, group)
        wide_rows[...] = gt[at].astype(F32)
        st.append(mv.start(wide_rows, o_gt.at[at]))
    ggs[...] = jnp.zeros_like(ggs)
    for b in range(dp):
        ggs[b, :, 0:shard] = gg[:, b * shard : (b + 1) * shard]
    sums = []
    for b in range(1, dp):
        to = jnp.bitwise_xor(d, b)
        cp = send(ggs.at[to], ggr.at[b], v_send.at[b], v_recv.at[b], (to, z))
        cp.start()
        sums.append(cp)
    gradient()
    total = ggs[d]
    for b, cp in enumerate(sums):
        cp.wait_recv()
        total = total + ggr[b + 1]
    ggo[...] = total
    line_sums = []
    for j in range(1, n):
        cp = send(
            ggo, ggz.at[j], v_send.at[dp + j - 1], v_recv.at[dp + j - 1], (d, lax.rem(z + j, n))
        )
        cp.start()
        line_sums.append(cp)
    gradient()
    for j, cp in enumerate(line_sums):
        cp.wait_recv()
        total = total + ggz[j + 1]
    v_gains[...] = total[0:3, 0:shard]
    v_b_in[...] = ggo[3:5, 0:shard]
    v_b_out[...] = ggo[5:6, 0:shard]
    st += [mv.start(a, b) for a, b in ((v_gains, o_gains), (v_b_in, o_b_in), (v_b_out, o_b_out))]
    for cp in sums + line_sums + [k_copy, v_copy] + kv + vec_copies:
        cp.wait_send()
    for g in (g_small, g_out, g_in):
        g.drain()
    for line in mix + one:
        line.drain()
    for cp in st:
        cp.wait()


def run_block(n, dp, tokens, context, cotangent, tables, frame_counts, text_counts, vec, s_qkv, s_small, s_ckv, s_out, s_in):
    rows, width = tokens.shape
    cols = s_qkv.shape[1] // 3
    units = s_out.shape[1]
    heads = cols // HD
    text, text_width = context.shape
    shard = width // dp
    half_rows = rows // 2
    sds = jax.ShapeDtypeStruct
    outs = [
        sds((width, 3 * cols), BF),
        sds((width, units), BF),
        sds((width, 2 * units), BF),
        sds((rows, width), BF),
        sds((heads, rows, 2 * rows), BF),
        sds((rows, width), BF),
        sds((rows, width), F32),
        sds((3, shard), F32),
        sds((2, shard), F32),
        sds((1, shard), F32),
        sds((shard, units), F32),
        sds((shard, 2 * units), F32),
        sds((shard, 2 * cols), F32),
        sds((text_width // dp, 2 * cols), F32),
        sds((shard, 4 * cols), F32),
    ]
    vm = pltpu.VMEM
    chunks = rows // 4 // CH
    full, head, own_x = vm((rows, width), BF), vm((rows, cols), BF), vm((half_rows, width), F32)
    keys = vm((2 * rows, cols), BF)
    scratch = [
        vm((dp,) + vec.shape, BF),
        vm((8, width), F32),
        vm((width, 2 * units), BF),
        vm((width, units), BF),
        vm((width, 3 * cols), BF),
        full,
        full,
        full,
        vm((rows, units), BF),
        vm((rows, 2 * units), BF),
        full,
        full,
        own_x,
        own_x,
        own_x,
        head,
        keys,
        keys,
        head,
        head,
        head,
        head,
        head,
        head,
        vm((rows, 3 * cols), BF),
        vm((2 * text, 2 * cols), BF),
        vm((2 * text, 2 * cols), F32),
        vm((heads, rows, 2 * text), BF),
        vm((2, half_rows, 2 * rows), BF),
        vm((2 * rows, cols), F32),
        vm((2 * rows, cols), F32),
        vm(context.shape, BF),
        vm(tables.shape, F32),
        vm((8, width), F32),
        vm((4, half_rows, width), BF),
        vm((4, half_rows, width), BF),
        vm((2, rows, cols), BF),
        vm((text, 2 * cols), BF),
        vm((text, 2 * cols), BF),
        vm((2, 4, shard, 2 * cols), BF),
        vm((2, 2, 2, shard // 2, 2 * cols), BF),
        vm((2, 2, shard // 2, 2 * cols), BF),
        vm((2, shard, 2 * cols), F32),
        vm((dp, 8, 256), F32),
        vm((dp, 8, 256), F32),
        vm((n, 8, 256), F32),
        vm((8, 256), F32),
        vm((3, shard), F32),
        vm((2, shard), F32),
        vm((1, shard), F32),
        DMA((5, 9)),
        DMA((5, 9)),
        DMA((5,)),
        DMA((dp,)),
        DMA((dp,)),
        DMA((3,)),
        DMA((3,)),
        DMA((3,)),
        DMA((3,)),
        *[DMA((12, 2, chunks))] * 4,
        DMA((2,)),
        DMA((2, 4)),
        DMA((2, 4)),
        DMA((2, 4)),
        DMA((2, 4)),
        DMA((2, 2)),
        DMA((2, 2)),
        DMA((2,)),
        DMA((dp + n - 1,)),
        DMA((dp + n - 1,)),
        DMA((32,)),
    ]
    ins = (tokens, context, cotangent, tables, frame_counts, text_counts, vec, s_qkv, s_small, s_ckv, s_out, s_in)
    scalars = pl.BlockSpec(memory_space=pltpu.SMEM)
    return pl.pallas_call(
        functools.partial(block_kernel, n, dp),
        out_shape=outs,
        in_specs=[HBM] * 4 + [scalars] * 2 + [HBM] * 6,
        out_specs=[HBM] * len(outs),
        scratch_shapes=scratch,
        compiler_params=pltpu.CompilerParams(
            collective_id=0, has_side_effects=True, vmem_limit_bytes=63 * 2**20
        ),
        name="block",
    )(*ins)[5:]


def prepare(tokens, context, frame_counts, text_counts, w_qkv, w_attn_out, w_cross_q, w_cross_kv, w_cross_out, w_in, w_out, norm_gains, b_in, b_out):
    shard, _, cols = w_qkv.shape
    rows = tokens.shape[0]
    vec = jnp.concatenate([norm_gains, b_in, b_out[None]], axis=0)
    vec = jnp.pad(vec, ((0, 16 - vec.shape[0]), (0, 256 - shard)))
    d = lax.axis_index("dp")
    half = d % 2
    m = HD // 4
    lane = jnp.arange(128) % HD
    frequency = 10000.0 ** (-(lane % m).astype(F32) / m)
    angle = (half * rows + jnp.arange(rows)).astype(F32)[:, None] * frequency[None]
    sine = jnp.sin(angle)
    tables = jnp.stack(
        [
            jnp.where(lane < 2 * m, jnp.cos(angle), 1.0),
            jnp.where(lane < m, -sine, 0.0),
            jnp.where((lane >= m) & (lane < 2 * m), sine, 0.0),
        ]
    )
    return (
        tables,
        frame_counts,
        text_counts,
        vec,
        w_qkv.reshape(shard, 3 * cols),
        jnp.concatenate([w_attn_out.T, w_cross_q, w_cross_out.T], axis=1),
        w_cross_kv.reshape(w_cross_kv.shape[0], 2 * cols),
        w_out.T,
        w_in.reshape(shard, -1),
    )


def from_partner(block, axis, stride):
    count = lax.axis_size(axis)
    route = []
    for low in range(count):
        high = low | 1 << stride
        if high != low and high < count:
            route += [(low, high), (high, low)]
    return lax.ppermute(block, axis, route)


def layer_norm(values, gain_row):
    centered = values - jnp.mean(values, axis=-1, keepdims=True)
    spread = jnp.mean(centered * centered, axis=-1, keepdims=True)
    return centered * lax.rsqrt(spread + epsilon) * gain_row


def rotate(tensor, positions):
    quarter = tensor.shape[-1] // 4
    frequency = 10000.0 ** (-jnp.arange(quarter, dtype=jnp.float32) / quarter)
    angles = positions[:, None] * frequency[None, :]
    cosine = jnp.cos(angles)[:, None, :]
    sine_part = jnp.sin(angles)[:, None, :]
    first_part = tensor[..., :quarter]
    second = tensor[..., quarter : 2 * quarter]
    return jnp.concatenate(
        [
            first_part * cosine - second * sine_part,
            second * cosine + first_part * sine_part,
            tensor[..., 2 * quarter :],
        ],
        axis=-1,
    )


def gated_unit(both):
    gate = both[:, 0]
    return gate * jax.nn.sigmoid(gate) * both[:, 1]


def in_order(own_part, other_part, which_half):
    lower_first = jnp.concatenate([own_part, other_part], axis=0)
    upper_first = jnp.concatenate([other_part, own_part], axis=0)
    return jnp.where(which_half == 0, lower_first, upper_first)


def own_rows(whole, which_half, row_count):
    return lax.dynamic_slice_in_dim(whole, which_half * row_count, row_count, 0)


def partner_rows(whole, which_half, row_count):
    return lax.dynamic_slice_in_dim(whole, (1 - which_half) * row_count, row_count, 0)


def masked_scores(query_block, key_all, key_live):
    scale = query_block.shape[-1] ** (-0.5)
    raw_scores = (
        jnp.einsum("qhd,khd->hqk", query_block, key_all, preferred_element_type=jnp.float32) * scale
    )
    return jnp.where(key_live[None, None, :], raw_scores, -1e30)


def attend_forward(queries, key_all, value_all, key_live):
    row_count, head_count, head_size = queries.shape
    block_rows = min(512, row_count)
    blocks = queries.reshape(row_count // block_rows, block_rows, head_count, head_size)

    def per_block(query_block):
        scores = masked_scores(query_block, key_all, key_live)
        row_max = jnp.max(scores, axis=-1, keepdims=True)
        weights = jnp.exp(scores - row_max)
        row_total = jnp.sum(weights, axis=-1, keepdims=True)
        attn_probs = weights / row_total
        block_out = jnp.einsum(
            "hqk,khd->qhd",
            attn_probs.astype(jnp.bfloat16),
            value_all,
            preferred_element_type=jnp.float32,
        )
        return (block_out, row_max + jnp.log(row_total))

    outputs, log_sums = lax.map(per_block, blocks)
    return (outputs.reshape(row_count, head_count, head_size), log_sums)


def attend_backward(queries, key_all, value_all, key_live, log_sums, grad_out):
    row_count, head_count, head_size = queries.shape
    block_rows = min(512, row_count)
    block_shape = (row_count // block_rows, block_rows, head_count, head_size)
    scale = head_size ** (-0.5)

    def per_block(running, block_item):
        query_block, grad_block, lse_block = block_item
        attn_probs = jnp.exp(masked_scores(query_block, key_all, key_live) - lse_block)
        grad_probs = jnp.einsum(
            "qhd,khd->hqk", grad_block, value_all, preferred_element_type=jnp.float32
        )
        row_inner = jnp.sum(attn_probs * grad_probs, axis=-1, keepdims=True)
        grad_scores = (attn_probs * (grad_probs - row_inner)).astype(jnp.bfloat16)
        grad_query = (
            jnp.einsum("hqk,khd->qhd", grad_scores, key_all, preferred_element_type=jnp.float32)
            * scale
        )
        grad_key = (
            running[0]
            + jnp.einsum(
                "hqk,qhd->khd", grad_scores, query_block, preferred_element_type=jnp.float32
            )
            * scale
        )
        grad_value = running[1] + jnp.einsum(
            "hqk,qhd->khd",
            attn_probs.astype(jnp.bfloat16),
            grad_block,
            preferred_element_type=jnp.float32,
        )
        return ((grad_key, grad_value), grad_query)

    zero_keys = jnp.zeros(key_all.shape, jnp.float32)
    (grad_key, grad_value), grad_query = lax.scan(
        per_block,
        (zero_keys, zero_keys),
        (queries.reshape(block_shape), grad_out.reshape(block_shape), log_sums),
    )
    return (grad_query.reshape(row_count, head_count, head_size), grad_key, grad_value)


def branch_total(partial_sum):
    return lax.psum(partial_sum, "mp")


def grad_total(partial_sum):
    return lax.psum(partial_sum, "mp")


def body(
    tokens,
    context,
    frame_counts,
    text_counts,
    w_qkv,
    w_attn_out,
    w_cross_q,
    w_cross_kv,
    w_cross_out,
    w_in,
    w_out,
    norm_gains,
    b_in,
    b_out,
    cotangent,
):
    gathered = (
        lax.all_gather(w_qkv, "dp", axis=0, tiled=True),
        lax.all_gather(w_attn_out, "dp", axis=1, tiled=True),
        lax.all_gather(w_cross_q, "dp", axis=0, tiled=True),
        lax.all_gather(w_cross_kv, "dp", axis=0, tiled=True),
        lax.all_gather(w_cross_out, "dp", axis=1, tiled=True),
        lax.all_gather(w_in, "dp", axis=0, tiled=True),
        lax.all_gather(w_out, "dp", axis=1, tiled=True),
        lax.all_gather(norm_gains, "dp", axis=1, tiled=True),
        lax.all_gather(b_in, "dp", axis=1, tiled=True),
        lax.all_gather(b_out, "dp", axis=0, tiled=True),
    )
    (
        qkv_full,
        attn_out_full,
        cross_q_full,
        cross_kv_full,
        cross_out_full,
        in_full,
        out_full,
        gains_full,
        b_in_full,
        b_out_full,
    ) = gathered
    row_count, model_width = tokens.shape
    text_rows, text_width = context.shape
    head_cols = qkv_full.shape[2]
    unit_cols = in_full.shape[2]
    head_count = head_cols // HD
    device_row = lax.axis_index("dp")
    which_half = device_row % 2
    clip_index = device_row // 2
    frame_live = lax.dynamic_index_in_dim(frame_counts, clip_index, 0, keepdims=False)
    text_live = lax.dynamic_index_in_dim(text_counts, clip_index, 0, keepdims=False)
    positions = (which_half * row_count + jnp.arange(row_count)).astype(jnp.float32)
    key_live = jnp.arange(2 * row_count) <= frame_live
    token_live = jnp.arange(2 * text_rows) < text_live
    gain_rows = gains_full.astype(jnp.float32)
    tokens_f = tokens.astype(jnp.float32)
    grad_y_mine = cotangent.astype(jnp.float32)
    norm_one, pull_one = jax.vjp(layer_norm, tokens_f, gain_rows[0])
    h_one = norm_one.astype(jnp.bfloat16)
    qkv = jnp.dot(
        h_one, qkv_full.reshape(model_width, 3 * head_cols), preferred_element_type=jnp.float32
    ).reshape(row_count, 3, head_count, HD)
    queries = rotate(qkv[:, 0], positions).astype(jnp.bfloat16)
    own_keys = rotate(qkv[:, 1], positions).astype(jnp.bfloat16).reshape(row_count, head_cols)
    own_values = qkv[:, 2].astype(jnp.bfloat16).reshape(row_count, head_cols)
    own_text = jnp.dot(
        context,
        cross_kv_full.reshape(text_width, 2 * head_cols),
        preferred_element_type=jnp.float32,
    ).astype(jnp.bfloat16)
    other = from_partner((own_keys, own_values, own_text), "dp", 0)
    key_all = in_order(own_keys, other[0], which_half).reshape(2 * row_count, head_count, HD)
    value_all = in_order(own_values, other[1], which_half).reshape(2 * row_count, head_count, HD)
    text_all = in_order(own_text, other[2], which_half).reshape(2 * text_rows, 2, head_count, HD)
    text_keys = text_all[:, 0]
    text_values = text_all[:, 1]
    self_attn, self_lse = attend_forward(queries, key_all, value_all, key_live)
    self_out = self_attn.reshape(row_count, head_cols).astype(jnp.bfloat16)
    self_part = jnp.dot(self_out, attn_out_full, preferred_element_type=jnp.float32)
    x_one = tokens_f + branch_total(self_part)
    norm_two, pull_two = jax.vjp(layer_norm, x_one, gain_rows[1])
    h_two = norm_two.astype(jnp.bfloat16)
    cross_queries = (
        jnp.dot(h_two, cross_q_full, preferred_element_type=jnp.float32)
        .astype(jnp.bfloat16)
        .reshape(row_count, head_count, HD)
    )
    cross_attn, cross_lse = attend_forward(cross_queries, text_keys, text_values, token_live)
    cross_out = cross_attn.reshape(row_count, head_cols).astype(jnp.bfloat16)
    cross_part = jnp.dot(cross_out, cross_out_full, preferred_element_type=jnp.float32)
    x_two = x_one + branch_total(cross_part)
    norm_three, pull_three = jax.vjp(layer_norm, x_two, gain_rows[2])
    h_three = norm_three.astype(jnp.bfloat16)
    both = jnp.dot(
        h_three, in_full.reshape(model_width, 2 * unit_cols), preferred_element_type=jnp.float32
    ).reshape(row_count, 2, unit_cols) + b_in_full.astype(jnp.float32)
    hidden_f, pull_unit = jax.vjp(gated_unit, both)
    hidden = hidden_f.astype(jnp.bfloat16)
    down_part = jnp.dot(hidden, out_full, preferred_element_type=jnp.float32)
    mixed = (x_two + branch_total(down_part) + b_out_full.astype(jnp.float32)).astype(jnp.bfloat16)
    again = (
        lax.all_gather(w_qkv, "dp", axis=0, tiled=True),
        lax.all_gather(w_attn_out, "dp", axis=1, tiled=True),
        lax.all_gather(w_cross_q, "dp", axis=0, tiled=True),
        lax.all_gather(w_cross_out, "dp", axis=1, tiled=True),
        lax.all_gather(w_in, "dp", axis=0, tiled=True),
        lax.all_gather(w_out, "dp", axis=1, tiled=True),
    )
    qkv_back = again[0]
    attn_out_back = again[1]
    cross_q_back = again[2]
    cross_out_back = again[3]
    in_back = again[4]
    out_back = again[5]
    grad_y = cotangent.astype(jnp.float32)
    grad_out_w = jnp.dot(hidden.T, cotangent, preferred_element_type=jnp.float32)
    grad_b_out = jnp.sum(grad_y, axis=0)
    grad_hidden = jnp.dot(cotangent, out_back.T, preferred_element_type=jnp.float32)
    grad_both = pull_unit(grad_hidden)[0].astype(jnp.bfloat16).reshape(row_count, 2 * unit_cols)
    grad_b_in = jnp.sum(grad_both, axis=0, dtype=jnp.float32).reshape(2, unit_cols)
    grad_in_w = jnp.dot(h_three.T, grad_both, preferred_element_type=jnp.float32).reshape(
        model_width, 2, unit_cols
    )
    three_part = jnp.dot(
        grad_both, in_back.reshape(model_width, 2 * unit_cols).T, preferred_element_type=jnp.float32
    )
    grad_x_norm, grad_gain_three = pull_three(grad_total(three_part))
    grad_x_two = grad_y_mine + grad_x_norm
    grad_two_b = grad_x_two.astype(jnp.bfloat16)
    grad_cross_out_w = jnp.dot(cross_out.T, grad_two_b, preferred_element_type=jnp.float32)
    grad_cross = (
        jnp.dot(grad_two_b, cross_out_back.T, preferred_element_type=jnp.float32)
        .astype(jnp.bfloat16)
        .reshape(row_count, head_count, HD)
    )
    grad_cq, grad_text_key, grad_text_value = attend_backward(
        cross_queries, text_keys, text_values, token_live, cross_lse, grad_cross
    )
    grad_cq_b = grad_cq.reshape(row_count, head_cols).astype(jnp.bfloat16)
    grad_cross_q_w = jnp.dot(h_two.T, grad_cq_b, preferred_element_type=jnp.float32)
    grad_text = jnp.stack([grad_text_key, grad_text_value], axis=1).reshape(
        2 * text_rows, 2 * head_cols
    )
    two_part = jnp.dot(grad_cq_b, cross_q_back.T, preferred_element_type=jnp.float32)
    grad_x_norm, grad_gain_two = pull_two(grad_total(two_part))
    grad_x_one = grad_x_two + grad_x_norm
    grad_one_b = grad_x_one.astype(jnp.bfloat16)
    grad_attn_out_w = jnp.dot(self_out.T, grad_one_b, preferred_element_type=jnp.float32)
    grad_self = (
        jnp.dot(grad_one_b, attn_out_back.T, preferred_element_type=jnp.float32)
        .astype(jnp.bfloat16)
        .reshape(row_count, head_count, HD)
    )
    grad_query, grad_key_all, grad_value_all = attend_backward(
        queries, key_all, value_all, key_live, self_lse, grad_self
    )
    grad_key_flat = grad_key_all.reshape(2 * row_count, head_cols)
    grad_value_flat = grad_value_all.reshape(2 * row_count, head_cols)
    back = from_partner(
        (
            partner_rows(grad_key_flat, which_half, row_count),
            partner_rows(grad_value_flat, which_half, row_count),
            partner_rows(grad_text, which_half, text_rows),
        ),
        "dp",
        0,
    )
    grad_key_own = (own_rows(grad_key_flat, which_half, row_count) + back[0]).reshape(
        row_count, head_count, HD
    )
    grad_value_own = own_rows(grad_value_flat, which_half, row_count) + back[1]
    grad_text_own = (own_rows(grad_text, which_half, text_rows) + back[2]).astype(jnp.bfloat16)
    grad_query_raw = rotate(grad_query, -positions).reshape(row_count, head_cols)
    grad_key_raw = rotate(grad_key_own, -positions).reshape(row_count, head_cols)
    grad_qkv_b = (
        jnp.stack([grad_query_raw, grad_key_raw, grad_value_own], axis=1)
        .astype(jnp.bfloat16)
        .reshape(row_count, 3 * head_cols)
    )
    grad_qkv_w = jnp.dot(h_one.T, grad_qkv_b, preferred_element_type=jnp.float32).reshape(
        model_width, 3, head_cols
    )
    grad_cross_kv_w = jnp.dot(context.T, grad_text_own, preferred_element_type=jnp.float32).reshape(
        text_width, 2, head_cols
    )
    one_part = jnp.dot(
        grad_qkv_b,
        qkv_back.reshape(model_width, 3 * head_cols).T,
        preferred_element_type=jnp.float32,
    )
    grad_x_norm, grad_gain_one = pull_one(grad_total(one_part))
    grad_tokens = grad_x_one + grad_x_norm
    grad_gains = jnp.stack([grad_gain_one, grad_gain_two, grad_gain_three], axis=0)
    summed = (
        lax.psum_scatter(grad_qkv_w, "dp", scatter_dimension=0, tiled=True),
        lax.psum_scatter(grad_attn_out_w, "dp", scatter_dimension=1, tiled=True),
        lax.psum_scatter(grad_cross_q_w, "dp", scatter_dimension=0, tiled=True),
        lax.psum_scatter(grad_cross_kv_w, "dp", scatter_dimension=0, tiled=True),
        lax.psum_scatter(grad_cross_out_w, "dp", scatter_dimension=1, tiled=True),
        lax.psum_scatter(grad_in_w, "dp", scatter_dimension=0, tiled=True),
        lax.psum_scatter(grad_out_w, "dp", scatter_dimension=1, tiled=True),
        lax.psum_scatter(grad_gains, "dp", scatter_dimension=1, tiled=True),
        lax.psum_scatter(grad_b_in, "dp", scatter_dimension=1, tiled=True),
        lax.psum_scatter(grad_b_out, "dp", scatter_dimension=0, tiled=True),
    )
    return (
        mixed,
        grad_tokens,
        summed[0],
        summed[1],
        summed[2],
        summed[3],
        summed[4],
        summed[5],
        summed[6],
        summed[7],
        summed[8],
        summed[9],
    )


def near_body(
    tokens,
    context,
    frame_counts,
    text_counts,
    w_qkv,
    w_attn_out,
    w_cross_q,
    w_cross_kv,
    w_cross_out,
    w_in,
    w_out,
    norm_gains,
    b_in,
    b_out,
    cotangent,
):
    n, dp = lax.axis_size("mp"), lax.axis_size("dp")
    shard, _, cols = w_qkv.shape
    small = prepare(
        tokens,
        context,
        frame_counts,
        text_counts,
        w_qkv,
        w_attn_out,
        w_cross_q,
        w_cross_kv,
        w_cross_out,
        w_in,
        w_out,
        norm_gains,
        b_in,
        b_out,
    )
    mixed, gt, gains, bias_in, bias_out, *parts = run_block(n, dp, tokens, context, cotangent, *small)
    g_out, g_in, g_mid, g_ckv, g_last = parts
    return (
        mixed,
        gt,
        g_last[:, cols:].reshape(shard, 3, cols),
        g_last[:, :cols].T,
        g_mid[:, cols:],
        g_ckv.reshape(-1, 2, cols),
        g_mid[:, :cols].T,
        g_in.reshape(shard, 2, -1),
        g_out.T,
        gains,
        bias_in,
        bias_out[0],
    )


def solution(mesh):
    in_specs = (
        P("dp", None),
        P("dp", None),
        P(),
        P(),
        P("dp", None, "mp"),
        P("mp", "dp"),
        P("dp", "mp"),
        P("dp", None, "mp"),
        P("mp", "dp"),
        P("dp", None, "mp"),
        P("mp", "dp"),
        P(None, "dp"),
        P(None, ("mp", "dp")),
        P("dp"),
        P("dp", None),
    )
    out_specs = (
        P("dp", None),
        P("dp", None),
        P("dp", None, "mp"),
        P("mp", "dp"),
        P("dp", "mp"),
        P("dp", None, "mp"),
        P("mp", "dp"),
        P("dp", None, "mp"),
        P("mp", "dp"),
        P(None, "dp"),
        P(None, ("mp", "dp")),
        P("dp"),
    )
    near = mesh.shape["dp"] == 8
    return jax.shard_map(
        near_body if near else body,
        mesh=mesh,
        in_specs=in_specs,
        out_specs=out_specs,
        check_vma=False,
    )
```
